32 devices in a mesh: section: 2 (over core), fsdp: 4 (over z), rep: 4 (over y, x).
Axes of the slice: x: 2, y: 2, z: 4, core: 2. Of those that a mesh axis runs over, the one named last changes fastest.
Arguments:
- tokens: bfloat16 [4, 2, 1024, 2048], P('rep', None, 'fsdp'), may hold values from -6 to 6
- segment_ids: int32 [4, 2, 1024], P('rep', None, 'fsdp'), may hold values from 0 to 1, as said below
- cotangent: bfloat16 [4, 2, 1024, 2048], P('rep', None, 'fsdp'), may hold values from -6 to 6
- norm_attn: bfloat16 [2, 2048], P('section', 'fsdp'), may hold values from 0.099609375 to 1.8984375
- w_query: bfloat16 [2, 2048, 2048], P('section', 'fsdp'), may hold values from -0.125 to 0.125
- w_key: bfloat16 [2, 2048, 512], P('section', 'fsdp'), may hold values from -0.125 to 0.125
- w_value: bfloat16 [2, 2048, 512], P('section', 'fsdp'), may hold values from -0.125 to 0.125
- w_output: bfloat16 [2, 2048, 2048], P('section', 'fsdp'), may hold values from -1 to 1
- norm_ffn: bfloat16 [2, 2048], P('section', 'fsdp'), may hold values from 0.099609375 to 1.8984375
- w_gate: bfloat16 [2, 2048, 8192], P('section', 'fsdp'), may hold values from -0.125 to 0.125
- w_up: bfloat16 [2, 2048, 8192], P('section', 'fsdp'), may hold values from -0.125 to 0.125
- w_down: bfloat16 [2, 8192, 2048], P('section', 'fsdp'), may hold values from -0.0625 to 0.0625
Outputs:
- section_outputs: bfloat16 [2, 4, 2, 1024, 2048], P('section', 'rep', None, 'fsdp')
- input_grads: bfloat16 [2, 4, 2, 1024, 2048], P('section', 'rep', None, 'fsdp')
- grad_norm_attn: float32 [2, 2048], P('section', 'fsdp')
- grad_w_query: float32 [2, 2048, 2048], P('section', 'fsdp')
- grad_w_key: float32 [2, 2048, 512], P('section', 'fsdp')
- grad_w_value: float32 [2, 2048, 512], P('section', 'fsdp')
- grad_w_output: float32 [2, 2048, 2048], P('section', 'fsdp')
- grad_norm_ffn: float32 [2, 2048], P('section', 'fsdp')
- grad_w_gate: float32 [2, 2048, 8192], P('section', 'fsdp')
- grad_w_up: float32 [2, 2048, 8192], P('section', 'fsdp')
- grad_w_down: float32 [2, 8192, 2048], P('section', 'fsdp')
The draws below stay inside these ranges and needn't reach their ends.
Inputs may be any that keep to these rules, and one draw needn't show every extreme that they name: `segment_ids`: along the 1024 positions of each micro-batch the ids never fall; positions with equal ids form one sequence; in some micro-batch one sequence fills all 1024 positions.
All inputs are finite; a program needn't handle non-finite values.
Results may differ from the reference program's by a relative error of at most 0.025.
Values may be sent and summed in bfloat16 or wider, within the bound.
A program may use at most 832 MiB of HBM per device.

```python
import jax
import jax.numpy as jnp
from jax import lax

D = 2048
HQ = 32
KVH = 8
HD = 64
FF = 8192
MB_TOKENS = 1024
MICRO = 2
SEQ_CUTS = 1
REPLICAS = 4


def draw_segment_ids(key, part):
    first_key, second_key = jax.random.split(jax.random.fold_in(key, 11))
    cut_points = jax.random.randint(first_key, (REPLICAS, MICRO, SEQ_CUTS), 1, MB_TOKENS)
    whole_row = jax.random.randint(second_key, (), 0, REPLICAS * MICRO)
    row_ids = jnp.arange(REPLICAS * MICRO).reshape(REPLICAS, MICRO)
    cut_points = jnp.where((row_ids == whole_row)[..., None], MB_TOKENS, cut_points)
    positions = jnp.arange(MB_TOKENS)
    counted = (cut_points[..., None, :] <= positions[:, None]).astype(jnp.int32)
    return jnp.sum(counted, axis=-1).astype(jnp.int32)


def steps_of(own_key, shape, shards, smallest, largest):
    def one(dim, shards_of):
        steps = jax.random.uniform(jax.random.fold_in(jax.random.fold_in(own_key, 6), dim), (shards_of,), jnp.float32, smallest / len(shards), largest / len(shards))
        return jnp.repeat(jnp.exp(steps), shape[dim] // shards_of).reshape((-1,) + (1,) * (len(shape) - dim - 1))

    level = one(*shards[0])
    for cut in shards[1:]:
        level = level * one(*cut)
    return level


def normal_values(own_key, extent, deviation, bound, cuts=(), held_as=jnp.bfloat16):
    entries = jax.random.normal(own_key, extent, jnp.float32) * deviation
    if len(cuts) > 0:
        entries = steps_of(own_key, extent, cuts, -0.22, 0.18) * entries
    return jnp.clip(entries, min=-bound, max=bound).astype(held_as)


def setup_inputs(seed: int = 0) -> dict:
    streams_of = jax.random.split(jax.random.key(seed), 13)
    return {
        "tokens": normal_values(streams_of[0], (REPLICAS, MICRO, MB_TOKENS, D), 1.0, 6.0, ((0, 4), (2, 4))),
        "segment_ids": draw_segment_ids(jax.random.fold_in(streams_of[12], 71), 0),
        "cotangent": normal_values(streams_of[2], (REPLICAS, MICRO, MB_TOKENS, D), 1.0, 6.0, ((0, 4), (2, 4))),
        "norm_attn": jnp.clip(1.0 + 0.18 * jax.random.normal(streams_of[3], (2, D), jnp.float32), 0.099609375, 1.8984375).astype(jnp.bfloat16),
        "w_query": normal_values(streams_of[4], (2, D, HQ * HD), D ** -0.5, 0.125, ((0, 2), (1, 4))),
        "w_key": normal_values(streams_of[5], (2, D, KVH * HD), D ** -0.5, 0.125, ((0, 2), (1, 4))),
        "w_value": normal_values(streams_of[6], (2, D, KVH * HD), D ** -0.5, 0.125, ((0, 2), (1, 4))),
        "w_output": normal_values(streams_of[7], (2, HQ * HD, D), (max(HQ * HD // 64, 1)) ** -0.5, 1.0, ((0, 2), (1, 4))),
        "norm_ffn": jnp.clip(1.0 + 0.18 * jax.random.normal(streams_of[8], (2, D), jnp.float32), 0.099609375, 1.8984375).astype(jnp.bfloat16),
        "w_gate": normal_values(streams_of[9], (2, D, FF), D ** -0.5, 0.125, ((0, 2), (1, 4))),
        "w_up": normal_values(streams_of[10], (2, D, FF), D ** -0.5, 0.125, ((0, 2), (1, 4))),
        "w_down": normal_values(streams_of[11], (2, FF, D), FF ** -0.5, 0.0625, ((0, 2), (1, 4))),
    }


epsilon = 1e-05
rope_base = 500000.0
masked_score = -1e+30

@jax.custom_vjp
def low(v):
    return lax.optimization_barrier(v.astype(jnp.bfloat16)).astype(jnp.float32)

@jax.custom_vjp
def low_back(v):
    return v

def low_keep(v):
    return (low(v), None)

def low_pass(kept, grad):
    return (grad,)

def back_keep(v):
    return (v, None)

def back_low(kept, grad):
    return (low(grad),)
low.defvjp(low_keep, low_pass)
low_back.defvjp(back_keep, back_low)

def rms_scale(values, gain_vec):
    return values * lax.rsqrt(lax.optimization_barrier(jnp.mean(values * values, axis=-1, keepdims=True)) + epsilon) * gain_vec

def rope_tables(positions):
    half_size = HD // 2
    frequency = rope_base ** (-(jnp.arange(half_size).astype(jnp.float32) * 2.0) / HD)
    angles = positions[:, None] * frequency[None, :]
    angles = jnp.concatenate([angles, angles], axis=-1)
    return (jnp.cos(angles)[:, None, :], jnp.sin(angles)[:, None, :])

def rotary(values, cosine_table, sine_table):
    half_size = values.shape[-1] // 2
    turned = jnp.concatenate([-values[..., half_size:], values[..., :half_size]], axis=-1)
    return values * cosine_table + turned * sine_table

def layer(block_in, params, cosine_table, sine_table, allowed):
    norm_attn, w_query, w_key, w_value, w_output, norm_ffn, w_gate, w_up, w_down = params
    highest = lax.Precision.HIGHEST
    rows_here = block_in.shape[0]
    scale = HD ** (-0.5)
    normed = low(rms_scale(block_in, norm_attn))
    query = low_back(jnp.dot(normed, w_query, precision=highest)).reshape(rows_here, HQ, HD)
    key_pre = low_back(jnp.dot(normed, w_key, precision=highest)).reshape(rows_here, KVH, HD)
    value_heads = low(low_back(jnp.dot(normed, w_value, precision=highest))).reshape(rows_here, KVH, HD)
    query_rot = low(rotary(query, cosine_table, sine_table)).reshape(rows_here, KVH, HQ // KVH, HD)
    key_rot = low(rotary(key_pre, cosine_table, sine_table))
    scores = low_back(jnp.einsum('tkgd,skd->kgts', query_rot, key_rot, precision=highest) * scale)
    scores = jnp.where(allowed[None, None], scores, masked_score)
    attn_probs = low(jax.nn.softmax(scores, axis=-1))
    mixed_heads = jnp.einsum('kgts,skd->tkgd', attn_probs, value_heads, precision=highest).reshape(rows_here, HQ * HD)
    mixed_heads = low(low_back(mixed_heads))
    residual = block_in + low_back(jnp.dot(mixed_heads, w_output, precision=highest))
    normed_ffn = low(rms_scale(residual, norm_ffn))
    gate_pre = low_back(jnp.dot(normed_ffn, w_gate, precision=highest))
    up_pre = low_back(jnp.dot(normed_ffn, w_up, precision=highest))
    hidden = low(jax.nn.silu(gate_pre) * up_pre)
    return residual + low_back(jnp.dot(hidden, w_down, precision=highest))

def reference(tokens, segment_ids, cotangent, norm_attn, w_query, w_key, w_value, w_output, norm_ffn, w_gate, w_up, w_down):
    weights = tuple((w.astype(jnp.float32) for w in (norm_attn, w_query, w_key, w_value, w_output, norm_ffn, w_gate, w_up, w_down)))
    params = (tuple((w[0] for w in weights)), tuple((w[1] for w in weights)))
    item_count = REPLICAS * MICRO
    flat_tokens = tokens.reshape(item_count, MB_TOKENS, D)
    flat_ids = segment_ids.reshape(item_count, MB_TOKENS)
    flat_cot = cotangent.reshape(item_count, MB_TOKENS, D)

    def per_item(running, item_data):
        block_x, seg_row, grad_item = item_data
        positions = jnp.arange(MB_TOKENS).astype(jnp.int32)
        seg_start = lax.optimization_barrier(jnp.sum((seg_row[None, :] < seg_row[:, None]).astype(jnp.int32), axis=-1))
        cosine_table, sine_table = rope_tables((positions - seg_start).astype(jnp.float32))
        allowed = (seg_row[None, :] == seg_row[:, None]) & (positions[None, :] <= positions[:, None])

        def forward(block_in, both, probe_zero):
            first_out = layer(block_in, both[0], cosine_table, sine_table, allowed)
            second_in = low(low_back(first_out)) + probe_zero
            second_out = layer(second_in, both[1], cosine_table, sine_table, allowed)
            return (first_out, second_out)
        probe_zero = jnp.zeros((MB_TOKENS, D), jnp.float32)
        (first_out, second_out), pull_back = jax.vjp(forward, block_x.astype(jnp.float32), params, probe_zero)
        grad_x, grad_params, grad_probe = pull_back((jnp.zeros_like(first_out), grad_item.astype(jnp.float32)))
        running = jax.tree.map(lambda left, right: left + right, running, grad_params)
        return (running, (first_out.astype(jnp.bfloat16), second_out.astype(jnp.bfloat16), grad_x.astype(jnp.bfloat16), grad_probe.astype(jnp.bfloat16)))
    start_sums = jax.tree.map(lambda w: jnp.zeros_like(w), params)
    sums_done, stacked = lax.scan(per_item, start_sums, (flat_tokens, flat_ids, flat_cot))
    first_all, second_all, grad_first, grad_second = stacked
    shape_out = (2, REPLICAS, MICRO, MB_TOKENS, D)
    section_outputs = jnp.stack([first_all, second_all]).reshape(shape_out)
    input_grads = jnp.stack([grad_first, grad_second]).reshape(shape_out)
    grads = tuple((jnp.stack([sums_done[0][i], sums_done[1][i]]) for i in range(9)))
    return (section_outputs, input_grads, grads[0], grads[1], grads[2], grads[3], grads[4], grads[5], grads[6], grads[7], grads[8])
```

```python
import jax
import jax.numpy as jnp
from jax import lax
from jax.sharding import PartitionSpec as P

HQ = 32
KVH = 8
HD = 64
FF = 8192

epsilon = 1e-05
rope_base = 500000.0
masked_score = -1e30
bf16 = jnp.bfloat16
f32 = jnp.float32
SWAP = [(0, 1), (1, 0)]


def partner(value, bit):
    count = lax.axis_size("rep")
    return lax.ppermute(value, "rep", [(i, i ^ bit) for i in range(count)])


def bit_list(count):
    found = []
    bit = 1
    while bit < count:
        found.append(bit)
        bit *= 2
    return found


def plane_gather(own):
    bits = bit_list(lax.axis_size("rep"))
    half = own.shape[0] // 2
    first, second = own[None, :half], own[None, half:]
    for bit in bits:
        first = jnp.concatenate([first, partner(first, bit)], axis=0)
    for bit in bits[::-1]:
        other = partner(second, bit)
        second = jnp.stack([second, other], axis=1).reshape((-1,) + own[:half].shape)
    return jnp.stack([first, second])


def plane_reduce(parts):
    bits = bit_list(lax.axis_size("rep"))
    first, second = parts[0], parts[1]
    for bit in bits[::-1]:
        keep, away = first[:bit], first[bit:]
        first = keep.astype(f32) + partner(away.astype(bf16), bit).astype(f32)
    for bit in bits:
        pair = second.reshape((-1, 2) + second.shape[1:])
        keep, away = pair[:, 0], pair[:, 1]
        second = keep.astype(f32) + partner(away.astype(bf16), bit).astype(f32)
    return jnp.concatenate([first[0], second[0]], axis=0)


def core_split(value, core):
    half = value.shape[0] // 2
    kept = lax.dynamic_slice_in_dim(value, core * half, half)
    sent = lax.dynamic_slice_in_dim(value, (1 - core) * half, half)
    got = lax.ppermute(sent, "section", SWAP)
    return (jnp.where(core == 0, kept, got), jnp.where(core == 0, got, kept))


def rope_tables(positions):
    half_size = HD // 2
    frequency = rope_base ** (-(jnp.arange(half_size).astype(f32) * 2.0) / HD)
    angles = positions[..., None] * frequency
    angles = jnp.concatenate([angles, angles], axis=-1)
    return (jnp.cos(angles), jnp.sin(angles))


def rotary(values, cosine_table, sine_table):
    half_size = values.shape[-1] // 2
    turned = jnp.concatenate([-values[..., half_size:], values[..., :half_size]], axis=-1)
    return values * cosine_table + turned * sine_table


def rotary_back(grad_rot, cosine_table, sine_table):
    half_size = grad_rot.shape[-1] // 2
    scaled = grad_rot * sine_table
    return grad_rot * cosine_table + jnp.concatenate(
        [scaled[..., half_size:], -scaled[..., :half_size]], axis=-1
    )


def times(left, weight):
    return jnp.dot(left, weight, preferred_element_type=f32)


def times_back(left, weight):
    return lax.dot_general(
        left, weight, (((1,), (1,)), ((), ())), preferred_element_type=f32
    )


def rows_product(left, right):
    return lax.dot_general(
        left, right, (((0,), (0,)), ((), ())), preferred_element_type=f32
    ).astype(bf16)


def scale_of(values):
    return lax.rsqrt(jnp.mean(values * values, axis=-1, keepdims=True) + epsilon)


def norm_back(grad, gain, unit, scale):
    scaled = gain * grad
    out = scale * (scaled - unit * jnp.mean(scaled * unit, axis=-1, keepdims=True))
    return (out, jnp.sum(grad * unit, axis=0))


def attend(query, keyvals, bias):
    two, reps, half, width = query.shape
    kv_heads = keyvals[0].shape[-1] // (2 * HD)
    group = width // HD // kv_heads
    q = query.reshape(two, reps, half, kv_heads, group, HD)
    kv = jnp.stack(keyvals).reshape(len(keyvals), two, reps, half, 2, kv_heads, HD)
    kv = kv.transpose(4, 2, 0, 1, 3, 5, 6).reshape(2, reps, -1, kv_heads, HD)
    q = q.transpose(1, 0, 2, 3, 4, 5).reshape(reps, two * half, kv_heads, group, HD)
    scores = jnp.einsum("jtkgd,jskd->jkgst", q, kv[0], preferred_element_type=f32) * HD ** (-0.5)
    scores = scores + bias[:, None, None].astype(f32)
    row_max = jnp.max(scores, axis=-2)
    exp_scores = jnp.exp(scores - row_max[..., None, :])
    total = jnp.sum(exp_scores, axis=-2)
    probs = (exp_scores / total[..., None, :]).astype(bf16)
    mixed = jnp.einsum("jkgst,jskd->jtkgd", probs, kv[1], preferred_element_type=f32).astype(bf16)
    mixed = mixed.reshape(reps, two, half, width).transpose(1, 0, 2, 3)
    log_total = (row_max + jnp.log(total)).reshape(reps, kv_heads * group, two * half)
    return (mixed, log_total)


def attend_back(query, keyvals, grad_mixed, log_total, bias):
    two, reps, half, width = query.shape
    kv_heads = keyvals[0].shape[-1] // (2 * HD)
    group = width // HD // kv_heads
    depth = len(keyvals)

    def heads(v):
        v = v.reshape(two, reps, half, kv_heads, group, HD)
        return v.transpose(1, 0, 2, 3, 4, 5).reshape(reps, two * half, kv_heads, group, HD)

    q, go = heads(query), heads(grad_mixed)
    kv = jnp.stack(keyvals).reshape(depth, two, reps, half, 2, kv_heads, HD)
    kv = kv.transpose(4, 2, 0, 1, 3, 5, 6).reshape(2, reps, -1, kv_heads, HD)
    scale = HD ** (-0.5)
    scores = jnp.einsum("jtkgd,jskd->jkgst", q, kv[0], preferred_element_type=f32) * scale
    scores = scores + bias[:, None, None].astype(f32)
    lse = log_total.reshape(reps, kv_heads, group, 1, two * half)
    probs = jnp.exp(scores - lse)
    grad_probs = jnp.einsum("jtkgd,jskd->jkgst", go, kv[1], preferred_element_type=f32)
    inner = jnp.sum(probs * grad_probs, axis=-2, keepdims=True)
    grad_scores = (probs * (grad_probs - inner)).astype(bf16)
    grad_q = jnp.einsum("jkgst,jskd->jtkgd", grad_scores, kv[0], preferred_element_type=f32) * scale
    grad_k = jnp.einsum("jkgst,jtkgd->jskd", grad_scores, q, preferred_element_type=f32) * scale
    grad_v = jnp.einsum("jkgst,jtkgd->jskd", probs.astype(bf16), go, preferred_element_type=f32)
    grad_q = grad_q.reshape(reps, two, half, width).transpose(1, 0, 2, 3)
    grad_kv = jnp.stack([grad_k, grad_v]).astype(bf16)
    grad_kv = grad_kv.reshape(2, reps, depth, two, half, kv_heads, HD)
    grad_kv = grad_kv.transpose(2, 3, 1, 4, 0, 5, 6).reshape(depth, two, reps, half, -1)
    return (grad_q, [grad_kv[i] for i in range(depth)])


def shards(
    tokens,
    segment_ids,
    cotangent,
    norm_attn,
    w_query,
    w_key,
    w_value,
    w_output,
    norm_ffn,
    w_gate,
    w_up,
    w_down,
):
    core = lax.axis_index("section")
    layer_z = lax.axis_index("fsdp")
    rep = lax.axis_index("rep")
    depth = lax.axis_size("fsdp")
    reps = lax.axis_size("rep")
    rows, width = tokens.shape[2:]
    half = rows // 2
    count = reps * rows
    q_width = HQ * HD // reps
    k_width = KVH * HD // reps
    ff_width = FF // reps
    ff_piece = FF // (reps * depth)

    gains = lax.all_gather(
        jnp.concatenate([norm_attn, norm_ffn], axis=0), ("section", "fsdp"), axis=0, tiled=False
    )
    gains = gains.reshape(2, depth, 2, -1).transpose(0, 2, 1, 3).reshape(2, 2, width).astype(f32)
    own_ids = lax.dynamic_index_in_dim(segment_ids[0], core, 0, keepdims=False)
    ids = lax.all_gather(own_ids, ("rep", "fsdp"), axis=0, tiled=True).reshape(reps, depth * rows)
    ids = jnp.stack([lax.dynamic_index_in_dim(ids, rep ^ j, 0, keepdims=False) for j in range(reps)])

    def columns(weight, size):
        return lax.dynamic_slice_in_dim(weight[0], rep * size, size, axis=1)

    def hidden_columns(weight):
        cut = weight[0].reshape(weight.shape[1], depth, reps, ff_piece)
        return lax.dynamic_index_in_dim(cut, rep, 2, keepdims=False).reshape(weight.shape[1], -1)

    qkv_cut = jnp.concatenate(
        [columns(w_query, q_width), columns(w_key, k_width), columns(w_value, k_width)], axis=1
    )
    out_rows = w_output.shape[1] // reps
    out_cut = lax.dynamic_slice_in_dim(w_output[0], rep * out_rows, out_rows)
    ffn_cut = jnp.concatenate([hidden_columns(w_gate), hidden_columns(w_up)], axis=1)
    down_cut = lax.dynamic_slice_in_dim(w_down[0], rep * ff_piece, ff_piece)

    def spread(pieces):
        return [lax.all_gather(v, ("fsdp", "section"), axis=0, tiled=True) for v in pieces]

    qkv_all = spread(core_split(qkv_cut, core))
    ffn_all = spread(core_split(ffn_cut, core))
    down_all = spread(core_split(down_cut, core))
    out_all = [
        lax.all_to_all(v, "rep", 0, 0, tiled=True) for v in spread(core_split(out_cut, core))
    ]

    row_at = layer_z * rows + jnp.arange(rows)
    query_ids = lax.dynamic_slice_in_dim(ids, layer_z * rows, rows, axis=1)
    starts = jnp.sum((ids[:, None, :] < query_ids[:, :, None]).astype(jnp.int32), axis=-1)
    cosine, sine = rope_tables((row_at[None, :] - starts).astype(f32))

    def by_half(table):
        return table.reshape(reps, 2, half, 1, HD).transpose(1, 0, 2, 3, 4)

    cosine, sine = by_half(cosine), by_half(sine)
    biases = []
    for step in range(depth):
        block = jnp.maximum(layer_z - step, 0)
        key_ids = lax.dynamic_slice_in_dim(ids, block * rows, rows, axis=1)
        key_at = (layer_z - step) * rows + jnp.arange(rows)
        allowed = (key_ids[:, :, None] == query_ids[:, None, :]) & (
            (key_at[:, None] <= row_at[None, :]) & (key_at[:, None] >= 0)
        )
        biases.append(jnp.where(allowed, 0.0, masked_score).astype(bf16))
    bias = jnp.concatenate(biases, axis=1)

    def flat(value):
        return value.reshape(count, -1)

    def blocks(value):
        return value.reshape(2, reps, half, -1)

    def forward(layer, layer_in):
        gain_attn, gain_ffn = gains[layer, 0], gains[layer, 1]
        scale_in = scale_of(layer_in)
        a_all = plane_gather((layer_in * scale_in * gain_attn).astype(bf16))
        qkv = times(flat(a_all), qkv_all[layer])
        query = qkv[:, :q_width].reshape(2, reps, half, -1, HD)
        key = qkv[:, q_width : q_width + k_width].reshape(2, reps, half, -1, HD)
        query = blocks(rotary(query, cosine, sine).astype(bf16))
        key = blocks(rotary(key, cosine, sine).astype(bf16))
        value = blocks(qkv[:, q_width + k_width :].astype(bf16))
        keyval = jnp.concatenate([key, value], axis=-1)
        keyvals = [keyval] + [
            lax.ppermute(keyval, "fsdp", [(i, i + s) for i in range(depth - s)])
            for s in range(1, depth)
        ]
        mixed, log_total = attend(query, keyvals, bias)
        residual = layer_in + plane_reduce(blocks(times(flat(mixed), out_all[layer]).astype(bf16)))
        scale_mid = scale_of(residual)
        b_all = plane_gather((residual * scale_mid * gain_ffn).astype(bf16))
        pre = times(flat(b_all), ffn_all[layer])
        gate, up = pre[:, :ff_width], pre[:, ff_width:]
        hidden = (jax.nn.silu(gate) * up).astype(bf16)
        out = residual + plane_reduce(blocks(times(hidden, down_all[layer]).astype(bf16)))
        kept = (layer_in, scale_in, a_all, query, keyvals, mixed, log_total)
        return out.astype(bf16), kept + (residual, scale_mid, b_all, gate, up, hidden)

    def collect(part):
        return lax.psum_scatter(part, ("fsdp", "section"), scatter_dimension=0, tiled=True)

    def backward(layer, grad_out, kept):
        (layer_in, scale_in, a_all, query, keyvals, mixed, log_total) = kept[:7]
        (residual, scale_mid, b_all, gate, up, hidden) = kept[7:]
        gain_attn, gain_ffn = gains[layer, 0], gains[layer, 1]
        gm_all = plane_gather(grad_out)
        grad_hidden = times_back(flat(gm_all), down_all[layer])
        sig = jax.nn.sigmoid(gate)
        grad_gate = (grad_hidden * up * (sig * (1.0 + gate * (1.0 - sig)))).astype(bf16)
        grad_up = (grad_hidden * (gate * sig)).astype(bf16)
        grad_pre = jnp.concatenate([grad_gate, grad_up], axis=1)
        db = plane_reduce(blocks(times_back(grad_pre, ffn_all[layer]).astype(bf16)))
        unit = residual * scale_mid
        grad_mid, gain_grad_ffn = norm_back(db, gain_ffn, unit, scale_mid)
        grad_mid = grad_mid + grad_out.astype(f32)
        go_all = plane_gather(grad_mid.astype(bf16))
        grad_down = collect(rows_product(hidden, flat(gm_all)))
        grad_ffn = collect(rows_product(flat(b_all), grad_pre))
        grad_mixed = blocks(times_back(flat(go_all), out_all[layer]).astype(bf16))
        grad_query, grad_kv = attend_back(query, keyvals, grad_mixed, log_total, bias)
        own_kv = grad_kv[0].astype(f32)
        for s in range(1, depth):
            got = lax.ppermute(grad_kv[s], "fsdp", [(i, i - s) for i in range(s, depth)])
            own_kv = own_kv + got.astype(f32)
        grad_o = rows_product(flat(mixed), flat(go_all))
        grad_o = collect(lax.all_to_all(grad_o, "rep", 0, 0, tiled=True))
        grad_query = grad_query.reshape(2, reps, half, -1, HD)
        grad_key = own_kv[..., :k_width].reshape(2, reps, half, -1, HD)
        grad_query = rotary_back(grad_query, cosine, sine).astype(bf16)
        grad_key = rotary_back(grad_key, cosine, sine).astype(bf16)
        grad_value = own_kv[..., k_width:].astype(bf16)
        grad_qkv = jnp.concatenate([flat(grad_query), flat(grad_key), flat(grad_value)], axis=1)
        da = plane_reduce(blocks(times_back(grad_qkv, qkv_all[layer]).astype(bf16)))
        unit = layer_in * scale_in
        grad_in, gain_grad_attn = norm_back(da, gain_attn, unit, scale_in)
        grad_in = (grad_in + grad_mid).astype(bf16)
        grad_proj = collect(rows_product(flat(a_all), grad_qkv))
        return grad_in, (grad_proj, grad_o, grad_ffn, grad_down), (gain_grad_attn, gain_grad_ffn)

    own_tokens = lax.dynamic_index_in_dim(tokens[0], core, 0, keepdims=False)
    own_cotangent = lax.dynamic_index_in_dim(cotangent[0], core, 0, keepdims=False)
    out0, kept0 = forward(0, own_tokens.astype(f32))
    out1, kept1 = forward(1, out0.astype(f32))
    grad1, weights1, gain1 = backward(1, own_cotangent, kept1)
    grad0, weights0, gain0 = backward(0, grad1, kept0)

    def swapped(zero, one):
        got = lax.ppermute(jnp.where(core == 0, one, zero), "section", SWAP)
        return jnp.where(core == 0, zero, got), jnp.where(core == 0, got, one)

    outputs = jnp.stack(swapped(out0, out1))[None, None]
    input_grads = jnp.stack(swapped(grad0, grad1))[None, None]

    gain_sums = lax.psum(jnp.stack([jnp.stack(gain0), jnp.stack(gain1)]), ("section", "fsdp", "rep"))
    gain_sums = lax.dynamic_index_in_dim(gain_sums, core, 0, keepdims=False)
    piece = width // depth
    gain_sums = lax.dynamic_slice_in_dim(gain_sums, layer_z * piece, piece, axis=1)

    def whole(zero, one):
        pair = jnp.concatenate(swapped(zero, one), axis=0)
        return lax.all_gather(pair, "rep", axis=0, tiled=False)

    proj, outp, ffn, down = (whole(a, b) for a, b in zip(weights0, weights1))

    def side(value):
        return value.transpose(1, 0, 2).reshape(value.shape[1], -1).astype(f32)[None]

    def hidden_side(value):
        value = value.reshape(reps, -1, depth, ff_piece).transpose(1, 2, 0, 3)
        return value.reshape(value.shape[0], -1).astype(f32)[None]

    def stacked(value):
        return value.reshape(-1, value.shape[-1]).astype(f32)[None]

    return (
        outputs,
        input_grads,
        gain_sums[0][None],
        side(proj[..., :q_width]),
        side(proj[..., q_width : q_width + k_width]),
        side(proj[..., q_width + k_width :]),
        stacked(outp),
        gain_sums[1][None],
        hidden_side(ffn[..., :ff_width]),
        hidden_side(ffn[..., ff_width:]),
        stacked(down),
    )


def solution(mesh):
    in_specs = (
        P("rep", None, "fsdp", None),
        P("rep", None, "fsdp"),
        P("rep", None, "fsdp", None),
        P("section", "fsdp"),
        P("section", "fsdp", None),
        P("section", "fsdp", None),
        P("section", "fsdp", None),
        P("section", "fsdp", None),
        P("section", "fsdp"),
        P("section", "fsdp", None),
        P("section", "fsdp", None),
        P("section", "fsdp", None),
    )
    out_specs = (
        P("section", "rep", None, "fsdp", None),
        P("section", "rep", None, "fsdp", None),
        P("section", "fsdp"),
        P("section", "fsdp", None),
        P("section", "fsdp", None),
        P("section", "fsdp", None),
        P("section", "fsdp", None),
        P("section", "fsdp"),
        P("section", "fsdp", None),
        P("section", "fsdp", None),
        P("section", "fsdp", None),
    )
    return jax.shard_map(shards, mesh=mesh, in_specs=in_specs, out_specs=out_specs, check_vma=False)
```

```python
import functools

import jax
import jax.numpy as jnp
from jax import lax
from jax.experimental import pallas as pl
from jax.experimental.pallas import tpu as pltpu
from jax.sharding import PartitionSpec as P

HQ = 32
KVH = 8
HD = 64
FF = 8192

epsilon = 1e-05
rope_base = 500000.0
masked_score = -1e30
bf16 = jnp.bfloat16
f32 = jnp.float32
SWAP = [(0, 1), (1, 0)]


def partner(value, bit):
    count = lax.axis_size("rep")
    return lax.ppermute(value, "rep", [(i, i ^ bit) for i in range(count)])


def bit_list(count):
    found = []
    bit = 1
    while bit < count:
        found.append(bit)
        bit *= 2
    return found


def gather_start(own):
    half = own.shape[0] // 2
    return own[None, :half], own[None, half:]


def gather_step(state, at):
    bits = bit_list(lax.axis_size("rep"))
    first, second = state
    first = jnp.concatenate([first, partner(first, bits[at])], axis=0)
    other = partner(second, bits[-1 - at])
    second = jnp.stack([second, other], axis=1).reshape((-1,) + second.shape[1:])
    return first, second


def gather_rest(state, at):
    for step in range(at, len(bit_list(lax.axis_size("rep")))):
        state = gather_step(state, step)
    return jnp.stack(state)


def plane_gather(own):
    return gather_rest(gather_start(own), 0)


def plane_reduce(parts):
    bits = bit_list(lax.axis_size("rep"))
    first, second = parts[0], parts[1]
    for bit in bits[::-1]:
        keep, away = first[:bit], first[bit:]
        first = keep.astype(f32) + partner(away.astype(bf16), bit).astype(f32)
    for bit in bits:
        pair = second.reshape((-1, 2) + second.shape[1:])
        keep, away = pair[:, 0], pair[:, 1]
        second = keep.astype(f32) + partner(away.astype(bf16), bit).astype(f32)
    return jnp.concatenate([first[0], second[0]], axis=0)


def rope_tables(positions):
    half_size = HD // 2
    frequency = rope_base ** (-(jnp.arange(half_size).astype(f32) * 2.0) / HD)
    angles = positions[..., None] * frequency
    angles = jnp.concatenate([angles, angles], axis=-1)
    return (jnp.cos(angles), jnp.sin(angles))


def rotary(values, cosine_table, sine_table):
    half_size = values.shape[-1] // 2
    turned = jnp.concatenate([-values[..., half_size:], values[..., :half_size]], axis=-1)
    return values * cosine_table + turned * sine_table


def rotary_back(grad_rot, cosine_table, sine_table):
    half_size = grad_rot.shape[-1] // 2
    scaled = grad_rot * sine_table
    return grad_rot * cosine_table + jnp.concatenate(
        [scaled[..., half_size:], -scaled[..., :half_size]], axis=-1
    )


def times(left, weight):
    return jnp.dot(left, weight, preferred_element_type=f32)


def times_back(left, weight):
    return lax.dot_general(
        left, weight, (((1,), (1,)), ((), ())), preferred_element_type=f32
    )


def rows_product(left, right):
    return lax.dot_general(
        left, right, (((0,), (0,)), ((), ())), preferred_element_type=f32
    ).astype(bf16)


def scale_of(values):
    return lax.rsqrt(jnp.mean(values * values, axis=-1, keepdims=True) + epsilon)


def norm_back(grad, gain, unit, scale):
    scaled = gain * grad
    out = scale * (scaled - unit * jnp.mean(scaled * unit, axis=-1, keepdims=True))
    return (out, jnp.sum(grad * unit, axis=0))


def sequence(ref):
    return ref[:, 0].reshape(-1, ref.shape[-1])


def scaled(value):
    return (value.astype(f32) * HD ** (-0.5)).astype(bf16)


def dot(left, right, left_dim, right_dim):
    return lax.dot_general(
        left, right, (((left_dim,), (right_dim,)), ((), ())), preferred_element_type=f32
    )


def attend_kernel(depth, query_ref, bias_ref, *refs):
    mixed_ref, log_ref = refs[depth:]
    keyval = jnp.concatenate([sequence(ref) for ref in refs[:depth]], axis=0)
    query = scaled(sequence(query_ref))
    bias = bias_ref[0].astype(f32)
    k_width = keyval.shape[1] // 2
    heads = query.shape[1] // HD
    group = heads // (k_width // HD)
    columns = []
    for head in range(heads):
        at = head // group * HD
        key = keyval[:, at : at + HD]
        value = keyval[:, k_width + at : k_width + at + HD]
        scores = dot(key, query[:, head * HD : (head + 1) * HD], 1, 1) + bias
        row_max = jnp.max(scores, axis=0, keepdims=True)
        weights = jnp.exp(scores - row_max)
        total = jnp.sum(weights, axis=0, keepdims=True)
        probs = (weights * (1.0 / total)).astype(bf16)
        columns.append(dot(value, probs, 0, 0))
        log_ref[0, head : head + 1, :] = row_max + jnp.log(total)
    mixed = jnp.concatenate(columns, axis=0).T.astype(bf16)
    mixed_ref[:, 0] = mixed.reshape(2, -1, mixed.shape[1])


def attend_back_kernel(depth, query_ref, grad_ref, log_ref, bias_ref, *refs):
    grad_query_ref, grad_refs = refs[depth], refs[depth + 1 :]
    keyval = jnp.concatenate([sequence(ref) for ref in refs[:depth]], axis=0)
    query = scaled(sequence(query_ref))
    grad = sequence(grad_ref)
    bias = bias_ref[0].astype(f32)
    k_width = keyval.shape[1] // 2
    heads = query.shape[1] // HD
    group = heads // (k_width // HD)
    columns, grad_keys, grad_values = [], [], []
    for head in range(heads):
        at = head // group * HD
        key = keyval[:, at : at + HD]
        value = keyval[:, k_width + at : k_width + at + HD]
        own_query = query[:, head * HD : (head + 1) * HD]
        own_grad = grad[:, head * HD : (head + 1) * HD]
        scores = dot(key, own_query, 1, 1) + bias
        probs = jnp.exp(scores - log_ref[0, head : head + 1, :])
        grad_probs = dot(value, own_grad, 1, 1)
        inner = jnp.sum(probs * grad_probs, axis=0, keepdims=True)
        grad_scores = (probs * (grad_probs - inner)).astype(bf16)
        columns.append(dot(key, grad_scores, 0, 0))
        grad_key = dot(grad_scores, own_query, 1, 0)
        grad_value = dot(probs.astype(bf16), own_grad, 1, 0)
        if head % group == 0:
            grad_keys.append(grad_key)
            grad_values.append(grad_value)
        else:
            grad_keys[-1] = grad_keys[-1] + grad_key
            grad_values[-1] = grad_values[-1] + grad_value
    grad_query = jnp.concatenate(columns, axis=0).T * HD ** (-0.5)
    grad_query_ref[:, 0] = grad_query.reshape(2, -1, grad_query.shape[1])
    both = jnp.concatenate(grad_keys + grad_values, axis=1).astype(bf16)
    rows = both.shape[0] // depth
    for step, ref in enumerate(grad_refs):
        part = both[step * rows : (step + 1) * rows]
        ref[:, 0] = part.reshape(2, rows // 2, part.shape[1])


def sequence_spec(array):
    two, _, half, columns = array.shape
    return pl.BlockSpec((two, 1, half, columns), lambda j: (0, j, 0, 0))


def row_spec(array):
    return pl.BlockSpec((1,) + array.shape[1:], lambda j: (j, 0, 0))


def attend(query, keyvals, bias):
    two, reps, half, width = query.shape
    logs = jax.ShapeDtypeStruct((reps, width // HD, two * half), f32)
    cells = reps * width * two * half * bias.shape[1]
    return pl.pallas_call(
        functools.partial(attend_kernel, len(keyvals)),
        grid=(reps,),
        in_specs=[sequence_spec(query), row_spec(bias)] + [sequence_spec(v) for v in keyvals],
        out_specs=[sequence_spec(query), row_spec(logs)],
        out_shape=[jax.ShapeDtypeStruct(query.shape, bf16), logs],
        compiler_params=pltpu.CompilerParams(vmem_limit_bytes=48 << 20),
        cost_estimate=pl.CostEstimate(
            flops=16 * cells, bytes_accessed=8 << 20, transcendentals=cells // HD
        ),
        name="attend",
    )(query, bias, *keyvals)


def attend_back(query, keyvals, grad_mixed, log_total, bias):
    two, reps, half, width = query.shape
    cells = reps * width * two * half * bias.shape[1]
    outs = pl.pallas_call(
        functools.partial(attend_back_kernel, len(keyvals)),
        grid=(reps,),
        in_specs=[sequence_spec(query), sequence_spec(grad_mixed), row_spec(log_total)]
        + [row_spec(bias)]
        + [sequence_spec(v) for v in keyvals],
        out_specs=[sequence_spec(query)] + [sequence_spec(v) for v in keyvals],
        out_shape=[jax.ShapeDtypeStruct(query.shape, f32)]
        + [jax.ShapeDtypeStruct(v.shape, bf16) for v in keyvals],
        compiler_params=pltpu.CompilerParams(vmem_limit_bytes=48 << 20),
        cost_estimate=pl.CostEstimate(
            flops=40 * cells, bytes_accessed=12 << 20, transcendentals=cells // HD
        ),
        name="attend_back",
    )(query, grad_mixed, log_total, bias, *keyvals)
    return outs[0], outs[1:]


def by_core(which, refs, write):
    for at, ref in enumerate(refs):
        pl.when(which == at)(functools.partial(write, ref))


def columns_kernel(info, zero, one_sent, zero_sent, one, out_ref):
    which = info[0] + 2 * pl.program_id(0)
    reps, _, piece = zero.shape[1:]

    def write(ref):
        for rep in range(reps):
            out_ref[:, rep * piece : (rep + 1) * piece] = ref[0, rep ^ info[1]].astype(f32)

    by_core(which, (zero, one_sent, zero_sent, one), write)


def rows_kernel(info, zero, one_sent, zero_sent, one, out_ref):
    which = info[0] + 2 * pl.program_id(1)

    def write(ref):
        out_ref[...] = ref[0, 0].astype(f32)

    by_core(which, (zero, one_sent, zero_sent, one), write)


def proj_kernel(info, zero, one_sent, zero_sent, one, query_ref, key_ref, value_ref):
    which = info[0] + 2 * pl.program_id(0)
    reps = zero.shape[1]

    def write(ref):
        for rep in range(reps):
            block = ref[0, rep ^ info[1]].astype(f32)
            start = 0
            for out_ref in (query_ref, key_ref, value_ref):
                size = out_ref.shape[1] // reps
                out_ref[:, rep * size : (rep + 1) * size] = block[:, start : start + size]
                start += size

    by_core(which, (zero, one_sent, zero_sent, one), write)


def assembled(kernel, grid, half_dim, block, index, out_blocks, out_index, out_shapes, info, four):
    def chosen(at):
        def where_from(*steps):
            taken = steps[-1][0] + 2 * steps[half_dim] == at
            return tuple(jnp.where(taken, v, 0) for v in index(*steps))

        return where_from

    return pl.pallas_call(
        kernel,
        grid_spec=pltpu.PrefetchScalarGridSpec(
            num_scalar_prefetch=1,
            grid=grid,
            in_specs=[pl.BlockSpec(block, chosen(at)) for at in range(4)],
            out_specs=[pl.BlockSpec(b, out_index) for b in out_blocks],
        ),
        out_shape=[jax.ShapeDtypeStruct(v, f32) for v in out_shapes],
        compiler_params=pltpu.CompilerParams(vmem_limit_bytes=40 << 20),
        name=kernel.__name__,
    )(info, *four)


def assemble_columns(info, four, offset, piece, pieces):
    _, reps, rows, _ = four[0].shape
    return assembled(
        columns_kernel,
        (2, 2, pieces),
        0,
        (1, reps, rows, piece),
        lambda k, sub, at, info: (sub, 0, 0, offset + at),
        [(rows, reps * piece)],
        lambda k, sub, at, info: (2 * k + sub, at),
        [(4 * rows, reps * piece * pieces)],
        info,
        four,
    )[0]


def assemble_rows(info, four):
    _, reps, rows, columns = four[0].shape
    return assembled(
        rows_kernel,
        (reps, 2, 2),
        1,
        (1, 1, rows, columns),
        lambda rep, k, sub, info: (sub, rep ^ info[1], 0, 0),
        [(rows, columns)],
        lambda rep, k, sub, info: (4 * rep + 2 * k + sub, 0),
        [(4 * reps * rows, columns)],
        info,
        four,
    )[0]


def assemble_proj(info, four, sizes):
    _, reps, rows, columns = four[0].shape
    return assembled(
        proj_kernel,
        (2, 2),
        0,
        (1, reps, rows, columns),
        lambda k, sub, info: (sub, 0, 0, 0),
        [(rows, reps * size) for size in sizes],
        lambda k, sub, info: (2 * k + sub, 0),
        [(4 * rows, reps * size) for size in sizes],
        info,
        four,
    )


def together(*values):
    return lax.optimization_barrier(values)


def sum_everywhere(value):
    for axis in ("rep", "fsdp", "section"):
        count = lax.axis_size(axis)
        for bit in bit_list(count):
            value = value + lax.ppermute(value, axis, [(i, i ^ bit) for i in range(count)])
    return value


def shards(
    tokens,
    segment_ids,
    cotangent,
    norm_attn,
    w_query,
    w_key,
    w_value,
    w_output,
    norm_ffn,
    w_gate,
    w_up,
    w_down,
):
    core = lax.axis_index("section")
    layer_z = lax.axis_index("fsdp")
    rep = lax.axis_index("rep")
    depth = lax.axis_size("fsdp")
    reps = lax.axis_size("rep")
    rows, width = tokens.shape[2:]
    half = rows // 2
    count = reps * rows
    q_width = HQ * HD // reps
    k_width = KVH * HD // reps
    ff_width = FF // reps
    ff_piece = FF // (reps * depth)

    def back(value, step):
        return lax.ppermute(value, "fsdp", [(i, i + step) for i in range(depth - step)])

    def by_layer(own, got):
        return (jnp.where(core == 0, own, got), jnp.where(core == 0, got, own))

    own_gain = jnp.concatenate([norm_attn, norm_ffn], axis=0)
    turned = jnp.stack(
        [own_gain]
        + [
            lax.ppermute(own_gain, "fsdp", [(i, (i + s) % depth) for i in range(depth)])
            for s in range(1, depth)
        ]
    )
    own_gain = jnp.concatenate(
        [
            lax.dynamic_index_in_dim(turned, (layer_z - k + depth) % depth, 0, keepdims=False)
            for k in range(depth)
        ],
        axis=1,
    ).astype(f32)
    gains = by_layer(own_gain, lax.ppermute(own_gain, "section", SWAP))

    plane_ids = lax.dynamic_index_in_dim(segment_ids[0], core, 0, keepdims=True)
    for bit in bit_list(reps):
        plane_ids = jnp.concatenate([plane_ids, partner(plane_ids, bit)], axis=0)
    ids = [plane_ids] + [back(plane_ids, step) for step in range(1, depth)]

    def split(cut, total):
        size = total // 2
        got = lax.ppermute(cut((1 - core) * size, size), "section", SWAP)
        return by_layer(cut(core * size, size), got)

    def spread(pieces):
        return [lax.all_gather(v, ("fsdp", "section"), axis=0, tiled=True) for v in pieces]

    def qkv_cut(row, size):
        parts = ((w_query, q_width), (w_key, k_width), (w_value, k_width))
        return jnp.concatenate(
            [lax.dynamic_slice(w[0], (row, rep * n), (size, n)) for w, n in parts], axis=1
        )

    def ffn_cut(row, size):
        return jnp.concatenate(
            [
                lax.dynamic_slice(
                    w[0], (row, k * reps * ff_piece + rep * ff_piece), (size, ff_piece)
                )
                for w in (w_gate, w_up)
                for k in range(depth)
            ],
            axis=1,
        )

    out_rows = w_output.shape[1] // reps

    def attn_cut(row, size):
        height = out_rows * size // w_query.shape[1]
        first = rep * out_rows + row * out_rows // w_query.shape[1]
        out = lax.dynamic_slice_in_dim(w_output[0], first, height)
        return jnp.concatenate([qkv_cut(row, size), out.reshape(size, -1)], axis=1)

    def all_ffn_cut(row, size):
        height = ff_piece * size // w_gate.shape[1]
        first = rep * ff_piece + row * ff_piece // w_gate.shape[1]
        down = lax.dynamic_slice_in_dim(w_down[0], first, height)
        return jnp.concatenate([ffn_cut(row, size), down.reshape(size, -1)], axis=1)

    attn_all = spread(split(attn_cut, w_query.shape[1]))
    qkv_width = q_width + 2 * k_width
    qkv_all = [v[:, :qkv_width] for v in attn_all]
    out_all = [
        lax.all_to_all(v[:, qkv_width:].reshape(-1, width), "rep", 0, 0, tiled=True)
        for v in attn_all
    ]
    both_all = spread(split(all_ffn_cut, w_gate.shape[1]))
    ffn_all = [v[:, : 2 * ff_width] for v in both_all]
    down_all = [v[:, 2 * ff_width :].reshape(ff_width, width) for v in both_all]

    starts = jnp.zeros((reps, rows), jnp.int32)
    biases = []
    within = jnp.arange(rows)
    for step in range(depth):
        key_ids, here = ids[step][:, :, None], plane_ids[:, None, :]
        exists = layer_z >= step
        starts = starts + jnp.sum((exists & (key_ids < here)).astype(jnp.int32), axis=1)
        allowed = exists & (key_ids == here)
        if step == 0:
            allowed = allowed & (within[:, None] <= within[None, :])
        biases.append(jnp.where(allowed, 0.0, masked_score).astype(bf16))
    bias = jnp.concatenate(biases, axis=1)
    cosine, sine = rope_tables((layer_z * rows + within - starts).astype(f32))

    def by_half(table):
        return table.reshape(reps, 2, half, 1, HD).transpose(1, 0, 2, 3, 4)

    cosine, sine = by_half(cosine), by_half(sine)

    def flat(value):
        return value.reshape(count, -1)

    def blocks(value):
        return value.reshape(2, reps, half, -1)

    def forward(layer, layer_in):
        gain_attn, gain_ffn = gains[layer][0], gains[layer][1]
        scale_in = scale_of(layer_in)
        a_all = plane_gather((layer_in * scale_in * gain_attn).astype(bf16))
        qkv = times(flat(a_all), qkv_all[layer])
        query = qkv[:, :q_width].reshape(2, reps, half, -1, HD)
        key = qkv[:, q_width : q_width + k_width].reshape(2, reps, half, -1, HD)
        query = blocks(rotary(query, cosine, sine).astype(bf16))
        key = blocks(rotary(key, cosine, sine).astype(bf16))
        value = blocks(qkv[:, q_width + k_width :].astype(bf16))
        keyval = jnp.concatenate([key, value], axis=-1)
        keyvals = [keyval] + [
            back(keyval, step) for step in range(1, depth)
        ]
        mixed, log_total = attend(query, keyvals, bias)
        residual = layer_in + plane_reduce(blocks(times(flat(mixed), out_all[layer]).astype(bf16)))
        scale_mid = scale_of(residual)
        b_all = plane_gather((residual * scale_mid * gain_ffn).astype(bf16))
        pre = times(flat(b_all), ffn_all[layer])
        gate, up = pre[:, :ff_width], pre[:, ff_width:]
        hidden = (jax.nn.silu(gate) * up).astype(bf16)
        out = residual + plane_reduce(blocks(times(hidden, down_all[layer]).astype(bf16)))
        kept = (layer_in, scale_in, a_all, query, keyvals, mixed, log_total)
        return out.astype(bf16), kept + (residual, scale_mid, b_all, gate, up, hidden)

    def core_sum(part):
        cube = part.reshape(depth, 2, -1, part.shape[1])
        mine = lax.dynamic_index_in_dim(cube, core, 1, keepdims=False)
        sent = lax.dynamic_index_in_dim(cube, 1 - core, 1, keepdims=False)
        got = lax.ppermute(sent, "section", SWAP)
        total = (mine.astype(f32) + got.astype(f32)).astype(bf16)
        return total.reshape(-1, part.shape[1])

    def collect(total):
        return lax.psum_scatter(total, "fsdp", scatter_dimension=0, tiled=True)

    def backward(layer, grad_out, kept, earlier):
        (layer_in, scale_in, a_all, query, keyvals, mixed, log_total) = kept[:7]
        (residual, scale_mid, b_all, gate, up, hidden) = kept[7:]
        gain_attn, gain_ffn = gains[layer][0], gains[layer][1]
        last = earlier is not None
        if last:
            old_proj, old_o, old_ffn, old_down = earlier
            grad_out, old_ffn = together(grad_out, old_ffn)
        gm_all = flat(plane_gather(grad_out))
        gm_all, part_down = together(gm_all, rows_product(hidden, gm_all))
        if last:
            gm_all, old_ffn, old_down = together(gm_all, old_ffn, old_down)
            ffn_state = gather_step(gather_start(old_ffn), 0)
            down_state = gather_step(gather_start(old_down), 0)
        grad_hidden = times_back(gm_all, down_all[layer])
        sig = jax.nn.sigmoid(gate)
        grad_gate = (grad_hidden * up * (sig * (1.0 + gate * (1.0 - sig)))).astype(bf16)
        grad_up = (grad_hidden * (gate * sig)).astype(bf16)
        grad_pre = jnp.concatenate([grad_gate, grad_up], axis=1)
        grad_pre, part_down = together(grad_pre, core_sum(part_down))
        own_down = collect(part_down)
        if last:
            grad_pre, *states = together(grad_pre, *ffn_state, *down_state)
            ffn_state, down_state = states[:2], states[2:]
            whole_down = gather_rest(down_state, 1)
        db = blocks(times_back(grad_pre, ffn_all[layer]).astype(bf16))
        db, grad_pre = together(db, grad_pre)
        if last:
            db, whole_down, old_o, old_proj = together(db, whole_down, old_o, old_proj)
        db = plane_reduce(db)
        unit = residual * scale_mid
        grad_mid, gain_grad_ffn = norm_back(db, gain_ffn, unit, scale_mid)
        grad_mid = grad_mid + grad_out.astype(f32)
        go = grad_mid.astype(bf16)
        go, part_ffn = together(go, core_sum(rows_product(flat(b_all), grad_pre)))
        own_ffn = collect(part_ffn)
        go_all = flat(plane_gather(go))
        grad_mixed = blocks(times_back(go_all, out_all[layer]).astype(bf16))
        part_o = lax.all_to_all(rows_product(flat(mixed), go_all), "rep", 0, 0, tiled=True)
        if last:
            tied = together(grad_mixed, old_o, old_proj, *ffn_state)
            grad_mixed, old_o, old_proj, ffn_state = tied[0], tied[1], tied[2], tied[3:]
            wholes = (
                plane_gather(old_proj),
                plane_gather(old_o),
                gather_rest(ffn_state, 1),
                whole_down,
            )
        grad_query, grad_kv = attend_back(query, keyvals, grad_mixed, log_total, bias)
        grad_query, own_down, *grad_kv = together(grad_query, own_down, *grad_kv)
        own_kv = grad_kv[0].astype(f32)
        for s in range(1, depth):
            got = lax.ppermute(grad_kv[s], "fsdp", [(i, i - s) for i in range(s, depth)])
            own_kv = own_kv + got.astype(f32)
        own_o = collect(core_sum(part_o))
        grad_query = grad_query.reshape(2, reps, half, -1, HD)
        grad_key = own_kv[..., :k_width].reshape(2, reps, half, -1, HD)
        grad_query = rotary_back(grad_query, cosine, sine).astype(bf16)
        grad_key = rotary_back(grad_key, cosine, sine).astype(bf16)
        grad_value = own_kv[..., k_width:].astype(bf16)
        grad_qkv = jnp.concatenate([flat(grad_query), flat(grad_key), flat(grad_value)], axis=1)
        da = blocks(times_back(grad_qkv, qkv_all[layer]).astype(bf16))
        da, grad_qkv = together(da, grad_qkv)
        if last:
            da, *wholes = together(da, *wholes)
            sent = [lax.ppermute(v, "section", [(0, 1)]) for v in wholes]
            own_down = plane_gather(own_down)
        da = plane_reduce(da)
        unit = layer_in * scale_in
        grad_in, gain_grad_attn = norm_back(da, gain_attn, unit, scale_in)
        grad_in = (grad_in + grad_mid).astype(bf16)
        grad_in, part_proj = together(grad_in, core_sum(rows_product(flat(a_all), grad_qkv)))
        own_proj = collect(part_proj)
        gain_grads = jnp.stack([gain_grad_attn, gain_grad_ffn])
        if not last:
            return grad_in, (own_proj, own_o, own_ffn, own_down), gain_grads, None
        tied = together(grad_in, own_ffn, own_o, own_down, *sent)
        grad_in, own_ffn, own_o, own_down, sent = tied[0], tied[1], tied[2], tied[3], tied[4:]
        sums = (plane_gather(own_proj), plane_gather(own_o), plane_gather(own_ffn), own_down)
        return grad_in, sums, gain_grads, list(zip(wholes, sent))

    own_tokens = lax.dynamic_index_in_dim(tokens[0], core, 0, keepdims=False)
    own_cotangent = lax.dynamic_index_in_dim(cotangent[0], core, 0, keepdims=False)
    out0, kept0 = forward(0, own_tokens.astype(f32))
    out1, kept1 = forward(1, out0.astype(f32))
    grad1, sums1, gain1, _ = backward(1, own_cotangent, kept1, None)
    grad0, whole0, gain0, whole1 = backward(0, grad1, kept0, sums1)

    def swapped(zero, one):
        got = lax.ppermute(jnp.where(core == 0, one, zero), "section", SWAP)
        return jnp.where(core == 0, zero, got), jnp.where(core == 0, got, one)

    outputs = jnp.stack(swapped(out0, out1))[None, None]
    input_grads = jnp.stack(swapped(grad0, grad1))[None, None]

    gain_sums = sum_everywhere(jnp.concatenate([gain0, gain1], axis=0))
    gain_sums = gain_sums.reshape(2, 2, depth, -1)
    gain_sums = lax.dynamic_index_in_dim(gain_sums, core, 0, keepdims=False)
    gain_sums = lax.dynamic_index_in_dim(gain_sums, layer_z, 1, keepdims=False)

    info = jnp.stack([core, rep]).astype(jnp.int32)

    def four(zero, one):
        return (zero, one[1], lax.ppermute(zero, "section", [(1, 0)]), one[0])

    proj, outp, ffn, down = (four(a, b) for a, b in zip(whole0, whole1))
    grad_gate = assemble_columns(info, ffn, 0, ff_piece, depth)
    grad_up = assemble_columns(info, ffn, depth, ff_piece, depth)
    grad_down = assemble_rows(info, down)
    grad_output = assemble_rows(info, outp)
    grad_query, grad_key, grad_value = assemble_proj(info, proj, (q_width, k_width, k_width))
    return (
        outputs,
        input_grads,
        gain_sums[0][None],
        grad_query[None],
        grad_key[None],
        grad_value[None],
        grad_output[None],
        gain_sums[1][None],
        grad_gate[None],
        grad_up[None],
        grad_down[None],
    )


def solution(mesh):
    in_specs = (
        P("rep", None, "fsdp", None),
        P("rep", None, "fsdp"),
        P("rep", None, "fsdp", None),
        P("section", "fsdp"),
        P("section", "fsdp", None),
        P("section", "fsdp", None),
        P("section", "fsdp", None),
        P("section", "fsdp", None),
        P("section", "fsdp"),
        P("section", "fsdp", None),
        P("section", "fsdp", None),
        P("section", "fsdp", None),
    )
    out_specs = (
        P("section", "rep", None, "fsdp", None),
        P("section", "rep", None, "fsdp", None),
        P("section", "fsdp"),
        P("section", "fsdp", None),
        P("section", "fsdp", None),
        P("section", "fsdp", None),
        P("section", "fsdp", None),
        P("section", "fsdp"),
        P("section", "fsdp", None),
        P("section", "fsdp", None),
        P("section", "fsdp", None),
    )
    return jax.shard_map(shards, mesh=mesh, in_specs=in_specs, out_specs=out_specs, check_vma=False)
```

```python
import functools

import jax
import jax.numpy as jnp
from jax import lax
from jax.experimental import pallas as pl
from jax.experimental.pallas import tpu as pltpu
from jax.sharding import PartitionSpec as P

HQ = 32
KVH = 8
HD = 64
FF = 8192

epsilon = 1e-05
rope_base = 500000.0
masked_score = -1e30
bf16 = jnp.bfloat16
f32 = jnp.float32
SWAP = [(0, 1), (1, 0)]


def partner(value, bit):
    count = lax.axis_size("rep")
    return lax.ppermute(value, "rep", [(i, i ^ bit) for i in range(count)])


def bit_list(count):
    found = []
    bit = 1
    while bit < count:
        found.append(bit)
        bit *= 2
    return found


def gather_start(own):
    half = own.shape[0] // 2
    return own[None, :half], own[None, half:]


def gather_step(state, at):
    bits = bit_list(lax.axis_size("rep"))
    first, second = state
    first = jnp.concatenate([first, partner(first, bits[at])], axis=0)
    other = partner(second, bits[-1 - at])
    second = jnp.stack([second, other], axis=1).reshape((-1,) + second.shape[1:])
    return first, second


def gather_rest(state, at):
    for step in range(at, len(bit_list(lax.axis_size("rep")))):
        state = gather_step(state, step)
    return jnp.stack(state)


def plane_gather(own):
    return gather_rest(gather_start(own), 0)


def plane_reduce(parts):
    bits = bit_list(lax.axis_size("rep"))
    first, second = parts[0], parts[1]
    for bit in bits[::-1]:
        keep, away = first[:bit], first[bit:]
        first = keep.astype(f32) + partner(away.astype(bf16), bit).astype(f32)
    for bit in bits:
        pair = second.reshape((-1, 2) + second.shape[1:])
        keep, away = pair[:, 0], pair[:, 1]
        second = keep.astype(f32) + partner(away.astype(bf16), bit).astype(f32)
    return jnp.concatenate([first[0], second[0]], axis=0)


def rope_tables(positions):
    half_size = HD // 2
    frequency = rope_base ** (-(jnp.arange(half_size).astype(f32) * 2.0) / HD)
    angles = positions[..., None] * frequency
    cosine, sine = jnp.cos(angles), jnp.sin(angles)
    return (
        jnp.concatenate([cosine] * 4, axis=-1),
        jnp.concatenate([-sine, sine] * 2, axis=-1),
    )


def times(left, weight):
    return jnp.dot(left, weight, preferred_element_type=f32)


def times_back(left, weight):
    return lax.dot_general(
        left, weight, (((1,), (1,)), ((), ())), preferred_element_type=f32
    )


def scale_of(values):
    return lax.rsqrt(jnp.mean(values * values, axis=-1, keepdims=True) + epsilon)


def norm_back(grad, gain, unit, scale):
    scaled = gain * grad
    out = scale * (scaled - unit * jnp.mean(scaled * unit, axis=-1, keepdims=True))
    return (out, jnp.sum(grad * unit, axis=0))


def sequence(ref):
    return ref[:, 0].reshape(-1, ref.shape[-1])


def scaled(value):
    return (value.astype(f32) * HD ** (-0.5)).astype(bf16)


def dot(left, right, left_dim, right_dim):
    return lax.dot_general(
        left, right, (((left_dim,), (right_dim,)), ((), ())), preferred_element_type=f32
    )


def attend_kernel(depth, query_ref, bias_ref, *refs):
    mixed_ref, log_ref = refs[depth:]
    keyval = jnp.concatenate([sequence(ref) for ref in refs[:depth]], axis=0)
    query = scaled(sequence(query_ref))
    bias = bias_ref[0].astype(f32)
    k_width = keyval.shape[1] // 2
    heads = query.shape[1] // HD
    group = heads // (k_width // HD)
    columns = []
    for head in range(heads):
        at = head // group * HD
        key = keyval[:, at : at + HD]
        value = keyval[:, k_width + at : k_width + at + HD]
        scores = dot(key, query[:, head * HD : (head + 1) * HD], 1, 1) + bias
        row_max = jnp.max(scores, axis=0, keepdims=True)
        weights = jnp.exp(scores - row_max)
        total = jnp.sum(weights, axis=0, keepdims=True)
        probs = (weights * (1.0 / total)).astype(bf16)
        columns.append(dot(value, probs, 0, 0))
        log_ref[0, head : head + 1, :] = row_max + jnp.log(total)
    mixed = jnp.concatenate(columns, axis=0).T.astype(bf16)
    mixed_ref[:, 0] = mixed.reshape(2, -1, mixed.shape[1])


def attend_back_kernel(depth, query_ref, grad_ref, log_ref, bias_ref, *refs):
    grad_query_ref, grad_refs = refs[depth], refs[depth + 1 :]
    keyval = jnp.concatenate([sequence(ref) for ref in refs[:depth]], axis=0)
    query = scaled(sequence(query_ref))
    grad = sequence(grad_ref)
    bias = bias_ref[0].astype(f32)
    k_width = keyval.shape[1] // 2
    heads = query.shape[1] // HD
    group = heads // (k_width // HD)
    columns, grad_keys, grad_values = [], [], []
    for head in range(heads):
        at = head // group * HD
        key = keyval[:, at : at + HD]
        value = keyval[:, k_width + at : k_width + at + HD]
        own_query = query[:, head * HD : (head + 1) * HD]
        own_grad = grad[:, head * HD : (head + 1) * HD]
        scores = dot(key, own_query, 1, 1) + bias
        probs = jnp.exp(scores - log_ref[0, head : head + 1, :])
        grad_probs = dot(value, own_grad, 1, 1)
        inner = jnp.sum(probs * grad_probs, axis=0, keepdims=True)
        grad_scores = (probs * (grad_probs - inner)).astype(bf16)
        columns.append(dot(key, grad_scores, 0, 0))
        grad_key = dot(grad_scores, own_query, 1, 0)
        grad_value = dot(probs.astype(bf16), own_grad, 1, 0)
        if head % group == 0:
            grad_keys.append(grad_key)
            grad_values.append(grad_value)
        else:
            grad_keys[-1] = grad_keys[-1] + grad_key
            grad_values[-1] = grad_values[-1] + grad_value
    grad_query = jnp.concatenate(columns, axis=0).T * HD ** (-0.5)
    grad_query_ref[:, 0] = grad_query.reshape(2, -1, grad_query.shape[1])
    both = jnp.concatenate(grad_keys + grad_values, axis=1).astype(bf16)
    rows = both.shape[0] // depth
    for step, ref in enumerate(grad_refs):
        part = both[step * rows : (step + 1) * rows]
        ref[:, 0] = part.reshape(2, rows // 2, part.shape[1])


def sequence_spec(array):
    two, _, half, columns = array.shape
    return pl.BlockSpec((two, 1, half, columns), lambda j: (0, j, 0, 0))


def row_spec(array):
    return pl.BlockSpec((1,) + array.shape[1:], lambda j: (j, 0, 0))


def attend(query, keyvals, bias):
    two, reps, half, width = query.shape
    logs = jax.ShapeDtypeStruct((reps, width // HD, two * half), f32)
    cells = reps * width * two * half * bias.shape[1]
    return pl.pallas_call(
        functools.partial(attend_kernel, len(keyvals)),
        grid=(reps,),
        in_specs=[sequence_spec(query), row_spec(bias)] + [sequence_spec(v) for v in keyvals],
        out_specs=[sequence_spec(query), row_spec(logs)],
        out_shape=[jax.ShapeDtypeStruct(query.shape, bf16), logs],
        compiler_params=pltpu.CompilerParams(vmem_limit_bytes=48 << 20),
        cost_estimate=pl.CostEstimate(
            flops=16 * cells, bytes_accessed=8 << 20, transcendentals=cells // HD
        ),
        name="attend",
    )(query, bias, *keyvals)


def attend_back(query, keyvals, grad_mixed, log_total, bias):
    two, reps, half, width = query.shape
    cells = reps * width * two * half * bias.shape[1]
    outs = pl.pallas_call(
        functools.partial(attend_back_kernel, len(keyvals)),
        grid=(reps,),
        in_specs=[sequence_spec(query), sequence_spec(grad_mixed), row_spec(log_total)]
        + [row_spec(bias)]
        + [sequence_spec(v) for v in keyvals],
        out_specs=[sequence_spec(query)] + [sequence_spec(v) for v in keyvals],
        out_shape=[jax.ShapeDtypeStruct(query.shape, f32)]
        + [jax.ShapeDtypeStruct(v.shape, bf16) for v in keyvals],
        compiler_params=pltpu.CompilerParams(vmem_limit_bytes=48 << 20),
        cost_estimate=pl.CostEstimate(
            flops=40 * cells, bytes_accessed=12 << 20, transcendentals=cells // HD
        ),
        name="attend_back",
    )(query, grad_mixed, log_total, bias, *keyvals)
    return outs[0], outs[1:]


def turned_pair(value):
    lane = lax.broadcasted_iota(jnp.int32, value.shape, 1)
    half = HD // 2
    ahead = pltpu.roll(value, value.shape[1] - half, 1)
    behind = pltpu.roll(value, half, 1)
    return jnp.where(lane % HD < half, ahead, behind)


def widened(table, width):
    return jnp.concatenate([table] * (width // table.shape[1]), axis=1)


def rows_of(ref):
    return ref[0].reshape(-1, ref.shape[-1])


def project_kernel(k_width, a_ref, weight_ref, cosine_ref, sine_ref, query_ref, keyval_ref):
    mixed = dot(rows_of(a_ref), weight_ref[...], 1, 0)
    width = mixed.shape[1]
    cosine = widened(rows_of(cosine_ref), width)
    sine = widened(rows_of(sine_ref), width)
    rotated = mixed * cosine + turned_pair(mixed) * sine
    lane = lax.broadcasted_iota(jnp.int32, mixed.shape, 1)
    rotated = jnp.where(lane < width - k_width, rotated, mixed).astype(bf16)
    q_width = query_ref.shape[-1]
    query_ref[0] = rotated[:, :q_width].reshape(query_ref.shape[1:])
    keyval_ref[0] = rotated[:, q_width:].reshape(keyval_ref.shape[1:])


def project_back_kernel(k_width, grad_ref, weight_ref, cosine_ref, sine_ref, *refs):
    parts, (joined_ref, out_ref) = refs[:-2], refs[-2:]
    keyval = rows_of(parts[0]).astype(f32)
    for part in parts[1:]:
        keyval = keyval + rows_of(part).astype(f32)
    joined = jnp.concatenate([rows_of(grad_ref), keyval], axis=1)
    width = joined.shape[1]
    cosine = widened(rows_of(cosine_ref), width)
    sine = widened(rows_of(sine_ref), width)
    rotated = joined * cosine - turned_pair(joined) * sine
    lane = lax.broadcasted_iota(jnp.int32, joined.shape, 1)
    rotated = jnp.where(lane < width - k_width, rotated, joined).astype(bf16)
    joined_ref[0] = rotated.reshape(joined_ref.shape[1:])
    out = dot(rotated, weight_ref[...], 1, 1).astype(bf16)
    out_ref[0] = out.reshape(out_ref.shape[1:])


def half_spec(array):
    return pl.BlockSpec((1,) + array.shape[1:], lambda i: (i, 0, 0, 0))


def all_spec(array):
    return pl.BlockSpec(array.shape, lambda i: (0, 0))


def project(a_all, weight, cosine, sine, q_width, k_width):
    shape = a_all.shape[:3]
    outs = [
        jax.ShapeDtypeStruct(shape + (q_width,), bf16),
        jax.ShapeDtypeStruct(shape + (2 * k_width,), bf16),
    ]
    cells = a_all.size * weight.shape[1]
    return pl.pallas_call(
        functools.partial(project_kernel, k_width),
        grid=(2,),
        in_specs=[half_spec(a_all), all_spec(weight), half_spec(cosine), half_spec(sine)],
        out_specs=[half_spec(v) for v in outs],
        out_shape=outs,
        compiler_params=pltpu.CompilerParams(vmem_limit_bytes=40 << 20),
        cost_estimate=pl.CostEstimate(
            flops=2 * cells, bytes_accessed=10 << 20, transcendentals=0
        ),
        name="project",
    )(a_all, weight, cosine, sine)


def project_back(grad_query, parts, weight, cosine, sine, k_width):
    shape = grad_query.shape[:3]
    outs = [
        jax.ShapeDtypeStruct(shape + (weight.shape[1],), bf16),
        jax.ShapeDtypeStruct(shape + (weight.shape[0],), bf16),
    ]
    cells = outs[0].size * weight.shape[0]
    return pl.pallas_call(
        functools.partial(project_back_kernel, k_width),
        grid=(2,),
        in_specs=[half_spec(grad_query), all_spec(weight), half_spec(cosine), half_spec(sine)]
        + [half_spec(v) for v in parts],
        out_specs=[half_spec(v) for v in outs],
        out_shape=outs,
        compiler_params=pltpu.CompilerParams(vmem_limit_bytes=48 << 20),
        cost_estimate=pl.CostEstimate(
            flops=2 * cells, bytes_accessed=14 << 20, transcendentals=0
        ),
        name="project_back",
    )(grad_query, weight, cosine, sine, *parts)


def by_core(which, refs, write):
    for at, ref in enumerate(refs):
        pl.when(which == at)(functools.partial(write, ref))


def columns_kernel(info, zero, one_sent, zero_sent, one, out_ref):
    which = info[0] + 2 * pl.program_id(0)
    reps, _, piece = zero.shape[1:]

    def write(ref):
        for rep in range(reps):
            out_ref[:, rep * piece : (rep + 1) * piece] = ref[0, rep ^ info[1]].astype(f32)

    by_core(which, (zero, one_sent, zero_sent, one), write)


def rows_kernel(info, zero, one_sent, zero_sent, one, out_ref):
    which = info[0] + 2 * pl.program_id(0)

    def write(ref):
        for rep in range(out_ref.shape[0]):
            out_ref[rep, 0] = ref[0, rep ^ info[1]].astype(f32)

    by_core(which, (zero, one_sent, zero_sent, one), write)


def proj_kernel(info, zero, one_sent, zero_sent, one, query_ref, key_ref, value_ref):
    which = info[0] + 2 * pl.program_id(0)
    reps = zero.shape[1]

    def write(ref):
        for rep in range(reps):
            block = ref[0, rep ^ info[1]].astype(f32)
            start = 0
            for out_ref in (query_ref, key_ref, value_ref):
                size = out_ref.shape[1] // reps
                out_ref[:, rep * size : (rep + 1) * size] = block[:, start : start + size]
                start += size

    by_core(which, (zero, one_sent, zero_sent, one), write)


def assembled(kernel, grid, half_dim, block, index, out_blocks, out_index, out_shapes, info, four):
    def chosen(at):
        def where_from(*steps):
            taken = steps[-1][0] + 2 * steps[half_dim] == at
            return tuple(jnp.where(taken, v, 0) for v in index(at % 2, *steps))

        return where_from

    return pl.pallas_call(
        kernel,
        grid_spec=pltpu.PrefetchScalarGridSpec(
            num_scalar_prefetch=1,
            grid=grid,
            in_specs=[pl.BlockSpec(block, chosen(at)) for at in range(4)],
            out_specs=[pl.BlockSpec(b, out_index) for b in out_blocks],
        ),
        out_shape=[jax.ShapeDtypeStruct(v, f32) for v in out_shapes],
        compiler_params=pltpu.CompilerParams(vmem_limit_bytes=40 << 20),
        name=kernel.__name__,
    )(info, *four)


def assemble_columns(info, four, offsets, piece, pieces):
    _, reps, rows, _ = four[0].shape
    return assembled(
        columns_kernel,
        (2, 2, pieces),
        0,
        (1, reps, rows, piece),
        lambda layer, k, sub, at, info: (sub, 0, 0, offsets[layer] + at),
        [(rows, reps * piece)],
        lambda k, sub, at, info: (2 * k + sub, at),
        [(4 * rows, reps * piece * pieces)],
        info,
        four,
    )[0]


def assemble_rows(info, four):
    _, reps, rows, columns = four[0].shape
    return assembled(
        rows_kernel,
        (2, 2),
        0,
        (1, reps, rows, columns),
        lambda layer, k, sub, info: (sub, 0, 0, 0),
        [(reps, 1, rows, columns)],
        lambda k, sub, info: (0, 2 * k + sub, 0, 0),
        [(reps, 4, rows, columns)],
        info,
        four,
    )[0].reshape(-1, columns)


def assemble_proj(info, four, sizes):
    _, reps, rows, columns = four[0].shape
    return assembled(
        proj_kernel,
        (2, 2),
        0,
        (1, reps, rows, columns),
        lambda layer, k, sub, info: (sub, 0, 0, 0),
        [(rows, reps * size) for size in sizes],
        lambda k, sub, info: (2 * k + sub, 0),
        [(4 * rows, reps * size) for size in sizes],
        info,
        four,
    )


def together(*values):
    return lax.optimization_barrier(values)


def shards(
    tokens,
    segment_ids,
    cotangent,
    norm_attn,
    w_query,
    w_key,
    w_value,
    w_output,
    norm_ffn,
    w_gate,
    w_up,
    w_down,
):
    core = lax.axis_index("section")
    layer_z = lax.axis_index("fsdp")
    rep = lax.axis_index("rep")
    depth = lax.axis_size("fsdp")
    reps = lax.axis_size("rep")
    rows, width = tokens.shape[2:]
    half = rows // 2
    count = reps * rows
    q_width = HQ * HD // reps
    k_width = KVH * HD // reps
    ff_width = FF // reps
    ff_piece = FF // (reps * depth)

    def back(value, step):
        return lax.ppermute(value, "fsdp", [(i, i + step) for i in range(depth - step)])

    def by_layer(own, got):
        return (jnp.where(core == 0, own, got), jnp.where(core == 0, got, own))

    own_gain = jnp.concatenate([norm_attn, norm_ffn], axis=0)
    turned = jnp.stack(
        [own_gain]
        + [
            lax.ppermute(own_gain, "fsdp", [(i, (i + s) % depth) for i in range(depth)])
            for s in range(1, depth)
        ]
    )
    own_gain = jnp.concatenate(
        [
            lax.dynamic_index_in_dim(turned, (layer_z - k + depth) % depth, 0, keepdims=False)
            for k in range(depth)
        ],
        axis=1,
    ).astype(f32)
    gains = by_layer(own_gain, lax.ppermute(own_gain, "section", SWAP))

    plane_ids = lax.dynamic_index_in_dim(segment_ids[0], core, 0, keepdims=True)
    for bit in bit_list(reps):
        plane_ids = jnp.concatenate([plane_ids, partner(plane_ids, bit)], axis=0)
    ids = [plane_ids] + [back(plane_ids, step) for step in range(1, depth)]

    def split(cut, total):
        size = total // 2
        got = lax.ppermute(cut((1 - core) * size, size), "section", SWAP)
        return by_layer(cut(core * size, size), got)

    def spread(pieces):
        return [lax.all_gather(v, ("fsdp", "section"), axis=0, tiled=True) for v in pieces]

    def qkv_cut(row, size):
        parts = ((w_query, q_width), (w_key, k_width), (w_value, k_width))
        return jnp.concatenate(
            [lax.dynamic_slice(w[0], (row, rep * n), (size, n)) for w, n in parts], axis=1
        )

    def ffn_cut(row, size):
        return jnp.concatenate(
            [
                lax.dynamic_slice(
                    w[0], (row, k * reps * ff_piece + rep * ff_piece), (size, ff_piece)
                )
                for w in (w_gate, w_up)
                for k in range(depth)
            ],
            axis=1,
        )

    out_rows = w_output.shape[1] // reps

    def attn_cut(row, size):
        height = out_rows * size // w_query.shape[1]
        first = rep * out_rows + row * out_rows // w_query.shape[1]
        out = lax.dynamic_slice_in_dim(w_output[0], first, height)
        return jnp.concatenate([qkv_cut(row, size), out.reshape(size, -1)], axis=1)

    def all_ffn_cut(row, size):
        height = ff_piece * size // w_gate.shape[1]
        first = rep * ff_piece + row * ff_piece // w_gate.shape[1]
        down = lax.dynamic_slice_in_dim(w_down[0], first, height)
        return jnp.concatenate([ffn_cut(row, size), down.reshape(size, -1)], axis=1)

    attn_all = spread(split(attn_cut, w_query.shape[1]))
    qkv_width = q_width + 2 * k_width
    qkv_all = [v[:, :qkv_width] for v in attn_all]
    out_all = [
        lax.all_to_all(v[:, qkv_width:].reshape(-1, width), "rep", 0, 0, tiled=True)
        for v in attn_all
    ]
    both_all = spread(split(all_ffn_cut, w_gate.shape[1]))
    ffn_all = [v[:, : 2 * ff_width] for v in both_all]
    down_all = [v[:, 2 * ff_width :].reshape(ff_width, width) for v in both_all]

    starts = jnp.zeros((reps, rows), jnp.int32)
    biases = []
    within = jnp.arange(rows)
    for step in range(depth):
        key_ids, here = ids[step][:, :, None], plane_ids[:, None, :]
        exists = layer_z >= step
        starts = starts + jnp.sum((exists & (key_ids < here)).astype(jnp.int32), axis=1)
        allowed = exists & (key_ids == here)
        if step == 0:
            allowed = allowed & (within[:, None] <= within[None, :])
        biases.append(jnp.where(allowed, 0.0, masked_score).astype(bf16))
    bias = jnp.concatenate(biases, axis=1)
    cosine, sine = rope_tables((layer_z * rows + within - starts).astype(f32))

    def by_half(table):
        return table.reshape(reps, 2, half, 2 * HD).transpose(1, 0, 2, 3)

    cosine, sine = by_half(cosine), by_half(sine)

    def flat(value):
        return value.reshape(count, -1)

    def blocks(value):
        return value.reshape(2, reps, half, -1)

    def forward(layer, layer_in):
        gain_attn, gain_ffn = gains[layer][0], gains[layer][1]
        scale_in = scale_of(layer_in)
        a_all = plane_gather((layer_in * scale_in * gain_attn).astype(bf16))
        query, keyval = project(a_all, qkv_all[layer], cosine, sine, q_width, k_width)
        keyvals = [keyval] + [
            back(keyval, step) for step in range(1, depth)
        ]
        mixed, log_total = attend(query, keyvals, bias)
        residual = layer_in + plane_reduce(blocks(times(flat(mixed), out_all[layer]).astype(bf16)))
        scale_mid = scale_of(residual)
        b_all = plane_gather((residual * scale_mid * gain_ffn).astype(bf16))
        pre = times(flat(b_all), ffn_all[layer])
        gate, up = pre[:, :ff_width], pre[:, ff_width:]
        hidden = (jax.nn.silu(gate) * up).astype(bf16)
        out = residual + plane_reduce(blocks(times(hidden, down_all[layer]).astype(bf16)))
        kept = (layer_in, scale_in, a_all, query, keyvals, mixed, log_total)
        return out.astype(bf16), kept + (residual, scale_mid, b_all, gate, up, hidden)

    def core_product(left, right, extra=None):
        size = left.shape[1] // (2 * depth)

        def half_of(value, which):
            return jnp.concatenate(
                [
                    lax.dynamic_slice_in_dim(value, (2 * k + which) * size, size, axis=1)
                    for k in range(depth)
                ],
                axis=1,
            )

        def product(which, right):
            found = dot(half_of(left, which), right, 0, 0)
            if extra is None:
                return found
            more = half_of(extra, which).T
            more = jnp.pad(more, ((0, 0), (0, 128 - more.shape[1])))
            return jnp.concatenate([found, more], axis=1)

        def finish(right, sent):
            got = lax.ppermute(sent, "section", SWAP)
            return (product(core, right) + got.astype(f32)).astype(bf16)

        return product(1 - core, right).astype(bf16), finish

    info = jnp.stack([core, rep]).astype(jnp.int32)

    def collect(total):
        return lax.psum_scatter(total, "fsdp", scatter_dimension=0, tiled=True)

    def backward(layer, grad_out, kept, earlier, ready):
        (layer_in, scale_in, a_all, query, keyvals, mixed, log_total) = kept[:7]
        (residual, scale_mid, b_all, gate, up, hidden) = kept[7:]
        gain_attn, gain_ffn = gains[layer][0], gains[layer][1]
        last = earlier is not None
        if last:
            old_rest, old_gate, old_up, old_down = earlier
            tall = old_up.shape[0]

            def in_one(*values):
                return jnp.concatenate([v.reshape(tall, -1) for v in values], axis=1)

            state = gather_step(gather_start(grad_out), 0)
            *state, old_gate, old_up, old_down = together(*state, old_gate, old_up, old_down)
            old_ffn = in_one(old_gate, old_up, old_down)
            gm_all = flat(gather_rest(state, 1))
            sent_down, finish = core_product(hidden, gm_all)
            gm_all, sent_down, old_ffn = together(gm_all, sent_down, old_ffn)
            ffn_state = gather_step(gather_start(old_ffn), 0)
        else:
            gm_all = flat(plane_gather(grad_out))
            sent_down, finish = core_product(hidden, gm_all)
            gm_all, sent_down, *ready = together(gm_all, sent_down, *ready)
        grad_hidden = times_back(gm_all, down_all[layer])
        sig = jax.nn.sigmoid(gate)
        grad_gate = (grad_hidden * up * (sig * (1.0 + gate * (1.0 - sig)))).astype(bf16)
        grad_up = (grad_hidden * (gate * sig)).astype(bf16)
        grad_pre = jnp.concatenate([grad_gate, grad_up], axis=1)
        part_down = finish(gm_all, sent_down)
        if last:
            grad_pre, *ffn_state = together(grad_pre, *ffn_state)
        own_down = collect(part_down)
        db = blocks(times_back(grad_pre, ffn_all[layer]).astype(bf16))
        db, grad_gate, grad_up = together(db, grad_gate, grad_up)
        db = plane_reduce(db)
        sent_gate, finish_gate = core_product(flat(b_all), grad_gate)
        sent_up, finish_up = core_product(flat(b_all), grad_up)
        unit = residual * scale_mid
        grad_mid, gain_grad_ffn = norm_back(db, gain_ffn, unit, scale_mid)
        grad_mid = grad_mid + grad_out.astype(f32)
        go = grad_mid.astype(bf16)
        go_all = flat(plane_gather(go))
        go_all, part_gate, part_up = together(
            go_all, finish_gate(grad_gate, sent_gate), finish_up(grad_up, sent_up)
        )
        own_gate, own_up = collect(part_gate), collect(part_up)
        grad_mixed = blocks(times_back(go_all, out_all[layer]).astype(bf16))
        if last:
            grad_mixed, own_down, old_rest, *ffn_state = together(
                grad_mixed, own_down, old_rest, *ffn_state
            )
            ffn_state = gather_step(ffn_state, 1)
            rest_state = gather_step(gather_start(old_rest), 0)
        else:
            grad_mixed, own_down = together(grad_mixed, own_down)
        grad_query, grad_kv = attend_back(query, keyvals, grad_mixed, log_total, bias)
        grad_query, go_all, *grad_kv = together(grad_query, go_all, *grad_kv)
        grad_kv = [grad_kv[0]] + [
            lax.ppermute(grad_kv[step], "fsdp", [(i, i - step) for i in range(step, depth)])
            for step in range(1, depth)
        ]
        sent_o, finish = core_product(flat(mixed), go_all)
        part_o = lax.all_to_all(finish(go_all, sent_o), "rep", 0, 0, tiled=True)
        grad_qkv, da = project_back(grad_query, grad_kv, qkv_all[layer], cosine, sine, k_width)
        grad_qkv = flat(grad_qkv)

        def input_side(da):
            unit = layer_in * scale_in
            grad_in, gain_grad_attn = norm_back(da, gain_attn, unit, scale_in)
            grad_in = (grad_in + grad_mid).astype(bf16)
            gain_grads = jnp.stack([gain_grad_attn, gain_grad_ffn])
            sent_proj, finish = core_product(flat(a_all), grad_qkv, gain_grads)
            part_proj = finish(grad_qkv, sent_proj)
            aside = part_o.reshape(part_proj.shape[0], -1)
            return grad_in, jnp.concatenate([part_proj, aside], axis=1)

        if not last:
            da, grad_qkv, part_o, own_gate = together(da, grad_qkv, part_o, own_gate)
            grad_in, part_rest = input_side(plane_reduce(da))
            return grad_in, (collect(part_rest), own_gate, own_up, own_down), ready

        def four(zero, ones):
            return (zero, ones[1], lax.ppermute(zero, "section", [(1, 0)]), ones[0])

        def cut_out(pair, first, like):
            size = like.size // (tall * reps)
            part = [v[..., first : first + size].reshape(like.shape) for v in pair]
            return part, first + size

        da, *states = together(da, *ffn_state, *rest_state)
        old_ffn = gather_rest(states[:2], 2)
        old_rest = gather_rest(states[2:], 1)
        da, own_gate, own_down = together(plane_reduce(da), own_gate, own_down)
        grad_in, part_rest = input_side(da)
        gate_state = gather_step(gather_start(own_gate), 0)
        down_state = gather_step(gather_start(own_down), 0)
        part_rest, own_up, *states = together(part_rest, own_up, *gate_state, *down_state)
        own_rest = collect(part_rest)
        zero_gate, zero_down = gather_rest(states[:2], 1), gather_rest(states[2:], 1)
        up_state = gather_step(gather_start(own_up), 0)
        zero_gate, zero_down, old_ffn, own_rest, *up_state = together(
            zero_gate, zero_down, old_ffn, own_rest, *up_state
        )
        zero_up = gather_rest(up_state, 1)
        zero_rest = plane_gather(own_rest)
        old_ffn = (old_ffn, lax.ppermute(old_ffn, "section", [(0, 1)]))
        old_rest = (old_rest, lax.ppermute(old_rest, "section", [(0, 1)]))
        grad_gate = assemble_columns(info, four(zero_gate, old_ffn), (0, 0), ff_piece, depth)
        old_down, _ = cut_out(old_ffn, 2 * own_up.shape[1], zero_down)
        grad_down = assemble_rows(info, four(zero_down, old_down))
        grad_gate, grad_down, zero_up, zero_rest, *old_rest = together(
            grad_gate, grad_down, zero_up, zero_rest, *old_rest
        )
        grad_up = assemble_columns(info, four(zero_up, old_ffn), (0, depth), ff_piece, depth)
        rest = four(zero_rest, old_rest)
        proj_width = own_rest.shape[1] - out_rows * width // (2 * tall)
        proj = [v[..., :proj_width] for v in rest]
        outs = [v[..., proj_width:].reshape(2, reps, -1, width) for v in rest]
        grad_output = assemble_rows(info, outs)
        projections = assemble_proj(info, proj, (q_width, k_width, k_width))
        return grad_in, proj, (*projections, grad_output, grad_gate, grad_up, grad_down)

    own_tokens = lax.dynamic_index_in_dim(tokens[0], core, 0, keepdims=False)
    own_cotangent = lax.dynamic_index_in_dim(cotangent[0], core, 0, keepdims=False)
    out0, kept0 = forward(0, own_tokens.astype(f32))
    out1, kept1 = forward(1, out0.astype(f32))

    def swapped(zero, one):
        got = lax.ppermute(jnp.where(core == 0, one, zero), "section", SWAP)
        return jnp.where(core == 0, zero, got), jnp.where(core == 0, got, one)

    grad1, sums1, outputs = backward(1, own_cotangent, kept1, None, swapped(out0, out1))
    grad0, proj, weight_grads = backward(0, grad1, kept0, sums1, None)
    outputs = jnp.stack(outputs)[None, None]
    input_grads = jnp.stack(swapped(grad0, grad1))[None, None]
    grad_query, grad_key, grad_value, grad_output, grad_gate, grad_up, grad_down = weight_grads
    gain_parts = [jnp.sum(v[..., qkv_width : qkv_width + 2].astype(f32), axis=1) for v in proj]
    gain_halves = (
        jnp.where(core == 0, gain_parts[0], gain_parts[1]),
        jnp.where(core == 0, gain_parts[2], gain_parts[3]),
    )
    gain_sums = jnp.concatenate(gain_halves, axis=0).reshape(-1, 2)
    return (
        outputs,
        input_grads,
        gain_sums[:, 0][None],
        grad_query[None],
        grad_key[None],
        grad_value[None],
        grad_output[None],
        gain_sums[:, 1][None],
        grad_gate[None],
        grad_up[None],
        grad_down[None],
    )


def solution(mesh):
    in_specs = (
        P("rep", None, "fsdp", None),
        P("rep", None, "fsdp"),
        P("rep", None, "fsdp", None),
        P("section", "fsdp"),
        P("section", "fsdp", None),
        P("section", "fsdp", None),
        P("section", "fsdp", None),
        P("section", "fsdp", None),
        P("section", "fsdp"),
        P("section", "fsdp", None),
        P("section", "fsdp", None),
        P("section", "fsdp", None),
    )
    out_specs = (
        P("section", "rep", None, "fsdp", None),
        P("section", "rep", None, "fsdp", None),
        P("section", "fsdp"),
        P("section", "fsdp", None),
        P("section", "fsdp", None),
        P("section", "fsdp", None),
        P("section", "fsdp", None),
        P("section", "fsdp"),
        P("section", "fsdp", None),
        P("section", "fsdp", None),
        P("section", "fsdp", None),
    )
    return jax.shard_map(shards, mesh=mesh, in_specs=in_specs, out_specs=out_specs, check_vma=False)
```

```python
import functools

import jax
import jax.numpy as jnp
from jax import lax
from jax.experimental import pallas as pl
from jax.experimental.pallas import tpu as pltpu
from jax.sharding import PartitionSpec as P

HQ = 32
KVH = 8
HD = 64
FF = 8192

epsilon = 1e-05
rope_base = 500000.0
masked_score = -1e30
bf16 = jnp.bfloat16
f32 = jnp.float32
SWAP = [(0, 1), (1, 0)]


def partner(value, bit):
    count = lax.axis_size("rep")
    return lax.ppermute(value, "rep", [(i, i ^ bit) for i in range(count)])


def bit_list(count):
    found = []
    bit = 1
    while bit < count:
        found.append(bit)
        bit *= 2
    return found


def gather_start(own):
    half = own.shape[0] // 2
    return own[None, :half], own[None, half:]


def gather_step(state, at):
    bits = bit_list(lax.axis_size("rep"))
    first, second = state
    first = jnp.concatenate([first, partner(first, bits[at])], axis=0)
    other = partner(second, bits[-1 - at])
    second = jnp.stack([second, other], axis=1).reshape((-1,) + second.shape[1:])
    return first, second


def gather_pair(state, at):
    for step in range(at, len(bit_list(lax.axis_size("rep")))):
        state = gather_step(state, step)
    return list(state)


def gather_rest(state, at):
    return jnp.stack(gather_pair(state, at))


def plane_gather(own):
    return gather_rest(gather_start(own), 0)


def plane_reduce(parts):
    bits = bit_list(lax.axis_size("rep"))
    first, second = parts[0], parts[1]
    for bit in bits[::-1]:
        keep, away = first[:bit], first[bit:]
        first = keep.astype(f32) + partner(away.astype(bf16), bit).astype(f32)
    for bit in bits:
        pair = second.reshape((-1, 2) + second.shape[1:])
        keep, away = pair[:, 0], pair[:, 1]
        second = keep.astype(f32) + partner(away.astype(bf16), bit).astype(f32)
    return jnp.concatenate([first[0], second[0]], axis=0)


def rope_tables(positions):
    half_size = HD // 2
    frequency = rope_base ** (-(jnp.arange(half_size).astype(f32) * 2.0) / HD)
    angles = positions[..., None] * frequency
    cosine, sine = jnp.cos(angles), jnp.sin(angles)
    return (
        jnp.concatenate([cosine] * 4, axis=-1),
        jnp.concatenate([-sine, sine] * 2, axis=-1),
    )


def times(left, weight):
    return jnp.dot(left, weight, preferred_element_type=f32)


def times_back(left, weight):
    return lax.dot_general(
        left, weight, (((1,), (1,)), ((), ())), preferred_element_type=f32
    )


def scale_of(values):
    return lax.rsqrt(jnp.mean(values * values, axis=-1, keepdims=True) + epsilon)


def norm_back(grad, gain, unit, scale):
    scaled = gain * grad
    out = scale * (scaled - unit * jnp.mean(scaled * unit, axis=-1, keepdims=True))
    return (out, jnp.sum(grad * unit, axis=0))


def sequence(ref):
    return ref[:, 0].reshape(-1, ref.shape[-1])


def scaled(value):
    return (value.astype(f32) * HD ** (-0.5)).astype(bf16)


def dot(left, right, left_dim, right_dim):
    return lax.dot_general(
        left, right, (((left_dim,), (right_dim,)), ((), ())), preferred_element_type=f32
    )


def attend_kernel(depth, query_ref, bias_ref, *refs):
    mixed_ref, log_ref = refs[depth:]
    keyval = jnp.concatenate([sequence(ref) for ref in refs[:depth]], axis=0)
    query = scaled(sequence(query_ref))
    bias = bias_ref[0].astype(f32)
    k_width = keyval.shape[1] // 2
    heads = query.shape[1] // HD
    group = heads // (k_width // HD)
    columns = []
    for head in range(heads):
        at = head // group * HD
        key = keyval[:, at : at + HD]
        value = keyval[:, k_width + at : k_width + at + HD]
        scores = dot(key, query[:, head * HD : (head + 1) * HD], 1, 1) + bias
        row_max = jnp.max(scores, axis=0, keepdims=True)
        weights = jnp.exp(scores - row_max)
        total = jnp.sum(weights, axis=0, keepdims=True)
        probs = (weights * (1.0 / total)).astype(bf16)
        columns.append(dot(value, probs, 0, 0))
        log_ref[0, head : head + 1, :] = row_max + jnp.log(total)
    mixed = jnp.concatenate(columns, axis=0).T.astype(bf16)
    mixed_ref[:, 0] = mixed.reshape(2, -1, mixed.shape[1])


def attend_back_kernel(depth, query_ref, grad_ref, log_ref, bias_ref, *refs):
    grad_query_ref, grad_refs = refs[depth], refs[depth + 1 :]
    keyval = jnp.concatenate([sequence(ref) for ref in refs[:depth]], axis=0)
    query = scaled(sequence(query_ref))
    grad = sequence(grad_ref)
    bias = bias_ref[0].astype(f32)
    k_width = keyval.shape[1] // 2
    heads = query.shape[1] // HD
    group = heads // (k_width // HD)
    columns, grad_keys, grad_values = [], [], []
    for head in range(heads):
        at = head // group * HD
        key = keyval[:, at : at + HD]
        value = keyval[:, k_width + at : k_width + at + HD]
        own_query = query[:, head * HD : (head + 1) * HD]
        own_grad = grad[:, head * HD : (head + 1) * HD]
        scores = dot(key, own_query, 1, 1) + bias
        probs = jnp.exp(scores - log_ref[0, head : head + 1, :])
        grad_probs = dot(value, own_grad, 1, 1)
        inner = jnp.sum(probs * grad_probs, axis=0, keepdims=True)
        grad_scores = (probs * (grad_probs - inner)).astype(bf16)
        columns.append(dot(key, grad_scores, 0, 0))
        grad_key = dot(grad_scores, own_query, 1, 0)
        grad_value = dot(probs.astype(bf16), own_grad, 1, 0)
        if head % group == 0:
            grad_keys.append(grad_key)
            grad_values.append(grad_value)
        else:
            grad_keys[-1] = grad_keys[-1] + grad_key
            grad_values[-1] = grad_values[-1] + grad_value
    grad_query = jnp.concatenate(columns, axis=0).T * HD ** (-0.5)
    grad_query_ref[:, 0] = grad_query.reshape(2, -1, grad_query.shape[1])
    both = jnp.concatenate(grad_keys + grad_values, axis=1).astype(bf16)
    rows = both.shape[0] // depth
    for step, ref in enumerate(grad_refs):
        part = both[step * rows : (step + 1) * rows]
        ref[:, 0] = part.reshape(2, rows // 2, part.shape[1])


def sequence_spec(array):
    two, _, half, columns = array.shape
    return pl.BlockSpec((two, 1, half, columns), lambda j: (0, j, 0, 0))


def row_spec(array):
    return pl.BlockSpec((1,) + array.shape[1:], lambda j: (j, 0, 0))


def attend(query, keyvals, bias):
    two, reps, half, width = query.shape
    logs = jax.ShapeDtypeStruct((reps, width // HD, two * half), f32)
    cells = reps * width * two * half * bias.shape[1]
    return pl.pallas_call(
        functools.partial(attend_kernel, len(keyvals)),
        grid=(reps,),
        in_specs=[sequence_spec(query), row_spec(bias)] + [sequence_spec(v) for v in keyvals],
        out_specs=[sequence_spec(query), row_spec(logs)],
        out_shape=[jax.ShapeDtypeStruct(query.shape, bf16), logs],
        compiler_params=pltpu.CompilerParams(vmem_limit_bytes=48 << 20),
        cost_estimate=pl.CostEstimate(
            flops=16 * cells, bytes_accessed=8 << 20, transcendentals=cells // HD
        ),
        name="attend",
    )(query, bias, *keyvals)


def attend_back(query, keyvals, grad_mixed, log_total, bias):
    two, reps, half, width = query.shape
    cells = reps * width * two * half * bias.shape[1]
    outs = pl.pallas_call(
        functools.partial(attend_back_kernel, len(keyvals)),
        grid=(reps,),
        in_specs=[sequence_spec(query), sequence_spec(grad_mixed), row_spec(log_total)]
        + [row_spec(bias)]
        + [sequence_spec(v) for v in keyvals],
        out_specs=[sequence_spec(query)] + [sequence_spec(v) for v in keyvals],
        out_shape=[jax.ShapeDtypeStruct(query.shape, f32)]
        + [jax.ShapeDtypeStruct(v.shape, bf16) for v in keyvals],
        compiler_params=pltpu.CompilerParams(vmem_limit_bytes=48 << 20),
        cost_estimate=pl.CostEstimate(
            flops=40 * cells, bytes_accessed=12 << 20, transcendentals=cells // HD
        ),
        name="attend_back",
    )(query, grad_mixed, log_total, bias, *keyvals)
    return outs[0], outs[1:]


def turned_pair(value):
    lane = lax.broadcasted_iota(jnp.int32, value.shape, 1)
    half = HD // 2
    ahead = pltpu.roll(value, value.shape[1] - half, 1)
    behind = pltpu.roll(value, half, 1)
    return jnp.where(lane % HD < half, ahead, behind)


def widened(table, width):
    return jnp.concatenate([table] * (width // table.shape[1]), axis=1)


def rows_of(ref):
    return ref[0].reshape(-1, ref.shape[-1])


def project_kernel(k_width, a_ref, weight_ref, cosine_ref, sine_ref, query_ref, keyval_ref):
    mixed = dot(rows_of(a_ref), weight_ref[...], 1, 0)
    width = mixed.shape[1]
    cosine = widened(rows_of(cosine_ref), width)
    sine = widened(rows_of(sine_ref), width)
    rotated = mixed * cosine + turned_pair(mixed) * sine
    lane = lax.broadcasted_iota(jnp.int32, mixed.shape, 1)
    rotated = jnp.where(lane < width - k_width, rotated, mixed).astype(bf16)
    q_width = query_ref.shape[-1]
    query_ref[0] = rotated[:, :q_width].reshape(query_ref.shape[1:])
    keyval_ref[0] = rotated[:, q_width:].reshape(keyval_ref.shape[1:])


def project_back_kernel(k_width, grad_ref, weight_ref, cosine_ref, sine_ref, *refs):
    parts, (joined_ref, out_ref) = refs[:-2], refs[-2:]
    keyval = rows_of(parts[0]).astype(f32)
    for part in parts[1:]:
        keyval = keyval + rows_of(part).astype(f32)
    joined = jnp.concatenate([rows_of(grad_ref), keyval], axis=1)
    width = joined.shape[1]
    cosine = widened(rows_of(cosine_ref), width)
    sine = widened(rows_of(sine_ref), width)
    rotated = joined * cosine - turned_pair(joined) * sine
    lane = lax.broadcasted_iota(jnp.int32, joined.shape, 1)
    rotated = jnp.where(lane < width - k_width, rotated, joined).astype(bf16)
    joined_ref[0] = rotated.reshape(joined_ref.shape[1:])
    out = dot(rotated, weight_ref[...], 1, 1).astype(bf16)
    out_ref[0] = out.reshape(out_ref.shape[1:])


def half_spec(array):
    return pl.BlockSpec((1,) + array.shape[1:], lambda i: (i, 0, 0, 0))


def all_spec(array):
    return pl.BlockSpec(array.shape, lambda i: (0, 0))


def project(a_all, weight, cosine, sine, q_width, k_width):
    shape = a_all.shape[:3]
    outs = [
        jax.ShapeDtypeStruct(shape + (q_width,), bf16),
        jax.ShapeDtypeStruct(shape + (2 * k_width,), bf16),
    ]
    cells = a_all.size * weight.shape[1]
    return pl.pallas_call(
        functools.partial(project_kernel, k_width),
        grid=(2,),
        in_specs=[half_spec(a_all), all_spec(weight), half_spec(cosine), half_spec(sine)],
        out_specs=[half_spec(v) for v in outs],
        out_shape=outs,
        compiler_params=pltpu.CompilerParams(vmem_limit_bytes=40 << 20),
        cost_estimate=pl.CostEstimate(
            flops=2 * cells, bytes_accessed=10 << 20, transcendentals=0
        ),
        name="project",
    )(a_all, weight, cosine, sine)


def project_back(grad_query, parts, weight, cosine, sine, k_width):
    shape = grad_query.shape[:3]
    outs = [
        jax.ShapeDtypeStruct(shape + (weight.shape[1],), bf16),
        jax.ShapeDtypeStruct(shape + (weight.shape[0],), bf16),
    ]
    cells = outs[0].size * weight.shape[0]
    return pl.pallas_call(
        functools.partial(project_back_kernel, k_width),
        grid=(2,),
        in_specs=[half_spec(grad_query), all_spec(weight), half_spec(cosine), half_spec(sine)]
        + [half_spec(v) for v in parts],
        out_specs=[half_spec(v) for v in outs],
        out_shape=outs,
        compiler_params=pltpu.CompilerParams(vmem_limit_bytes=48 << 20),
        cost_estimate=pl.CostEstimate(
            flops=2 * cells, bytes_accessed=14 << 20, transcendentals=0
        ),
        name="project_back",
    )(grad_query, weight, cosine, sine, *parts)


def by_place(info, refs, write):
    which = info[0] + 2 * pl.program_id(0) + 4 * pl.program_id(1)
    for at, ref in enumerate(refs):
        pl.when(which == at)(functools.partial(write, ref))


def columns_kernel(piece, info, *refs):
    out_ref = refs[8]
    reps, _, taken = refs[0].shape

    def write(ref):
        for at in range(taken // piece):
            for rep in range(reps):
                start = (at * reps + rep) * piece
                found = ref[rep ^ info[1], :, at * piece : (at + 1) * piece]
                out_ref[:, start : start + piece] = found.astype(f32)

    by_place(info, refs[:8], write)


def rows_kernel(info, *refs):
    out_ref = refs[8]

    def write(ref):
        for rep in range(out_ref.shape[0]):
            out_ref[rep, 0] = ref[rep ^ info[1]].astype(f32)

    by_place(info, refs[:8], write)


def rest_kernel(proj_width, info, *refs):
    outs, output_ref = refs[8:11], refs[11]
    reps, rows, width = refs[0].shape
    height, piece = output_ref.shape[2], width - proj_width

    def write(ref):
        for rep in range(reps):
            block = ref[rep ^ info[1]].astype(f32)
            start = 0
            for out_ref in outs:
                size = out_ref.shape[1] // reps
                out_ref[:, rep * size : (rep + 1) * size] = block[:, start : start + size]
                start += size
            for at in range(rows // height):
                part = block[at * height : (at + 1) * height, proj_width:]
                output_ref[rep, 0, :, at * piece : (at + 1) * piece] = part

    by_place(info, refs[:8], write)


def assembled(kernel, grid, block, index, out_blocks, out_index, out_shapes, info, eight):
    def chosen(at):
        def where_from(*steps):
            taken = steps[-1][0] + 2 * steps[0] + 4 * steps[1] == at
            return tuple(jnp.where(taken, v, 0) for v in index(at % 2, *steps))

        return where_from

    return pl.pallas_call(
        kernel,
        grid_spec=pltpu.PrefetchScalarGridSpec(
            num_scalar_prefetch=1,
            grid=grid,
            in_specs=[pl.BlockSpec(block, chosen(at)) for at in range(8)],
            out_specs=[pl.BlockSpec(b, f) for b, f in zip(out_blocks, out_index)],
        ),
        out_shape=[jax.ShapeDtypeStruct(v, f32) for v in out_shapes],
        compiler_params=pltpu.CompilerParams(vmem_limit_bytes=56 << 20),
        name="assemble",
    )(info, *eight)


def assemble_columns(info, eight, offsets, piece, pieces):
    reps, rows, _ = eight[0].shape
    step = 2 if pieces % 2 == 0 else 1
    return assembled(
        functools.partial(columns_kernel, piece),
        (2, 2, pieces // step),
        (reps, rows, step * piece),
        lambda layer, k, sub, at, info: (0, 0, offsets[layer] // step + at),
        [(rows, step * reps * piece)],
        [lambda k, sub, at, info: (2 * k + sub, at)],
        [(4 * rows, reps * piece * pieces)],
        info,
        eight,
    )[0]


def assemble_rows(info, eight):
    reps, rows, columns = eight[0].shape
    return assembled(
        rows_kernel,
        (2, 2),
        (reps, rows, columns),
        lambda layer, k, sub, info: (0, 0, 0),
        [(reps, 1, rows, columns)],
        [lambda k, sub, info: (0, 2 * k + sub, 0, 0)],
        [(reps, 4, rows, columns)],
        info,
        eight,
    )[0].reshape(-1, columns)


def assemble_rest(info, eight, sizes, proj_width, height, width):
    reps, rows, columns = eight[0].shape
    outs = assembled(
        functools.partial(rest_kernel, proj_width),
        (2, 2),
        (reps, rows, columns),
        lambda layer, k, sub, info: (0, 0, 0),
        [(rows, reps * size) for size in sizes] + [(reps, 1, height, width // 2)],
        [lambda k, sub, info: (2 * k + sub, 0)] * len(sizes)
        + [lambda k, sub, info: (0, k, 0, sub)],
        [(4 * rows, reps * size) for size in sizes] + [(reps, 2, height, width)],
        info,
        eight,
    )
    return (*outs[:-1], outs[-1].reshape(-1, width))


def together(*values):
    return lax.optimization_barrier(values)


def shards(
    tokens,
    segment_ids,
    cotangent,
    norm_attn,
    w_query,
    w_key,
    w_value,
    w_output,
    norm_ffn,
    w_gate,
    w_up,
    w_down,
):
    core = lax.axis_index("section")
    layer_z = lax.axis_index("fsdp")
    rep = lax.axis_index("rep")
    depth = lax.axis_size("fsdp")
    reps = lax.axis_size("rep")
    rows, width = tokens.shape[2:]
    half = rows // 2
    count = reps * rows
    q_width = HQ * HD // reps
    k_width = KVH * HD // reps
    ff_width = FF // reps
    ff_piece = FF // (reps * depth)

    def back(value, step):
        return lax.ppermute(value, "fsdp", [(i, i + step) for i in range(depth - step)])

    def by_layer(own, got):
        return (jnp.where(core == 0, own, got), jnp.where(core == 0, got, own))

    own_gain = jnp.concatenate([norm_attn, norm_ffn], axis=0)
    turned = jnp.stack(
        [own_gain]
        + [
            lax.ppermute(own_gain, "fsdp", [(i, (i + s) % depth) for i in range(depth)])
            for s in range(1, depth)
        ]
    )
    own_gain = jnp.concatenate(
        [
            lax.dynamic_index_in_dim(turned, (layer_z - k + depth) % depth, 0, keepdims=False)
            for k in range(depth)
        ],
        axis=1,
    ).astype(f32)
    gains = by_layer(own_gain, lax.ppermute(own_gain, "section", SWAP))

    plane_ids = lax.dynamic_index_in_dim(segment_ids[0], core, 0, keepdims=True)
    for bit in bit_list(reps):
        plane_ids = jnp.concatenate([plane_ids, partner(plane_ids, bit)], axis=0)
    ids = [plane_ids] + [back(plane_ids, step) for step in range(1, depth)]

    def split(cut, total):
        size = total // 2
        got = lax.ppermute(cut((1 - core) * size, size), "section", SWAP)
        return by_layer(cut(core * size, size), got)

    def spread(pieces):
        return [lax.all_gather(v, ("fsdp", "section"), axis=0, tiled=True) for v in pieces]

    def qkv_cut(row, size):
        parts = ((w_query, q_width), (w_key, k_width), (w_value, k_width))
        return jnp.concatenate(
            [lax.dynamic_slice(w[0], (row, rep * n), (size, n)) for w, n in parts], axis=1
        )

    def ffn_cut(row, size):
        return jnp.concatenate(
            [
                lax.dynamic_slice(
                    w[0], (row, k * reps * ff_piece + rep * ff_piece), (size, ff_piece)
                )
                for w in (w_gate, w_up)
                for k in range(depth)
            ],
            axis=1,
        )

    out_rows = w_output.shape[1] // reps

    def attn_cut(row, size):
        height = out_rows * size // w_query.shape[1]
        first = rep * out_rows + row * out_rows // w_query.shape[1]
        out = lax.dynamic_slice_in_dim(w_output[0], first, height)
        return jnp.concatenate([qkv_cut(row, size), out.reshape(size, -1)], axis=1)

    def all_ffn_cut(row, size):
        height = ff_piece * size // w_gate.shape[1]
        first = rep * ff_piece + row * ff_piece // w_gate.shape[1]
        down = lax.dynamic_slice_in_dim(w_down[0], first, height)
        return jnp.concatenate([ffn_cut(row, size), down.reshape(size, -1)], axis=1)

    attn_all = spread(split(attn_cut, w_query.shape[1]))
    qkv_width = q_width + 2 * k_width
    qkv_all = [v[:, :qkv_width] for v in attn_all]
    out_all = [
        lax.all_to_all(v[:, qkv_width:].reshape(-1, width), "rep", 0, 0, tiled=True)
        for v in attn_all
    ]
    both_all = spread(split(all_ffn_cut, w_gate.shape[1]))
    ffn_all = [v[:, : 2 * ff_width] for v in both_all]
    down_all = [v[:, 2 * ff_width :].reshape(ff_width, width) for v in both_all]

    starts = jnp.zeros((reps, rows), jnp.int32)
    biases = []
    within = jnp.arange(rows)
    for step in range(depth):
        key_ids, here = ids[step][:, :, None], plane_ids[:, None, :]
        exists = layer_z >= step
        starts = starts + jnp.sum((exists & (key_ids < here)).astype(jnp.int32), axis=1)
        allowed = exists & (key_ids == here)
        if step == 0:
            allowed = allowed & (within[:, None] <= within[None, :])
        biases.append(jnp.where(allowed, 0.0, masked_score).astype(bf16))
    bias = jnp.concatenate(biases, axis=1)
    cosine, sine = rope_tables((layer_z * rows + within - starts).astype(f32))

    def by_half(table):
        return table.reshape(reps, 2, half, 2 * HD).transpose(1, 0, 2, 3)

    cosine, sine = by_half(cosine), by_half(sine)

    def flat(value):
        return value.reshape(count, -1)

    def blocks(value):
        return value.reshape(2, reps, half, -1)

    def forward(layer, layer_in):
        gain_attn, gain_ffn = gains[layer][0], gains[layer][1]
        scale_in = scale_of(layer_in)
        a_all = plane_gather((layer_in * scale_in * gain_attn).astype(bf16))
        query, keyval = project(a_all, qkv_all[layer], cosine, sine, q_width, k_width)
        keyvals = [keyval] + [
            back(keyval, step) for step in range(1, depth)
        ]
        mixed, log_total = attend(query, keyvals, bias)
        residual = layer_in + plane_reduce(blocks(times(flat(mixed), out_all[layer]).astype(bf16)))
        scale_mid = scale_of(residual)
        b_all = plane_gather((residual * scale_mid * gain_ffn).astype(bf16))
        pre = times(flat(b_all), ffn_all[layer])
        gate, up = pre[:, :ff_width], pre[:, ff_width:]
        hidden = (jax.nn.silu(gate) * up).astype(bf16)
        out = residual + plane_reduce(blocks(times(hidden, down_all[layer]).astype(bf16)))
        kept = (layer_in, scale_in, a_all, query, keyvals, mixed, log_total)
        return out.astype(bf16), kept + (residual, scale_mid, b_all, gate, up, hidden)

    def core_product(left, right, extra=None):
        size = left.shape[1] // (2 * depth)

        def half_of(value, which):
            return jnp.concatenate(
                [
                    lax.dynamic_slice_in_dim(value, (2 * k + which) * size, size, axis=1)
                    for k in range(depth)
                ],
                axis=1,
            )

        def product(which, right):
            found = dot(half_of(left, which), right, 0, 0)
            if extra is None:
                return found
            more = half_of(extra, which).T
            more = jnp.pad(more, ((0, 0), (0, 128 - more.shape[1])))
            return jnp.concatenate([found, more], axis=1)

        def finish(right, sent):
            got = lax.ppermute(sent, "section", SWAP)
            return (product(core, right) + got.astype(f32)).astype(bf16)

        return product(1 - core, right).astype(bf16), finish

    info = jnp.stack([core, rep]).astype(jnp.int32)

    def collect(total):
        return lax.psum_scatter(total, "fsdp", scatter_dimension=0, tiled=True)

    def backward(layer, grad_out, kept, earlier, ready):
        (layer_in, scale_in, a_all, query, keyvals, mixed, log_total) = kept[:7]
        (residual, scale_mid, b_all, gate, up, hidden) = kept[7:]
        gain_attn, gain_ffn = gains[layer][0], gains[layer][1]
        last = earlier is not None
        if last:
            old_rest, old_gate, old_up, old_down = earlier
            tall = old_up.shape[0]

            state = gather_step(gather_start(grad_out), 0)
            *state, old_gate, old_up = together(*state, old_gate, old_up)
            old_ffn = jnp.concatenate([old_gate, old_up], axis=1)
            gm_all = flat(gather_rest(state, 1))
            sent_down, finish = core_product(hidden, gm_all)
            gm_all, sent_down, old_ffn = together(gm_all, sent_down, old_ffn)
            ffn_state = gather_step(gather_start(old_ffn), 0)
        else:
            gm_all = flat(plane_gather(grad_out))
            sent_down, finish = core_product(hidden, gm_all)
            gm_all, sent_down, *ready = together(gm_all, sent_down, *ready)
        grad_hidden = times_back(gm_all, down_all[layer])
        sig = jax.nn.sigmoid(gate)
        grad_gate = (grad_hidden * up * (sig * (1.0 + gate * (1.0 - sig)))).astype(bf16)
        grad_up = (grad_hidden * (gate * sig)).astype(bf16)
        grad_pre = jnp.concatenate([grad_gate, grad_up], axis=1)
        part_down = finish(gm_all, sent_down)
        if last:
            grad_pre, *ffn_state = together(grad_pre, *ffn_state)
        own_down = collect(part_down)
        db = blocks(times_back(grad_pre, ffn_all[layer]).astype(bf16))
        db, grad_gate, grad_up = together(db, grad_gate, grad_up)
        db = plane_reduce(db)
        sent_gate, finish_gate = core_product(flat(b_all), grad_gate)
        sent_up, finish_up = core_product(flat(b_all), grad_up)
        unit = residual * scale_mid
        grad_mid, gain_grad_ffn = norm_back(db, gain_ffn, unit, scale_mid)
        grad_mid = grad_mid + grad_out.astype(f32)
        go = grad_mid.astype(bf16)
        go_all = flat(plane_gather(go))
        go_all, part_gate, part_up = together(
            go_all, finish_gate(grad_gate, sent_gate), finish_up(grad_up, sent_up)
        )
        own_gate, own_up = collect(part_gate), collect(part_up)
        grad_mixed = blocks(times_back(go_all, out_all[layer]).astype(bf16))
        if last:
            grad_mixed, own_down, old_rest, *ffn_state = together(
                grad_mixed, own_down, old_rest, *ffn_state
            )
            ffn_state = gather_step(ffn_state, 1)
            rest_state = gather_step(gather_start(old_rest), 0)
        else:
            grad_mixed, own_down = together(grad_mixed, own_down)
        own_down = gather_pair(gather_start(own_down), 0)
        grad_query, grad_kv = attend_back(query, keyvals, grad_mixed, log_total, bias)
        grad_query, go_all, *grad_kv = together(grad_query, go_all, *grad_kv)
        grad_kv = [grad_kv[0]] + [
            lax.ppermute(grad_kv[step], "fsdp", [(i, i - step) for i in range(step, depth)])
            for step in range(1, depth)
        ]
        sent_o, finish = core_product(flat(mixed), go_all)
        part_o = lax.all_to_all(finish(go_all, sent_o), "rep", 0, 0, tiled=True)
        grad_qkv, da = project_back(grad_query, grad_kv, qkv_all[layer], cosine, sine, k_width)
        grad_qkv = flat(grad_qkv)

        def input_side(da):
            unit = layer_in * scale_in
            grad_in, gain_grad_attn = norm_back(da, gain_attn, unit, scale_in)
            grad_in = (grad_in + grad_mid).astype(bf16)
            gain_grads = jnp.stack([gain_grad_attn, gain_grad_ffn])
            sent_proj, finish = core_product(flat(a_all), grad_qkv, gain_grads)
            part_proj = finish(grad_qkv, sent_proj)
            pieces = part_proj.shape[0] // part_o.shape[0]
            aside = part_o.reshape(depth, -1, pieces, width // pieces).transpose(0, 2, 1, 3)
            aside = aside.reshape(part_proj.shape[0], -1)
            return grad_in, jnp.concatenate([part_proj, aside], axis=1)

        if not last:
            da, grad_qkv, part_o, own_gate, *own_down = together(
                da, grad_qkv, part_o, own_gate, *own_down
            )
            grad_in, part_rest = input_side(plane_reduce(da))
            return grad_in, (collect(part_rest), own_gate, own_up, own_down), ready

        def send(pair):
            return [lax.ppermute(v, "section", [(0, 1)]) for v in pair]

        def eight(zero, one, one_sent):
            found = []
            for sub in range(2):
                got = lax.ppermute(zero[sub], "section", [(1, 0)])
                found += [zero[sub], one_sent[sub], got, one[sub]]
            return found

        da, *states = together(da, *own_down, *ffn_state, *rest_state)
        zero_down = states[:2]
        old_ffn, old_rest = gather_pair(states[2:4], 2), gather_pair(states[4:], 1)
        olds_sent = send(old_ffn) + send(old_down)
        da, own_gate = together(plane_reduce(da), own_gate)
        grad_in, part_rest = input_side(da)
        gate_state = gather_step(gather_start(own_gate), 0)
        tied = together(part_rest, own_up, *gate_state, *olds_sent, *old_rest)
        part_rest, own_up = tied[:2]
        gate_state, olds_sent, old_rest = tied[2:4], tied[4:8], tied[8:]
        ffn_sent, down_sent = olds_sent[:2], olds_sent[2:]
        own_rest = collect(part_rest)
        rest_sent = send(old_rest)
        zero_gate = gather_pair(gate_state, 1)
        up_state = gather_step(gather_start(own_up), 0)
        own_rest, *tied = together(own_rest, *zero_gate, *up_state, *rest_sent)
        zero_gate, up_state, rest_sent = tied[:2], tied[2:4], tied[4:]
        zero_up, zero_rest = gather_pair(up_state, 1), gather_pair(gather_start(own_rest), 0)
        places = eight(zero_gate, old_ffn, ffn_sent)
        grad_gate = assemble_columns(info, places, (0, 0), ff_piece, depth)
        grad_down = assemble_rows(info, eight(zero_down, old_down, down_sent))
        grad_gate, grad_down, *tied = together(grad_gate, grad_down, *zero_up, *zero_rest)
        zero_up, zero_rest = tied[:2], tied[2:]
        places = eight(zero_up, old_ffn, ffn_sent)
        grad_up = assemble_columns(info, places, (0, depth), ff_piece, depth)
        height = out_rows // 2
        proj_width = own_rest.shape[1] - height * width // tall
        places = eight(zero_rest, old_rest, rest_sent)
        sizes = (q_width, k_width, k_width)
        rest = assemble_rest(info, places, sizes, proj_width, height, width)
        gain_parts = [
            jnp.sum(v[..., qkv_width : qkv_width + 2].astype(f32), axis=0) for v in places
        ]
        gain_sums = jnp.concatenate(
            [
                jnp.where(core == 0, gain_parts[at], gain_parts[at + 1])
                for at in (0, 4, 2, 6)
            ],
            axis=0,
        )
        return grad_in, gain_sums, (*rest, grad_gate, grad_up, grad_down)

    own_tokens = lax.dynamic_index_in_dim(tokens[0], core, 0, keepdims=False)
    own_cotangent = lax.dynamic_index_in_dim(cotangent[0], core, 0, keepdims=False)
    out0, kept0 = forward(0, own_tokens.astype(f32))
    out1, kept1 = forward(1, out0.astype(f32))

    def swapped(zero, one):
        got = lax.ppermute(jnp.where(core == 0, one, zero), "section", SWAP)
        return jnp.where(core == 0, zero, got), jnp.where(core == 0, got, one)

    grad1, sums1, outputs = backward(1, own_cotangent, kept1, None, swapped(out0, out1))
    grad0, gain_sums, weight_grads = backward(0, grad1, kept0, sums1, None)
    outputs = jnp.stack(outputs)[None, None]
    input_grads = jnp.stack(swapped(grad0, grad1))[None, None]
    grad_query, grad_key, grad_value, grad_output, grad_gate, grad_up, grad_down = weight_grads
    return (
        outputs,
        input_grads,
        gain_sums[:, 0][None],
        grad_query[None],
        grad_key[None],
        grad_value[None],
        grad_output[None],
        gain_sums[:, 1][None],
        grad_gate[None],
        grad_up[None],
        grad_down[None],
    )


def solution(mesh):
    in_specs = (
        P("rep", None, "fsdp", None),
        P("rep", None, "fsdp"),
        P("rep", None, "fsdp", None),
        P("section", "fsdp"),
        P("section", "fsdp", None),
        P("section", "fsdp", None),
        P("section", "fsdp", None),
        P("section", "fsdp", None),
        P("section", "fsdp"),
        P("section", "fsdp", None),
        P("section", "fsdp", None),
        P("section", "fsdp", None),
    )
    out_specs = (
        P("section", "rep", None, "fsdp", None),
        P("section", "rep", None, "fsdp", None),
        P("section", "fsdp"),
        P("section", "fsdp", None),
        P("section", "fsdp", None),
        P("section", "fsdp", None),
        P("section", "fsdp", None),
        P("section", "fsdp"),
        P("section", "fsdp", None),
        P("section", "fsdp", None),
        P("section", "fsdp", None),
    )
    return jax.shard_map(shards, mesh=mesh, in_specs=in_specs, out_specs=out_specs, check_vma=False)
```

```python
import functools

import jax
import jax.numpy as jnp
from jax import lax
from jax.experimental import pallas as pl
from jax.experimental.pallas import tpu as pltpu
from jax.sharding import PartitionSpec as P

HQ = 32
KVH = 8
HD = 64
FF = 8192

epsilon = 1e-05
rope_base = 500000.0
masked_score = -1e30
bf16 = jnp.bfloat16
f32 = jnp.float32
SWAP = [(0, 1), (1, 0)]


def partner(value, bit):
    count = lax.axis_size("rep")
    return lax.ppermute(value, "rep", [(i, i ^ bit) for i in range(count)])


def bit_list(count):
    found = []
    bit = 1
    while bit < count:
        found.append(bit)
        bit *= 2
    return found


def gather_start(own):
    half = own.shape[0] // 2
    return own[None, :half], own[None, half:]


def gather_step(state, at):
    bits = bit_list(lax.axis_size("rep"))
    first, second = state
    first = jnp.concatenate([first, partner(first, bits[at])], axis=0)
    other = partner(second, bits[-1 - at])
    second = jnp.stack([second, other], axis=1).reshape((-1,) + second.shape[1:])
    return first, second


def gather_pair(state, at):
    for step in range(at, len(bit_list(lax.axis_size("rep")))):
        state = gather_step(state, step)
    return list(state)


def gather_rest(state, at):
    return jnp.stack(gather_pair(state, at))


def plane_gather(own):
    return gather_rest(gather_start(own), 0)


def plane_reduce(parts):
    bits = bit_list(lax.axis_size("rep"))
    first, second = parts[0], parts[1]
    for bit in bits[::-1]:
        keep, away = first[:bit], first[bit:]
        first = keep.astype(f32) + partner(away.astype(bf16), bit).astype(f32)
    for bit in bits:
        pair = second.reshape((-1, 2) + second.shape[1:])
        keep, away = pair[:, 0], pair[:, 1]
        second = keep.astype(f32) + partner(away.astype(bf16), bit).astype(f32)
    return jnp.concatenate([first[0], second[0]], axis=0)


def rope_tables(positions):
    half_size = HD // 2
    frequency = rope_base ** (-(jnp.arange(half_size).astype(f32) * 2.0) / HD)
    angles = positions[..., None] * frequency
    cosine, sine = jnp.cos(angles), jnp.sin(angles)
    return (
        jnp.concatenate([cosine] * 4, axis=-1),
        jnp.concatenate([-sine, sine] * 2, axis=-1),
    )


def times(left, weight):
    return jnp.dot(left, weight, preferred_element_type=f32)


def times_back(left, weight):
    return lax.dot_general(
        left, weight, (((1,), (1,)), ((), ())), preferred_element_type=f32
    )


def scale_of(values):
    return lax.rsqrt(jnp.mean(values * values, axis=-1, keepdims=True) + epsilon)


def norm_back(grad, gain, unit, scale):
    scaled = gain * grad
    out = scale * (scaled - unit * jnp.mean(scaled * unit, axis=-1, keepdims=True))
    return (out, jnp.sum(grad * unit, axis=0))


def sequence(ref):
    return ref[:, 0].reshape(-1, ref.shape[-1])


def scaled(value):
    return (value.astype(f32) * HD ** (-0.5)).astype(bf16)


def dot(left, right, left_dim, right_dim):
    return lax.dot_general(
        left, right, (((left_dim,), (right_dim,)), ((), ())), preferred_element_type=f32
    )


def attend_kernel(depth, query_ref, bias_ref, *refs):
    mixed_ref, log_ref = refs[depth:]
    keyval = jnp.concatenate([sequence(ref) for ref in refs[:depth]], axis=0)
    query = scaled(sequence(query_ref))
    bias = bias_ref[0].astype(f32)
    k_width = keyval.shape[1] // 2
    heads = query.shape[1] // HD
    group = heads // (k_width // HD)
    columns = []
    for head in range(heads):
        at = head // group * HD
        key = keyval[:, at : at + HD]
        value = keyval[:, k_width + at : k_width + at + HD]
        scores = dot(key, query[:, head * HD : (head + 1) * HD], 1, 1) + bias
        row_max = jnp.max(scores, axis=0, keepdims=True)
        weights = jnp.exp(scores - row_max)
        total = jnp.sum(weights, axis=0, keepdims=True)
        probs = (weights * (1.0 / total)).astype(bf16)
        columns.append(dot(value, probs, 0, 0))
        log_ref[0, head : head + 1, :] = row_max + jnp.log(total)
    mixed = jnp.concatenate(columns, axis=0).T.astype(bf16)
    mixed_ref[:, 0] = mixed.reshape(2, -1, mixed.shape[1])


def attend_back_kernel(depth, query_ref, grad_ref, log_ref, bias_ref, *refs):
    grad_query_ref, grad_refs = refs[depth], refs[depth + 1 :]
    keyval = jnp.concatenate([sequence(ref) for ref in refs[:depth]], axis=0)
    query = scaled(sequence(query_ref))
    grad = sequence(grad_ref)
    bias = bias_ref[0].astype(f32)
    k_width = keyval.shape[1] // 2
    heads = query.shape[1] // HD
    group = heads // (k_width // HD)
    columns, grad_keys, grad_values = [], [], []
    for head in range(heads):
        at = head // group * HD
        key = keyval[:, at : at + HD]
        value = keyval[:, k_width + at : k_width + at + HD]
        own_query = query[:, head * HD : (head + 1) * HD]
        own_grad = grad[:, head * HD : (head + 1) * HD]
        scores = dot(key, own_query, 1, 1) + bias
        probs = jnp.exp(scores - log_ref[0, head : head + 1, :])
        grad_probs = dot(value, own_grad, 1, 1)
        inner = jnp.sum(probs * grad_probs, axis=0, keepdims=True)
        grad_scores = (probs * (grad_probs - inner)).astype(bf16)
        columns.append(dot(key, grad_scores, 0, 0))
        grad_key = dot(grad_scores, own_query, 1, 0)
        grad_value = dot(probs.astype(bf16), own_grad, 1, 0)
        if head % group == 0:
            grad_keys.append(grad_key)
            grad_values.append(grad_value)
        else:
            grad_keys[-1] = grad_keys[-1] + grad_key
            grad_values[-1] = grad_values[-1] + grad_value
    grad_query = jnp.concatenate(columns, axis=0).T * HD ** (-0.5)
    grad_query_ref[:, 0] = grad_query.reshape(2, -1, grad_query.shape[1])
    both = jnp.concatenate(grad_keys + grad_values, axis=1).astype(bf16)
    rows = both.shape[0] // depth
    for step, ref in enumerate(grad_refs):
        part = both[step * rows : (step + 1) * rows]
        ref[:, 0] = part.reshape(2, rows // 2, part.shape[1])


def sequence_spec(array):
    two, _, half, columns = array.shape
    return pl.BlockSpec((two, 1, half, columns), lambda j: (0, j, 0, 0))


def row_spec(array):
    return pl.BlockSpec((1,) + array.shape[1:], lambda j: (j, 0, 0))


def attend(query, keyvals, bias):
    two, reps, half, width = query.shape
    logs = jax.ShapeDtypeStruct((reps, width // HD, two * half), f32)
    cells = reps * width * two * half * bias.shape[1]
    return pl.pallas_call(
        functools.partial(attend_kernel, len(keyvals)),
        grid=(reps,),
        in_specs=[sequence_spec(query), row_spec(bias)] + [sequence_spec(v) for v in keyvals],
        out_specs=[sequence_spec(query), row_spec(logs)],
        out_shape=[jax.ShapeDtypeStruct(query.shape, bf16), logs],
        compiler_params=pltpu.CompilerParams(vmem_limit_bytes=48 << 20),
        cost_estimate=pl.CostEstimate(
            flops=16 * cells, bytes_accessed=8 << 20, transcendentals=cells // HD
        ),
        name="attend",
    )(query, bias, *keyvals)


def attend_back(query, keyvals, grad_mixed, log_total, bias):
    two, reps, half, width = query.shape
    cells = reps * width * two * half * bias.shape[1]
    outs = pl.pallas_call(
        functools.partial(attend_back_kernel, len(keyvals)),
        grid=(reps,),
        in_specs=[sequence_spec(query), sequence_spec(grad_mixed), row_spec(log_total)]
        + [row_spec(bias)]
        + [sequence_spec(v) for v in keyvals],
        out_specs=[sequence_spec(query)] + [sequence_spec(v) for v in keyvals],
        out_shape=[jax.ShapeDtypeStruct(query.shape, f32)]
        + [jax.ShapeDtypeStruct(v.shape, bf16) for v in keyvals],
        compiler_params=pltpu.CompilerParams(vmem_limit_bytes=48 << 20),
        cost_estimate=pl.CostEstimate(
            flops=40 * cells, bytes_accessed=12 << 20, transcendentals=cells // HD
        ),
        name="attend_back",
    )(query, grad_mixed, log_total, bias, *keyvals)
    return outs[0], outs[1:]


def turned_pair(value):
    lane = lax.broadcasted_iota(jnp.int32, value.shape, 1)
    half = HD // 2
    ahead = pltpu.roll(value, value.shape[1] - half, 1)
    behind = pltpu.roll(value, half, 1)
    return jnp.where(lane % HD < half, ahead, behind)


def widened(table, width):
    return jnp.concatenate([table] * (width // table.shape[1]), axis=1)


def rows_of(ref):
    return ref[0].reshape(-1, ref.shape[-1])


def project_kernel(k_width, a_ref, weight_ref, cosine_ref, sine_ref, query_ref, keyval_ref):
    mixed = dot(rows_of(a_ref), weight_ref[...], 1, 0)
    width = mixed.shape[1]
    cosine = widened(rows_of(cosine_ref), width)
    sine = widened(rows_of(sine_ref), width)
    rotated = mixed * cosine + turned_pair(mixed) * sine
    lane = lax.broadcasted_iota(jnp.int32, mixed.shape, 1)
    rotated = jnp.where(lane < width - k_width, rotated, mixed).astype(bf16)
    q_width = query_ref.shape[-1]
    query_ref[0] = rotated[:, :q_width].reshape(query_ref.shape[1:])
    keyval_ref[0] = rotated[:, q_width:].reshape(keyval_ref.shape[1:])


def project_back_kernel(k_width, grad_ref, weight_ref, cosine_ref, sine_ref, *refs):
    parts, (joined_ref, out_ref) = refs[:-2], refs[-2:]
    keyval = rows_of(parts[0]).astype(f32)
    for part in parts[1:]:
        keyval = keyval + rows_of(part).astype(f32)
    joined = jnp.concatenate([rows_of(grad_ref), keyval], axis=1)
    width = joined.shape[1]
    cosine = widened(rows_of(cosine_ref), width)
    sine = widened(rows_of(sine_ref), width)
    rotated = joined * cosine - turned_pair(joined) * sine
    lane = lax.broadcasted_iota(jnp.int32, joined.shape, 1)
    rotated = jnp.where(lane < width - k_width, rotated, joined).astype(bf16)
    joined_ref[0] = rotated.reshape(joined_ref.shape[1:])
    out = dot(rotated, weight_ref[...], 1, 1).astype(bf16)
    out_ref[0] = out.reshape(out_ref.shape[1:])


def half_spec(array):
    return pl.BlockSpec((1,) + array.shape[1:], lambda i: (i, 0, 0, 0))


def all_spec(array):
    return pl.BlockSpec(array.shape, lambda i: (0, 0))


def project(a_all, weight, cosine, sine, q_width, k_width):
    shape = a_all.shape[:3]
    outs = [
        jax.ShapeDtypeStruct(shape + (q_width,), bf16),
        jax.ShapeDtypeStruct(shape + (2 * k_width,), bf16),
    ]
    cells = a_all.size * weight.shape[1]
    return pl.pallas_call(
        functools.partial(project_kernel, k_width),
        grid=(2,),
        in_specs=[half_spec(a_all), all_spec(weight), half_spec(cosine), half_spec(sine)],
        out_specs=[half_spec(v) for v in outs],
        out_shape=outs,
        compiler_params=pltpu.CompilerParams(vmem_limit_bytes=40 << 20),
        cost_estimate=pl.CostEstimate(
            flops=2 * cells, bytes_accessed=10 << 20, transcendentals=0
        ),
        name="project",
    )(a_all, weight, cosine, sine)


def project_back(grad_query, parts, weight, cosine, sine, k_width):
    shape = grad_query.shape[:3]
    outs = [
        jax.ShapeDtypeStruct(shape + (weight.shape[1],), bf16),
        jax.ShapeDtypeStruct(shape + (weight.shape[0],), bf16),
    ]
    cells = outs[0].size * weight.shape[0]
    return pl.pallas_call(
        functools.partial(project_back_kernel, k_width),
        grid=(2,),
        in_specs=[half_spec(grad_query), all_spec(weight), half_spec(cosine), half_spec(sine)]
        + [half_spec(v) for v in parts],
        out_specs=[half_spec(v) for v in outs],
        out_shape=outs,
        compiler_params=pltpu.CompilerParams(vmem_limit_bytes=48 << 20),
        cost_estimate=pl.CostEstimate(
            flops=2 * cells, bytes_accessed=14 << 20, transcendentals=0
        ),
        name="project_back",
    )(grad_query, weight, cosine, sine, *parts)


def by_place(info, refs, write):
    which = info[0] + 2 * pl.program_id(0) + 4 * pl.program_id(1)
    for at, ref in enumerate(refs):
        pl.when(which == at)(functools.partial(write, ref))


def columns_kernel(piece, info, *refs):
    out_ref = refs[8]
    reps, _, taken = refs[0].shape

    def write(ref):
        for at in range(taken // piece):
            for rep in range(reps):
                start = (at * reps + rep) * piece
                found = ref[rep ^ info[1], :, at * piece : (at + 1) * piece]
                out_ref[:, start : start + piece] = found.astype(f32)

    by_place(info, refs[:8], write)


def rows_kernel(info, *refs):
    out_ref = refs[8]

    def write(ref):
        for rep in range(out_ref.shape[0]):
            out_ref[rep, 0] = ref[rep ^ info[1]].astype(f32)

    by_place(info, refs[:8], write)


def rest_kernel(proj_width, info, *refs):
    outs, output_ref = refs[8:11], refs[11]
    reps, rows, width = refs[0].shape
    height, piece = output_ref.shape[2], width - proj_width

    def write(ref):
        for rep in range(reps):
            block = ref[rep ^ info[1]].astype(f32)
            start = 0
            for out_ref in outs:
                size = out_ref.shape[1] // reps
                out_ref[:, rep * size : (rep + 1) * size] = block[:, start : start + size]
                start += size
            for at in range(rows // height):
                part = block[at * height : (at + 1) * height, proj_width:]
                output_ref[rep, 0, :, at * piece : (at + 1) * piece] = part

    by_place(info, refs[:8], write)


def assembled(kernel, grid, block, index, out_blocks, out_index, out_shapes, info, eight):
    def chosen(at):
        def where_from(*steps):
            taken = steps[-1][0] + 2 * steps[0] + 4 * steps[1] == at
            return tuple(jnp.where(taken, v, 0) for v in index(at % 2, *steps))

        return where_from

    return pl.pallas_call(
        kernel,
        grid_spec=pltpu.PrefetchScalarGridSpec(
            num_scalar_prefetch=1,
            grid=grid,
            in_specs=[pl.BlockSpec(block, chosen(at)) for at in range(8)],
            out_specs=[pl.BlockSpec(b, f) for b, f in zip(out_blocks, out_index)],
        ),
        out_shape=[jax.ShapeDtypeStruct(v, f32) for v in out_shapes],
        compiler_params=pltpu.CompilerParams(vmem_limit_bytes=56 << 20),
        name="assemble",
    )(info, *eight)


def assemble_columns(info, eight, offsets, piece, pieces):
    reps, rows, _ = eight[0].shape
    step = 2 if pieces % 2 == 0 else 1
    return assembled(
        functools.partial(columns_kernel, piece),
        (2, 2, pieces // step),
        (reps, rows, step * piece),
        lambda layer, k, sub, at, info: (0, 0, offsets[layer] // step + at),
        [(rows, step * reps * piece)],
        [lambda k, sub, at, info: (2 * k + sub, at)],
        [(4 * rows, reps * piece * pieces)],
        info,
        eight,
    )[0]


def assemble_rows(info, eight):
    reps, rows, columns = eight[0].shape
    return assembled(
        rows_kernel,
        (2, 2),
        (reps, rows, columns),
        lambda layer, k, sub, info: (0, 0, 0),
        [(reps, 1, rows, columns)],
        [lambda k, sub, info: (0, 2 * k + sub, 0, 0)],
        [(reps, 4, rows, columns)],
        info,
        eight,
    )[0].reshape(-1, columns)


def assemble_rest(info, eight, sizes, proj_width, height, width):
    reps, rows, columns = eight[0].shape
    outs = assembled(
        functools.partial(rest_kernel, proj_width),
        (2, 2),
        (reps, rows, columns),
        lambda layer, k, sub, info: (0, 0, 0),
        [(rows, reps * size) for size in sizes] + [(reps, 1, height, width // 2)],
        [lambda k, sub, info: (2 * k + sub, 0)] * len(sizes)
        + [lambda k, sub, info: (0, k, 0, sub)],
        [(4 * rows, reps * size) for size in sizes] + [(reps, 2, height, width)],
        info,
        eight,
    )
    return (*outs[:-1], outs[-1].reshape(-1, width))


def together(*values):
    return lax.optimization_barrier(values)


def shards(
    tokens,
    segment_ids,
    cotangent,
    norm_attn,
    w_query,
    w_key,
    w_value,
    w_output,
    norm_ffn,
    w_gate,
    w_up,
    w_down,
):
    core = lax.axis_index("section")
    layer_z = lax.axis_index("fsdp")
    rep = lax.axis_index("rep")
    depth = lax.axis_size("fsdp")
    reps = lax.axis_size("rep")
    rows, width = tokens.shape[2:]
    half = rows // 2
    count = reps * rows
    q_width = HQ * HD // reps
    k_width = KVH * HD // reps
    ff_width = FF // reps
    ff_piece = FF // (reps * depth)

    def back(value, step):
        return lax.ppermute(value, "fsdp", [(i, i + step) for i in range(depth - step)])

    def by_layer(own, got):
        return (jnp.where(core == 0, own, got), jnp.where(core == 0, got, own))

    own_gain = jnp.concatenate([norm_attn, norm_ffn], axis=0)
    turned = jnp.stack(
        [own_gain]
        + [
            lax.ppermute(own_gain, "fsdp", [(i, (i + s) % depth) for i in range(depth)])
            for s in range(1, depth)
        ]
    )
    own_gain = jnp.concatenate(
        [
            lax.dynamic_index_in_dim(turned, (layer_z - k + depth) % depth, 0, keepdims=False)
            for k in range(depth)
        ],
        axis=1,
    ).astype(f32)
    gains = by_layer(own_gain, lax.ppermute(own_gain, "section", SWAP))

    plane_ids = lax.dynamic_index_in_dim(segment_ids[0], core, 0, keepdims=True)
    for bit in bit_list(reps):
        plane_ids = jnp.concatenate([plane_ids, partner(plane_ids, bit)], axis=0)
    ids = [plane_ids] + [back(plane_ids, step) for step in range(1, depth)]

    def split(cut, total):
        size = total // 2
        got = lax.ppermute(cut((1 - core) * size, size), "section", SWAP)
        return by_layer(cut(core * size, size), got)

    def spread(pieces):
        return [lax.all_gather(v, ("fsdp", "section"), axis=0, tiled=True) for v in pieces]

    def qkv_cut(row, size):
        parts = ((w_query, q_width), (w_key, k_width), (w_value, k_width))
        return jnp.concatenate(
            [lax.dynamic_slice(w[0], (row, rep * n), (size, n)) for w, n in parts], axis=1
        )

    def ffn_cut(row, size):
        return jnp.concatenate(
            [
                lax.dynamic_slice(
                    w[0], (row, k * reps * ff_piece + rep * ff_piece), (size, ff_piece)
                )
                for w in (w_gate, w_up)
                for k in range(depth)
            ],
            axis=1,
        )

    out_rows = w_output.shape[1] // reps

    def attn_cut(row, size):
        height = out_rows * size // w_query.shape[1]
        first = rep * out_rows + row * out_rows // w_query.shape[1]
        out = lax.dynamic_slice_in_dim(w_output[0], first, height)
        return jnp.concatenate([qkv_cut(row, size), out.reshape(size, -1)], axis=1)

    def all_ffn_cut(row, size):
        height = ff_piece * size // w_gate.shape[1]
        first = rep * ff_piece + row * ff_piece // w_gate.shape[1]
        down = lax.dynamic_slice_in_dim(w_down[0], first, height)
        return jnp.concatenate([ffn_cut(row, size), down.reshape(size, -1)], axis=1)

    attn_all = spread(split(attn_cut, w_query.shape[1]))
    qkv_width = q_width + 2 * k_width
    qkv_all = [v[:, :qkv_width] for v in attn_all]
    out_all = [
        lax.all_to_all(v[:, qkv_width:].reshape(-1, width), "rep", 0, 0, tiled=True)
        for v in attn_all
    ]
    both_all = spread(split(all_ffn_cut, w_gate.shape[1]))
    ffn_all = [v[:, : 2 * ff_width] for v in both_all]
    down_all = [v[:, 2 * ff_width :].reshape(ff_width, width) for v in both_all]

    starts = jnp.zeros((reps, rows), jnp.int32)
    biases = []
    within = jnp.arange(rows)
    for step in range(depth):
        key_ids, here = ids[step][:, :, None], plane_ids[:, None, :]
        exists = layer_z >= step
        starts = starts + jnp.sum((exists & (key_ids < here)).astype(jnp.int32), axis=1)
        allowed = exists & (key_ids == here)
        if step == 0:
            allowed = allowed & (within[:, None] <= within[None, :])
        biases.append(jnp.where(allowed, 0.0, masked_score).astype(bf16))
    bias = jnp.concatenate(biases, axis=1)
    cosine, sine = rope_tables((layer_z * rows + within - starts).astype(f32))

    def by_half(table):
        return table.reshape(reps, 2, half, 2 * HD).transpose(1, 0, 2, 3)

    cosine, sine = by_half(cosine), by_half(sine)

    def flat(value):
        return value.reshape(count, -1)

    def blocks(value):
        return value.reshape(2, reps, half, -1)

    def forward(layer, layer_in):
        gain_attn, gain_ffn = gains[layer][0], gains[layer][1]
        scale_in = scale_of(layer_in)
        a_all = plane_gather((layer_in * scale_in * gain_attn).astype(bf16))
        query, keyval = project(a_all, qkv_all[layer], cosine, sine, q_width, k_width)
        keyvals = [keyval] + [
            back(keyval, step) for step in range(1, depth)
        ]
        mixed, log_total = attend(query, keyvals, bias)
        residual = layer_in + plane_reduce(blocks(times(flat(mixed), out_all[layer]).astype(bf16)))
        scale_mid = scale_of(residual)
        b_all = plane_gather((residual * scale_mid * gain_ffn).astype(bf16))
        pre = times(flat(b_all), ffn_all[layer])
        gate, up = pre[:, :ff_width], pre[:, ff_width:]
        hidden = (jax.nn.silu(gate) * up).astype(bf16)
        out = residual + plane_reduce(blocks(times(hidden, down_all[layer]).astype(bf16)))
        kept = (layer_in, scale_in, a_all, query, keyvals, mixed, log_total)
        return out.astype(bf16), kept + (residual, scale_mid, b_all, gate, up, hidden)

    def core_product(left, right, extra=None):
        size = left.shape[1] // (2 * depth)

        def half_of(value, which):
            return jnp.concatenate(
                [
                    lax.dynamic_slice_in_dim(value, (2 * k + which) * size, size, axis=1)
                    for k in range(depth)
                ],
                axis=1,
            )

        def product(which, right):
            found = dot(half_of(left, which), right, 0, 0)
            if extra is None:
                return found
            more = half_of(extra, which).T
            more = jnp.pad(more, ((0, 0), (0, 128 - more.shape[1])))
            return jnp.concatenate([found, more], axis=1)

        def finish(right, sent):
            got = lax.ppermute(sent, "section", SWAP)
            return (product(core, right) + got.astype(f32)).astype(bf16)

        return product(1 - core, right).astype(bf16), finish

    info = jnp.stack([core, rep]).astype(jnp.int32)

    def collect(total):
        return lax.psum_scatter(total, "fsdp", scatter_dimension=0, tiled=True)

    def backward(layer, grad_out, kept, earlier, ready):
        (layer_in, scale_in, a_all, query, keyvals, mixed, log_total) = kept[:7]
        (residual, scale_mid, b_all, gate, up, hidden) = kept[7:]
        gain_attn, gain_ffn = gains[layer][0], gains[layer][1]
        last = earlier is not None
        if last:
            old_rest, old_gate, old_up, old_down = earlier
            tall = old_up.shape[0]

            state = gather_step(gather_start(grad_out), 0)
            *state, old_gate, old_up = together(*state, old_gate, old_up)
            old_ffn = jnp.concatenate([old_gate, old_up], axis=1)
            gm_all = flat(gather_rest(state, 1))
            sent_down, finish = core_product(hidden, gm_all)
            gm_all, sent_down, old_ffn = together(gm_all, sent_down, old_ffn)
            ffn_state = gather_step(gather_start(old_ffn), 0)
        else:
            gm_all = flat(plane_gather(grad_out))
            sent_down, finish = core_product(hidden, gm_all)
            gm_all, sent_down, *ready = together(gm_all, sent_down, *ready)
        grad_hidden = times_back(gm_all, down_all[layer])
        sig = jax.nn.sigmoid(gate)
        grad_gate = (grad_hidden * up * (sig * (1.0 + gate * (1.0 - sig)))).astype(bf16)
        grad_up = (grad_hidden * (gate * sig)).astype(bf16)
        grad_pre = jnp.concatenate([grad_gate, grad_up], axis=1)
        part_down = finish(gm_all, sent_down)
        if last:
            grad_pre, *ffn_state = together(grad_pre, *ffn_state)
        own_down = collect(part_down)
        db = blocks(times_back(grad_pre, ffn_all[layer]).astype(bf16))
        db, grad_gate, grad_up = together(db, grad_gate, grad_up)
        db = plane_reduce(db)
        sent_gate, finish_gate = core_product(flat(b_all), grad_gate)
        sent_up, finish_up = core_product(flat(b_all), grad_up)
        unit = residual * scale_mid
        grad_mid, gain_grad_ffn = norm_back(db, gain_ffn, unit, scale_mid)
        grad_mid = grad_mid + grad_out.astype(f32)
        go = grad_mid.astype(bf16)
        if last:
            go, old_rest = together(go, old_rest)
        go_all = flat(plane_gather(go))
        go_all, part_gate, part_up = together(
            go_all, finish_gate(grad_gate, sent_gate), finish_up(grad_up, sent_up)
        )
        own_gate, own_up = collect(part_gate), collect(part_up)
        grad_mixed = blocks(times_back(go_all, out_all[layer]).astype(bf16))
        def output_part(go_all):
            sent_o, finish_o = core_product(flat(mixed), go_all)
            return lax.all_to_all(finish_o(go_all, sent_o), "rep", 0, 0, tiled=True)

        if last:
            grad_mixed, old_rest, *ffn_state = together(grad_mixed, old_rest, *ffn_state)
            ffn_state = gather_step(ffn_state, 1)
            rest_state = gather_step(gather_start(old_rest), 0)
            part_o = output_part(go_all)
        else:
            grad_mixed, own_down = together(grad_mixed, own_down)
            own_down = gather_pair(gather_start(own_down), 0)
        grad_query, grad_kv = attend_back(query, keyvals, grad_mixed, log_total, bias)
        if last:
            grad_query, part_o, own_down, *grad_kv = together(
                grad_query, part_o, own_down, *grad_kv
            )
            own_down = gather_pair(gather_start(own_down), 0)
        else:
            grad_query, go_all, *grad_kv = together(grad_query, go_all, *grad_kv)
        grad_kv = [grad_kv[0]] + [
            lax.ppermute(grad_kv[step], "fsdp", [(i, i - step) for i in range(step, depth)])
            for step in range(1, depth)
        ]
        if not last:
            part_o = output_part(go_all)
        grad_qkv, da = project_back(grad_query, grad_kv, qkv_all[layer], cosine, sine, k_width)
        grad_qkv = flat(grad_qkv)

        def input_side(da):
            unit = layer_in * scale_in
            grad_in, gain_grad_attn = norm_back(da, gain_attn, unit, scale_in)
            grad_in = (grad_in + grad_mid).astype(bf16)
            gain_grads = jnp.stack([gain_grad_attn, gain_grad_ffn])
            sent_proj, finish = core_product(flat(a_all), grad_qkv, gain_grads)
            part_proj = finish(grad_qkv, sent_proj)
            pieces = part_proj.shape[0] // part_o.shape[0]
            aside = part_o.reshape(depth, -1, pieces, width // pieces).transpose(0, 2, 1, 3)
            aside = aside.reshape(part_proj.shape[0], -1)
            return grad_in, jnp.concatenate([part_proj, aside], axis=1)

        if not last:
            da, grad_qkv, part_o, own_gate, *own_down = together(
                da, grad_qkv, part_o, own_gate, *own_down
            )
            grad_in, part_rest = input_side(plane_reduce(da))
            return grad_in, (collect(part_rest), own_gate, own_up, own_down), ready

        def send(pair):
            return [lax.ppermute(v, "section", [(0, 1)]) for v in pair]

        def eight(zero, one, one_sent):
            found = []
            for sub in range(2):
                got = lax.ppermute(zero[sub], "section", [(1, 0)])
                found += [zero[sub], one_sent[sub], got, one[sub]]
            return found

        da, *states = together(da, *own_down, *ffn_state, *rest_state)
        zero_down = states[:2]
        old_ffn, old_rest = gather_pair(states[2:4], 2), gather_pair(states[4:], 1)
        olds_sent = send(old_ffn) + send(old_down)
        da, own_gate = together(plane_reduce(da), own_gate)
        grad_in, part_rest = input_side(da)
        gate_state = gather_step(gather_start(own_gate), 0)
        tied = together(part_rest, own_up, *gate_state, *olds_sent, *old_rest)
        part_rest, own_up = tied[:2]
        gate_state, olds_sent, old_rest = tied[2:4], tied[4:8], tied[8:]
        ffn_sent, down_sent = olds_sent[:2], olds_sent[2:]
        own_rest = collect(part_rest)
        rest_sent = send(old_rest)
        zero_gate = gather_pair(gate_state, 1)
        up_state = gather_step(gather_start(own_up), 0)
        own_rest, *tied = together(own_rest, *zero_gate, *up_state, *rest_sent)
        zero_gate, up_state, rest_sent = tied[:2], tied[2:4], tied[4:]
        zero_up, zero_rest = gather_pair(up_state, 1), gather_pair(gather_start(own_rest), 0)
        places = eight(zero_gate, old_ffn, ffn_sent)
        grad_gate = assemble_columns(info, places, (0, 0), ff_piece, depth)
        grad_down = assemble_rows(info, eight(zero_down, old_down, down_sent))
        grad_gate, grad_down, *tied = together(grad_gate, grad_down, *zero_up, *zero_rest)
        zero_up, zero_rest = tied[:2], tied[2:]
        places = eight(zero_up, old_ffn, ffn_sent)
        grad_up = assemble_columns(info, places, (0, depth), ff_piece, depth)
        height = out_rows // 2
        proj_width = own_rest.shape[1] - height * width // tall
        places = eight(zero_rest, old_rest, rest_sent)
        sizes = (q_width, k_width, k_width)
        rest = assemble_rest(info, places, sizes, proj_width, height, width)
        gain_parts = [
            jnp.sum(v[..., qkv_width : qkv_width + 2].astype(f32), axis=0) for v in places
        ]
        gain_sums = jnp.concatenate(
            [
                jnp.where(core == 0, gain_parts[at], gain_parts[at + 1])
                for at in (0, 4, 2, 6)
            ],
            axis=0,
        )
        return grad_in, gain_sums, (*rest, grad_gate, grad_up, grad_down)

    own_tokens = lax.dynamic_index_in_dim(tokens[0], core, 0, keepdims=False)
    own_cotangent = lax.dynamic_index_in_dim(cotangent[0], core, 0, keepdims=False)
    out0, kept0 = forward(0, own_tokens.astype(f32))
    out1, kept1 = forward(1, out0.astype(f32))

    def swapped(zero, one):
        got = lax.ppermute(jnp.where(core == 0, one, zero), "section", SWAP)
        return jnp.where(core == 0, zero, got), jnp.where(core == 0, got, one)

    grad1, sums1, outputs = backward(1, own_cotangent, kept1, None, swapped(out0, out1))
    grad0, gain_sums, weight_grads = backward(0, grad1, kept0, sums1, None)
    outputs = jnp.stack(outputs)[None, None]
    input_grads = jnp.stack(swapped(grad0, grad1))[None, None]
    grad_query, grad_key, grad_value, grad_output, grad_gate, grad_up, grad_down = weight_grads
    return (
        outputs,
        input_grads,
        gain_sums[:, 0][None],
        grad_query[None],
        grad_key[None],
        grad_value[None],
        grad_output[None],
        gain_sums[:, 1][None],
        grad_gate[None],
        grad_up[None],
        grad_down[None],
    )


def solution(mesh):
    in_specs = (
        P("rep", None, "fsdp", None),
        P("rep", None, "fsdp"),
        P("rep", None, "fsdp", None),
        P("section", "fsdp"),
        P("section", "fsdp", None),
        P("section", "fsdp", None),
        P("section", "fsdp", None),
        P("section", "fsdp", None),
        P("section", "fsdp"),
        P("section", "fsdp", None),
        P("section", "fsdp", None),
        P("section", "fsdp", None),
    )
    out_specs = (
        P("section", "rep", None, "fsdp", None),
        P("section", "rep", None, "fsdp", None),
        P("section", "fsdp"),
        P("section", "fsdp", None),
        P("section", "fsdp", None),
        P("section", "fsdp", None),
        P("section", "fsdp", None),
        P("section", "fsdp"),
        P("section", "fsdp", None),
        P("section", "fsdp", None),
        P("section", "fsdp", None),
    )
    return jax.shard_map(shards, mesh=mesh, in_specs=in_specs, out_specs=out_specs, check_vma=False)
```

```python
import functools

import jax
import jax.numpy as jnp
from jax import lax
from jax.experimental import pallas as pl
from jax.experimental.pallas import tpu as pltpu
from jax.sharding import PartitionSpec as P

HQ = 32
KVH = 8
HD = 64
FF = 8192

epsilon = 1e-05
rope_base = 500000.0
masked_score = -1e30
bf16 = jnp.bfloat16
f32 = jnp.float32
SWAP = [(0, 1), (1, 0)]


def partner(value, bit):
    count = lax.axis_size("rep")
    return lax.ppermute(value, "rep", [(i, i ^ bit) for i in range(count)])


def bit_list(count):
    found = []
    bit = 1
    while bit < count:
        found.append(bit)
        bit *= 2
    return found


def gather_start(own):
    half = own.shape[0] // 2
    return own[None, :half], own[None, half:]


def gather_step(state, at):
    bits = bit_list(lax.axis_size("rep"))
    first, second = state
    first = jnp.concatenate([first, partner(first, bits[at])], axis=0)
    other = partner(second, bits[-1 - at])
    second = jnp.stack([second, other], axis=1).reshape((-1,) + second.shape[1:])
    return first, second


def gather_pair(state, at):
    for step in range(at, len(bit_list(lax.axis_size("rep")))):
        state = gather_step(state, step)
    return list(state)


def gather_rest(state, at):
    return jnp.stack(gather_pair(state, at))


def plane_gather(own):
    return gather_rest(gather_start(own), 0)


def plane_reduce(parts):
    bits = bit_list(lax.axis_size("rep"))
    first, second = parts[0], parts[1]
    for bit in bits[::-1]:
        keep, away = first[:bit], first[bit:]
        first = keep.astype(f32) + partner(away.astype(bf16), bit).astype(f32)
    for bit in bits:
        pair = second.reshape((-1, 2) + second.shape[1:])
        keep, away = pair[:, 0], pair[:, 1]
        second = keep.astype(f32) + partner(away.astype(bf16), bit).astype(f32)
    return jnp.concatenate([first[0], second[0]], axis=0)


def rope_tables(positions):
    half_size = HD // 2
    frequency = rope_base ** (-(jnp.arange(half_size).astype(f32) * 2.0) / HD)
    angles = positions[..., None] * frequency
    cosine, sine = jnp.cos(angles), jnp.sin(angles)
    return (
        jnp.concatenate([cosine] * 4, axis=-1),
        jnp.concatenate([-sine, sine] * 2, axis=-1),
    )


def times(left, weight):
    return jnp.dot(left, weight, preferred_element_type=f32)


def times_back(left, weight):
    return lax.dot_general(
        left, weight, (((1,), (1,)), ((), ())), preferred_element_type=f32
    )


def scale_of(values):
    return lax.rsqrt(jnp.mean(values * values, axis=-1, keepdims=True) + epsilon)


def norm_back(grad, gain, unit, scale):
    scaled = gain * grad
    out = scale * (scaled - unit * jnp.mean(scaled * unit, axis=-1, keepdims=True))
    return (out, jnp.sum(grad * unit, axis=0))


def sequence(ref):
    return ref[:, 0].reshape(-1, ref.shape[-1])


def scaled(value):
    return (value.astype(f32) * HD ** (-0.5)).astype(bf16)


def dot(left, right, left_dim, right_dim):
    return lax.dot_general(
        left, right, (((left_dim,), (right_dim,)), ((), ())), preferred_element_type=f32
    )


def attend_kernel(depth, query_ref, bias_ref, *refs):
    mixed_ref, log_ref = refs[depth:]
    keyval = jnp.concatenate([sequence(ref) for ref in refs[:depth]], axis=0)
    query = scaled(sequence(query_ref))
    bias = bias_ref[0].astype(f32)
    k_width = keyval.shape[1] // 2
    heads = query.shape[1] // HD
    group = heads // (k_width // HD)
    columns = []
    for head in range(heads):
        at = head // group * HD
        key = keyval[:, at : at + HD]
        value = keyval[:, k_width + at : k_width + at + HD]
        scores = dot(key, query[:, head * HD : (head + 1) * HD], 1, 1) + bias
        row_max = jnp.max(scores, axis=0, keepdims=True)
        weights = jnp.exp(scores - row_max)
        total = jnp.sum(weights, axis=0, keepdims=True)
        probs = (weights * (1.0 / total)).astype(bf16)
        columns.append(dot(value, probs, 0, 0))
        log_ref[0, head : head + 1, :] = row_max + jnp.log(total)
    mixed = jnp.concatenate(columns, axis=0).T.astype(bf16)
    mixed_ref[:, 0] = mixed.reshape(2, -1, mixed.shape[1])


def attend_back_kernel(depth, query_ref, grad_ref, log_ref, bias_ref, *refs):
    grad_query_ref, grad_refs = refs[depth], refs[depth + 1 :]
    keyval = jnp.concatenate([sequence(ref) for ref in refs[:depth]], axis=0)
    query = scaled(sequence(query_ref))
    grad = sequence(grad_ref)
    bias = bias_ref[0].astype(f32)
    k_width = keyval.shape[1] // 2
    heads = query.shape[1] // HD
    group = heads // (k_width // HD)
    columns, grad_keys, grad_values = [], [], []
    for head in range(heads):
        at = head // group * HD
        key = keyval[:, at : at + HD]
        value = keyval[:, k_width + at : k_width + at + HD]
        own_query = query[:, head * HD : (head + 1) * HD]
        own_grad = grad[:, head * HD : (head + 1) * HD]
        scores = dot(key, own_query, 1, 1) + bias
        probs = jnp.exp(scores - log_ref[0, head : head + 1, :])
        grad_probs = dot(value, own_grad, 1, 1)
        inner = jnp.sum(probs * grad_probs, axis=0, keepdims=True)
        grad_scores = (probs * (grad_probs - inner)).astype(bf16)
        columns.append(dot(key, grad_scores, 0, 0))
        grad_key = dot(grad_scores, own_query, 1, 0)
        grad_value = dot(probs.astype(bf16), own_grad, 1, 0)
        if head % group == 0:
            grad_keys.append(grad_key)
            grad_values.append(grad_value)
        else:
            grad_keys[-1] = grad_keys[-1] + grad_key
            grad_values[-1] = grad_values[-1] + grad_value
    grad_query = jnp.concatenate(columns, axis=0).T * HD ** (-0.5)
    grad_query_ref[:, 0] = grad_query.reshape(2, -1, grad_query.shape[1])
    both = jnp.concatenate(grad_keys + grad_values, axis=1).astype(bf16)
    rows = both.shape[0] // depth
    for step, ref in enumerate(grad_refs):
        part = both[step * rows : (step + 1) * rows]
        ref[:, 0] = part.reshape(2, rows // 2, part.shape[1])


def sequence_spec(array):
    two, _, half, columns = array.shape
    return pl.BlockSpec((two, 1, half, columns), lambda j: (0, j, 0, 0))


def row_spec(array):
    return pl.BlockSpec((1,) + array.shape[1:], lambda j: (j, 0, 0))


def attend(query, keyvals, bias):
    two, reps, half, width = query.shape
    logs = jax.ShapeDtypeStruct((reps, width // HD, two * half), f32)
    cells = reps * width * two * half * bias.shape[1]
    return pl.pallas_call(
        functools.partial(attend_kernel, len(keyvals)),
        grid=(reps,),
        in_specs=[sequence_spec(query), row_spec(bias)] + [sequence_spec(v) for v in keyvals],
        out_specs=[sequence_spec(query), row_spec(logs)],
        out_shape=[jax.ShapeDtypeStruct(query.shape, bf16), logs],
        compiler_params=pltpu.CompilerParams(vmem_limit_bytes=48 << 20),
        cost_estimate=pl.CostEstimate(
            flops=16 * cells, bytes_accessed=8 << 20, transcendentals=cells // HD
        ),
        name="attend",
    )(query, bias, *keyvals)


def attend_back(query, keyvals, grad_mixed, log_total, bias):
    two, reps, half, width = query.shape
    cells = reps * width * two * half * bias.shape[1]
    outs = pl.pallas_call(
        functools.partial(attend_back_kernel, len(keyvals)),
        grid=(reps,),
        in_specs=[sequence_spec(query), sequence_spec(grad_mixed), row_spec(log_total)]
        + [row_spec(bias)]
        + [sequence_spec(v) for v in keyvals],
        out_specs=[sequence_spec(query)] + [sequence_spec(v) for v in keyvals],
        out_shape=[jax.ShapeDtypeStruct(query.shape, f32)]
        + [jax.ShapeDtypeStruct(v.shape, bf16) for v in keyvals],
        compiler_params=pltpu.CompilerParams(vmem_limit_bytes=48 << 20),
        cost_estimate=pl.CostEstimate(
            flops=40 * cells, bytes_accessed=12 << 20, transcendentals=cells // HD
        ),
        name="attend_back",
    )(query, grad_mixed, log_total, bias, *keyvals)
    return outs[0], outs[1:]


def turned_pair(value):
    lane = lax.broadcasted_iota(jnp.int32, value.shape, 1)
    half = HD // 2
    ahead = pltpu.roll(value, value.shape[1] - half, 1)
    behind = pltpu.roll(value, half, 1)
    return jnp.where(lane % HD < half, ahead, behind)


def widened(table, width):
    return jnp.concatenate([table] * (width // table.shape[1]), axis=1)


def rows_of(ref):
    return ref[0].reshape(-1, ref.shape[-1])


def project_kernel(k_width, a_ref, weight_ref, cosine_ref, sine_ref, query_ref, keyval_ref):
    mixed = dot(rows_of(a_ref), weight_ref[...], 1, 0)
    width = mixed.shape[1]
    cosine = widened(rows_of(cosine_ref), width)
    sine = widened(rows_of(sine_ref), width)
    rotated = mixed * cosine + turned_pair(mixed) * sine
    lane = lax.broadcasted_iota(jnp.int32, mixed.shape, 1)
    rotated = jnp.where(lane < width - k_width, rotated, mixed).astype(bf16)
    q_width = query_ref.shape[-1]
    query_ref[0] = rotated[:, :q_width].reshape(query_ref.shape[1:])
    keyval_ref[0] = rotated[:, q_width:].reshape(keyval_ref.shape[1:])


def project_back_kernel(k_width, grad_ref, weight_ref, cosine_ref, sine_ref, *refs):
    parts, (joined_ref, out_ref) = refs[:-2], refs[-2:]
    keyval = rows_of(parts[0]).astype(f32)
    for part in parts[1:]:
        keyval = keyval + rows_of(part).astype(f32)
    joined = jnp.concatenate([rows_of(grad_ref), keyval], axis=1)
    width = joined.shape[1]
    cosine = widened(rows_of(cosine_ref), width)
    sine = widened(rows_of(sine_ref), width)
    rotated = joined * cosine - turned_pair(joined) * sine
    lane = lax.broadcasted_iota(jnp.int32, joined.shape, 1)
    rotated = jnp.where(lane < width - k_width, rotated, joined).astype(bf16)
    joined_ref[0] = rotated.reshape(joined_ref.shape[1:])
    out = dot(rotated, weight_ref[...], 1, 1).astype(bf16)
    out_ref[0] = out.reshape(out_ref.shape[1:])


def half_spec(array):
    return pl.BlockSpec((1,) + array.shape[1:], lambda i: (i, 0, 0, 0))


def all_spec(array):
    return pl.BlockSpec(array.shape, lambda i: (0, 0))


def project(a_all, weight, cosine, sine, q_width, k_width):
    shape = a_all.shape[:3]
    outs = [
        jax.ShapeDtypeStruct(shape + (q_width,), bf16),
        jax.ShapeDtypeStruct(shape + (2 * k_width,), bf16),
    ]
    cells = a_all.size * weight.shape[1]
    return pl.pallas_call(
        functools.partial(project_kernel, k_width),
        grid=(2,),
        in_specs=[half_spec(a_all), all_spec(weight), half_spec(cosine), half_spec(sine)],
        out_specs=[half_spec(v) for v in outs],
        out_shape=outs,
        compiler_params=pltpu.CompilerParams(vmem_limit_bytes=40 << 20),
        cost_estimate=pl.CostEstimate(
            flops=2 * cells, bytes_accessed=10 << 20, transcendentals=0
        ),
        name="project",
    )(a_all, weight, cosine, sine)


def project_back(grad_query, parts, weight, cosine, sine, k_width):
    shape = grad_query.shape[:3]
    outs = [
        jax.ShapeDtypeStruct(shape + (weight.shape[1],), bf16),
        jax.ShapeDtypeStruct(shape + (weight.shape[0],), bf16),
    ]
    cells = outs[0].size * weight.shape[0]
    return pl.pallas_call(
        functools.partial(project_back_kernel, k_width),
        grid=(2,),
        in_specs=[half_spec(grad_query), all_spec(weight), half_spec(cosine), half_spec(sine)]
        + [half_spec(v) for v in parts],
        out_specs=[half_spec(v) for v in outs],
        out_shape=outs,
        compiler_params=pltpu.CompilerParams(vmem_limit_bytes=48 << 20),
        cost_estimate=pl.CostEstimate(
            flops=2 * cells, bytes_accessed=14 << 20, transcendentals=0
        ),
        name="project_back",
    )(grad_query, weight, cosine, sine, *parts)


def by_place(info, refs, write):
    which = info[0] + 2 * pl.program_id(0) + 4 * pl.program_id(1)
    for at, ref in enumerate(refs):
        pl.when(which == at)(functools.partial(write, ref))


def columns_kernel(piece, info, *refs):
    out_ref = refs[8]
    reps, _, taken = refs[0].shape

    def write(ref):
        for at in range(taken // piece):
            for rep in range(reps):
                start = (at * reps + rep) * piece
                found = ref[rep ^ info[1], :, at * piece : (at + 1) * piece]
                out_ref[:, start : start + piece] = found.astype(f32)

    by_place(info, refs[:8], write)


def rows_kernel(info, *refs):
    out_ref = refs[8]

    def write(ref):
        for rep in range(out_ref.shape[0]):
            out_ref[rep, 0] = ref[rep ^ info[1]].astype(f32)

    by_place(info, refs[:8], write)


def rest_kernel(proj_width, info, *refs):
    outs, output_ref = refs[8:11], refs[11]
    reps, rows, width = refs[0].shape
    height, piece = output_ref.shape[2], width - proj_width

    def write(ref):
        for rep in range(reps):
            block = ref[rep ^ info[1]].astype(f32)
            start = 0
            for out_ref in outs:
                size = out_ref.shape[1] // reps
                out_ref[:, rep * size : (rep + 1) * size] = block[:, start : start + size]
                start += size
            for at in range(rows // height):
                part = block[at * height : (at + 1) * height, proj_width:]
                output_ref[rep, 0, :, at * piece : (at + 1) * piece] = part

    by_place(info, refs[:8], write)


def assembled(kernel, grid, block, index, out_blocks, out_index, out_shapes, info, eight):
    def chosen(at):
        def where_from(*steps):
            taken = steps[-1][0] + 2 * steps[0] + 4 * steps[1] == at
            return tuple(jnp.where(taken, v, 0) for v in index(at % 2, *steps))

        return where_from

    return pl.pallas_call(
        kernel,
        grid_spec=pltpu.PrefetchScalarGridSpec(
            num_scalar_prefetch=1,
            grid=grid,
            in_specs=[pl.BlockSpec(block, chosen(at)) for at in range(8)],
            out_specs=[pl.BlockSpec(b, f) for b, f in zip(out_blocks, out_index)],
        ),
        out_shape=[jax.ShapeDtypeStruct(v, f32) for v in out_shapes],
        compiler_params=pltpu.CompilerParams(vmem_limit_bytes=56 << 20),
        name="assemble",
    )(info, *eight)


def assemble_columns(info, eight, offsets, piece, pieces):
    reps, rows, _ = eight[0].shape
    step = 2 if pieces % 2 == 0 else 1
    return assembled(
        functools.partial(columns_kernel, piece),
        (2, 2, pieces // step),
        (reps, rows, step * piece),
        lambda layer, k, sub, at, info: (0, 0, offsets[layer] // step + at),
        [(rows, step * reps * piece)],
        [lambda k, sub, at, info: (2 * k + sub, at)],
        [(4 * rows, reps * piece * pieces)],
        info,
        eight,
    )[0]


def assemble_rows(info, eight):
    reps, rows, columns = eight[0].shape
    return assembled(
        rows_kernel,
        (2, 2),
        (reps, rows, columns),
        lambda layer, k, sub, info: (0, 0, 0),
        [(reps, 1, rows, columns)],
        [lambda k, sub, info: (0, 2 * k + sub, 0, 0)],
        [(reps, 4, rows, columns)],
        info,
        eight,
    )[0].reshape(-1, columns)


def assemble_rest(info, eight, sizes, proj_width, height, width):
    reps, rows, columns = eight[0].shape
    outs = assembled(
        functools.partial(rest_kernel, proj_width),
        (2, 2),
        (reps, rows, columns),
        lambda layer, k, sub, info: (0, 0, 0),
        [(rows, reps * size) for size in sizes] + [(reps, 1, height, width // 2)],
        [lambda k, sub, info: (2 * k + sub, 0)] * len(sizes)
        + [lambda k, sub, info: (0, k, 0, sub)],
        [(4 * rows, reps * size) for size in sizes] + [(reps, 2, height, width)],
        info,
        eight,
    )
    return (*outs[:-1], outs[-1].reshape(-1, width))


def together(*values):
    return lax.optimization_barrier(values)


def shards(
    tokens,
    segment_ids,
    cotangent,
    norm_attn,
    w_query,
    w_key,
    w_value,
    w_output,
    norm_ffn,
    w_gate,
    w_up,
    w_down,
):
    core = lax.axis_index("section")
    layer_z = lax.axis_index("fsdp")
    rep = lax.axis_index("rep")
    depth = lax.axis_size("fsdp")
    reps = lax.axis_size("rep")
    rows, width = tokens.shape[2:]
    half = rows // 2
    count = reps * rows
    q_width = HQ * HD // reps
    k_width = KVH * HD // reps
    ff_width = FF // reps
    ff_piece = FF // (reps * depth)

    def back(value, step):
        return lax.ppermute(value, "fsdp", [(i, i + step) for i in range(depth - step)])

    def by_layer(own, got):
        return (jnp.where(core == 0, own, got), jnp.where(core == 0, got, own))

    own_gain = jnp.concatenate([norm_attn, norm_ffn], axis=0)
    turned = jnp.stack(
        [own_gain]
        + [
            lax.ppermute(own_gain, "fsdp", [(i, (i + s) % depth) for i in range(depth)])
            for s in range(1, depth)
        ]
    )
    own_gain = jnp.concatenate(
        [
            lax.dynamic_index_in_dim(turned, (layer_z - k + depth) % depth, 0, keepdims=False)
            for k in range(depth)
        ],
        axis=1,
    ).astype(f32)
    gains = by_layer(own_gain, lax.ppermute(own_gain, "section", SWAP))

    plane_ids = lax.dynamic_index_in_dim(segment_ids[0], core, 0, keepdims=True)
    for bit in bit_list(reps):
        plane_ids = jnp.concatenate([plane_ids, partner(plane_ids, bit)], axis=0)
    ids = [plane_ids] + [back(plane_ids, step) for step in range(1, depth)]

    def split(cut, total):
        size = total // 2
        got = lax.ppermute(cut((1 - core) * size, size), "section", SWAP)
        return by_layer(cut(core * size, size), got)

    def spread(pieces):
        return [lax.all_gather(v, ("fsdp", "section"), axis=0, tiled=True) for v in pieces]

    def qkv_cut(row, size):
        parts = ((w_query, q_width), (w_key, k_width), (w_value, k_width))
        return jnp.concatenate(
            [lax.dynamic_slice(w[0], (row, rep * n), (size, n)) for w, n in parts], axis=1
        )

    def ffn_cut(row, size):
        return jnp.concatenate(
            [
                lax.dynamic_slice(
                    w[0], (row, k * reps * ff_piece + rep * ff_piece), (size, ff_piece)
                )
                for w in (w_gate, w_up)
                for k in range(depth)
            ],
            axis=1,
        )

    out_rows = w_output.shape[1] // reps

    def attn_cut(row, size):
        height = out_rows * size // w_query.shape[1]
        first = rep * out_rows + row * out_rows // w_query.shape[1]
        out = lax.dynamic_slice_in_dim(w_output[0], first, height)
        return jnp.concatenate([qkv_cut(row, size), out.reshape(size, -1)], axis=1)

    def all_ffn_cut(row, size):
        height = ff_piece * size // w_gate.shape[1]
        first = rep * ff_piece + row * ff_piece // w_gate.shape[1]
        down = lax.dynamic_slice_in_dim(w_down[0], first, height)
        return jnp.concatenate([ffn_cut(row, size), down.reshape(size, -1)], axis=1)

    attn_all = spread(split(attn_cut, w_query.shape[1]))
    qkv_width = q_width + 2 * k_width
    qkv_all = [v[:, :qkv_width] for v in attn_all]
    out_all = [
        lax.all_to_all(v[:, qkv_width:].reshape(-1, width), "rep", 0, 0, tiled=True)
        for v in attn_all
    ]
    both_all = spread(split(all_ffn_cut, w_gate.shape[1]))
    ffn_all = [v[:, : 2 * ff_width] for v in both_all]
    down_all = [v[:, 2 * ff_width :].reshape(ff_width, width) for v in both_all]

    starts = jnp.zeros((reps, rows), jnp.int32)
    biases = []
    within = jnp.arange(rows)
    for step in range(depth):
        key_ids, here = ids[step][:, :, None], plane_ids[:, None, :]
        exists = layer_z >= step
        starts = starts + jnp.sum((exists & (key_ids < here)).astype(jnp.int32), axis=1)
        allowed = exists & (key_ids == here)
        if step == 0:
            allowed = allowed & (within[:, None] <= within[None, :])
        biases.append(jnp.where(allowed, 0.0, masked_score).astype(bf16))
    bias = jnp.concatenate(biases, axis=1)
    cosine, sine = rope_tables((layer_z * rows + within - starts).astype(f32))

    def by_half(table):
        return table.reshape(reps, 2, half, 2 * HD).transpose(1, 0, 2, 3)

    cosine, sine = by_half(cosine), by_half(sine)

    def flat(value):
        return value.reshape(count, -1)

    def blocks(value):
        return value.reshape(2, reps, half, -1)

    def forward(layer, layer_in):
        gain_attn, gain_ffn = gains[layer][0], gains[layer][1]
        scale_in = scale_of(layer_in)
        a_all = plane_gather((layer_in * scale_in * gain_attn).astype(bf16))
        query, keyval = project(a_all, qkv_all[layer], cosine, sine, q_width, k_width)
        keyvals = [keyval] + [
            back(keyval, step) for step in range(1, depth)
        ]
        mixed, log_total = attend(query, keyvals, bias)
        residual = layer_in + plane_reduce(blocks(times(flat(mixed), out_all[layer]).astype(bf16)))
        scale_mid = scale_of(residual)
        b_all = plane_gather((residual * scale_mid * gain_ffn).astype(bf16))
        pre = times(flat(b_all), ffn_all[layer]).astype(bf16)
        gate, up = pre[:, :ff_width], pre[:, ff_width:]
        hidden = (jax.nn.silu(gate.astype(f32)) * up.astype(f32)).astype(bf16)
        out = residual + plane_reduce(blocks(times(hidden, down_all[layer]).astype(bf16)))
        kept = (layer_in, scale_in, a_all, query, keyvals, mixed, log_total)
        return out.astype(bf16), kept + (residual, scale_mid, b_all, gate, up, hidden)

    def core_product(left, right, extra=None):
        size = left.shape[1] // (2 * depth)

        def half_of(value, which):
            return jnp.concatenate(
                [
                    lax.dynamic_slice_in_dim(value, (2 * k + which) * size, size, axis=1)
                    for k in range(depth)
                ],
                axis=1,
            )

        def product(which, right):
            found = dot(half_of(left, which), right, 0, 0)
            if extra is None:
                return found
            more = half_of(extra, which).T
            more = jnp.pad(more, ((0, 0), (0, 128 - more.shape[1])))
            return jnp.concatenate([found, more], axis=1)

        def finish(right, sent):
            got = lax.ppermute(sent, "section", SWAP)
            return (product(core, right) + got.astype(f32)).astype(bf16)

        return product(1 - core, right).astype(bf16), finish

    info = jnp.stack([core, rep]).astype(jnp.int32)

    def collect(total):
        return lax.psum_scatter(total, "fsdp", scatter_dimension=0, tiled=True)

    def backward(layer, grad_out, kept, earlier, ready):
        (layer_in, scale_in, a_all, query, keyvals, mixed, log_total) = kept[:7]
        (residual, scale_mid, b_all, gate, up, hidden) = kept[7:]
        gain_attn, gain_ffn = gains[layer][0], gains[layer][1]
        last = earlier is not None
        if last:
            old_rest, old_gate, old_up, old_down = earlier
            tall = old_up.shape[0]

            state = gather_step(gather_start(grad_out), 0)
            *state, old_gate, old_up = together(*state, old_gate, old_up)
            old_ffn = jnp.concatenate([old_gate, old_up], axis=1)
            gm_all = flat(gather_rest(state, 1))
            sent_down, finish = core_product(hidden, gm_all)
            gm_all, sent_down, old_ffn = together(gm_all, sent_down, old_ffn)
            ffn_state = gather_step(gather_start(old_ffn), 0)
        else:
            gm_all = flat(plane_gather(grad_out))
            sent_down, finish = core_product(hidden, gm_all)
            gm_all, sent_down, *ready = together(gm_all, sent_down, *ready)
        grad_hidden = times_back(gm_all, down_all[layer])
        gate, up = gate.astype(f32), up.astype(f32)
        sig = jax.nn.sigmoid(gate)
        grad_gate = (grad_hidden * up * (sig * (1.0 + gate * (1.0 - sig)))).astype(bf16)
        grad_up = (grad_hidden * (gate * sig)).astype(bf16)
        grad_pre = jnp.concatenate([grad_gate, grad_up], axis=1)
        part_down = finish(gm_all, sent_down)
        if last:
            grad_pre, *ffn_state = together(grad_pre, *ffn_state)
        own_down = collect(part_down)
        db = blocks(times_back(grad_pre, ffn_all[layer]).astype(bf16))
        db, grad_gate, grad_up = together(db, grad_gate, grad_up)
        db = plane_reduce(db)
        sent_gate, finish_gate = core_product(flat(b_all), grad_gate)
        sent_up, finish_up = core_product(flat(b_all), grad_up)
        unit = residual * scale_mid
        grad_mid, gain_grad_ffn = norm_back(db, gain_ffn, unit, scale_mid)
        grad_mid = grad_mid + grad_out.astype(f32)
        go = grad_mid.astype(bf16)
        if last:
            go, old_rest = together(go, old_rest)
        go_all = flat(plane_gather(go))
        go_all, part_gate, part_up = together(
            go_all, finish_gate(grad_gate, sent_gate), finish_up(grad_up, sent_up)
        )
        own_gate, own_up = collect(part_gate), collect(part_up)
        grad_mixed = blocks(times_back(go_all, out_all[layer]).astype(bf16))
        def output_part(go_all):
            sent_o, finish_o = core_product(flat(mixed), go_all)
            return lax.all_to_all(finish_o(go_all, sent_o), "rep", 0, 0, tiled=True)

        if last:
            grad_mixed, old_rest, *ffn_state = together(grad_mixed, old_rest, *ffn_state)
            ffn_state = gather_step(ffn_state, 1)
            rest_state = gather_step(gather_start(old_rest), 0)
            part_o = output_part(go_all)
        else:
            grad_mixed, own_down = together(grad_mixed, own_down)
            own_down = gather_pair(gather_start(own_down), 0)
        grad_query, grad_kv = attend_back(query, keyvals, grad_mixed, log_total, bias)
        if last:
            grad_query, part_o, own_down, *grad_kv = together(
                grad_query, part_o, own_down, *grad_kv
            )
            own_down = gather_pair(gather_start(own_down), 0)
        else:
            grad_query, go_all, *grad_kv = together(grad_query, go_all, *grad_kv)
        grad_kv = [grad_kv[0]] + [
            lax.ppermute(grad_kv[step], "fsdp", [(i, i - step) for i in range(step, depth)])
            for step in range(1, depth)
        ]
        if not last:
            part_o = output_part(go_all)
        grad_qkv, da = project_back(grad_query, grad_kv, qkv_all[layer], cosine, sine, k_width)
        grad_qkv = flat(grad_qkv)

        def input_side(da):
            unit = layer_in * scale_in
            grad_in, gain_grad_attn = norm_back(da, gain_attn, unit, scale_in)
            grad_in = (grad_in + grad_mid).astype(bf16)
            gain_grads = jnp.stack([gain_grad_attn, gain_grad_ffn])
            sent_proj, finish = core_product(flat(a_all), grad_qkv, gain_grads)
            part_proj = finish(grad_qkv, sent_proj)
            pieces = part_proj.shape[0] // part_o.shape[0]
            aside = part_o.reshape(depth, -1, pieces, width // pieces).transpose(0, 2, 1, 3)
            aside = aside.reshape(part_proj.shape[0], -1)
            return grad_in, jnp.concatenate([part_proj, aside], axis=1)

        if not last:
            da, grad_qkv, part_o, own_gate, *own_down = together(
                da, grad_qkv, part_o, own_gate, *own_down
            )
            grad_in, part_rest = input_side(plane_reduce(da))
            return grad_in, (collect(part_rest), own_gate, own_up, own_down), ready

        def send(pair):
            return [lax.ppermute(v, "section", [(0, 1)]) for v in pair]

        def eight(zero, one, one_sent):
            found = []
            for sub in range(2):
                got = lax.ppermute(zero[sub], "section", [(1, 0)])
                found += [zero[sub], one_sent[sub], got, one[sub]]
            return found

        da, *states = together(da, *own_down, *ffn_state, *rest_state)
        zero_down = states[:2]
        old_ffn, old_rest = gather_pair(states[2:4], 2), gather_pair(states[4:], 1)
        olds_sent = send(old_ffn) + send(old_down)
        da, own_gate = together(plane_reduce(da), own_gate)
        grad_in, part_rest = input_side(da)
        gate_state = gather_step(gather_start(own_gate), 0)
        own_rest = collect(part_rest)
        own_up, *tied = together(own_up, *gate_state, *olds_sent, *old_rest)
        gate_state, olds_sent, old_rest = tied[:2], tied[2:6], tied[6:]
        ffn_sent, down_sent = olds_sent[:2], olds_sent[2:]
        rest_sent = send(old_rest)
        zero_gate = gather_pair(gate_state, 1)
        up_state = gather_step(gather_start(own_up), 0)
        tied = together(*zero_gate, *up_state, *rest_sent)
        zero_gate, up_state, rest_sent = tied[:2], tied[2:4], tied[4:]
        zero_up = gather_pair(up_state, 1)
        places = eight(zero_gate, old_ffn, ffn_sent)
        grad_gate = assemble_columns(info, places, (0, 0), ff_piece, depth)
        grad_down = assemble_rows(info, eight(zero_down, old_down, down_sent))
        grad_gate, grad_down, own_rest, *zero_up = together(
            grad_gate, grad_down, own_rest, *zero_up
        )
        rest_state = gather_step(gather_start(own_rest), 0)
        places = eight(zero_up, old_ffn, ffn_sent)
        grad_up = assemble_columns(info, places, (0, depth), ff_piece, depth)
        grad_up, *rest_state = together(grad_up, *rest_state)
        zero_rest = gather_pair(rest_state, 1)
        height = out_rows // 2
        proj_width = own_rest.shape[1] - height * width // tall
        places = eight(zero_rest, old_rest, rest_sent)
        sizes = (q_width, k_width, k_width)
        rest = assemble_rest(info, places, sizes, proj_width, height, width)
        gain_parts = [
            jnp.sum(v[..., qkv_width : qkv_width + 2].astype(f32), axis=0) for v in places
        ]
        gain_sums = jnp.concatenate(
            [
                jnp.where(core == 0, gain_parts[at], gain_parts[at + 1])
                for at in (0, 4, 2, 6)
            ],
            axis=0,
        )
        return grad_in, gain_sums, (*rest, grad_gate, grad_up, grad_down)

    own_tokens = lax.dynamic_index_in_dim(tokens[0], core, 0, keepdims=False)
    own_cotangent = lax.dynamic_index_in_dim(cotangent[0], core, 0, keepdims=False)
    out0, kept0 = forward(0, own_tokens.astype(f32))
    out1, kept1 = forward(1, out0.astype(f32))

    def swapped(zero, one):
        got = lax.ppermute(jnp.where(core == 0, one, zero), "section", SWAP)
        return jnp.where(core == 0, zero, got), jnp.where(core == 0, got, one)

    grad1, sums1, outputs = backward(1, own_cotangent, kept1, None, swapped(out0, out1))
    grad0, gain_sums, weight_grads = backward(0, grad1, kept0, sums1, None)
    outputs = jnp.stack(outputs)[None, None]
    input_grads = jnp.stack(swapped(grad0, grad1))[None, None]
    grad_query, grad_key, grad_value, grad_output, grad_gate, grad_up, grad_down = weight_grads
    return (
        outputs,
        input_grads,
        gain_sums[:, 0][None],
        grad_query[None],
        grad_key[None],
        grad_value[None],
        grad_output[None],
        gain_sums[:, 1][None],
        grad_gate[None],
        grad_up[None],
        grad_down[None],
    )


def solution(mesh):
    in_specs = (
        P("rep", None, "fsdp", None),
        P("rep", None, "fsdp"),
        P("rep", None, "fsdp", None),
        P("section", "fsdp"),
        P("section", "fsdp", None),
        P("section", "fsdp", None),
        P("section", "fsdp", None),
        P("section", "fsdp", None),
        P("section", "fsdp"),
        P("section", "fsdp", None),
        P("section", "fsdp", None),
        P("section", "fsdp", None),
    )
    out_specs = (
        P("section", "rep", None, "fsdp", None),
        P("section", "rep", None, "fsdp", None),
        P("section", "fsdp"),
        P("section", "fsdp", None),
        P("section", "fsdp", None),
        P("section", "fsdp", None),
        P("section", "fsdp", None),
        P("section", "fsdp"),
        P("section", "fsdp", None),
        P("section", "fsdp", None),
        P("section", "fsdp", None),
    )
    return jax.shard_map(shards, mesh=mesh, in_specs=in_specs, out_specs=out_specs, check_vma=False)
```

```python
import functools

import jax
import jax.numpy as jnp
from jax import lax
from jax.experimental import pallas as pl
from jax.experimental.pallas import tpu as pltpu
from jax.sharding import PartitionSpec as P

HQ = 32
KVH = 8
HD = 64
FF = 8192

epsilon = 1e-05
rope_base = 500000.0
masked_score = -1e30
bf16 = jnp.bfloat16
f32 = jnp.float32
SWAP = [(0, 1), (1, 0)]


def partner(value, bit):
    count = lax.axis_size("rep")
    return lax.ppermute(value, "rep", [(i, i ^ bit) for i in range(count)])


def bit_list(count):
    found = []
    bit = 1
    while bit < count:
        found.append(bit)
        bit *= 2
    return found


def gather_start(own):
    half = own.shape[0] // 2
    return own[None, :half], own[None, half:]


def gather_step(state, at):
    bits = bit_list(lax.axis_size("rep"))
    first, second = state
    first = jnp.concatenate([first, partner(first, bits[at])], axis=0)
    other = partner(second, bits[-1 - at])
    second = jnp.stack([second, other], axis=1).reshape((-1,) + second.shape[1:])
    return first, second


def gather_pair(state, at):
    for step in range(at, len(bit_list(lax.axis_size("rep")))):
        state = gather_step(state, step)
    return list(state)


def gather_rest(state, at):
    return jnp.stack(gather_pair(state, at))


def plane_gather(own):
    return gather_rest(gather_start(own), 0)


def plane_reduce(parts):
    bits = bit_list(lax.axis_size("rep"))
    first, second = parts[0], parts[1]
    for bit in bits[::-1]:
        keep, away = first[:bit], first[bit:]
        first = keep.astype(f32) + partner(away.astype(bf16), bit).astype(f32)
    for bit in bits:
        pair = second.reshape((-1, 2) + second.shape[1:])
        keep, away = pair[:, 0], pair[:, 1]
        second = keep.astype(f32) + partner(away.astype(bf16), bit).astype(f32)
    return jnp.concatenate([first[0], second[0]], axis=0)


def rope_tables(positions):
    half_size = HD // 2
    frequency = rope_base ** (-(jnp.arange(half_size).astype(f32) * 2.0) / HD)
    angles = positions[..., None] * frequency
    cosine, sine = jnp.cos(angles), jnp.sin(angles)
    return (
        jnp.concatenate([cosine] * 4, axis=-1),
        jnp.concatenate([-sine, sine] * 2, axis=-1),
    )


def times(left, weight):
    return jnp.dot(left, weight, preferred_element_type=f32)


def times_back(left, weight):
    return lax.dot_general(
        left, weight, (((1,), (1,)), ((), ())), preferred_element_type=f32
    )


def scale_of(values):
    return lax.rsqrt(jnp.mean(values * values, axis=-1, keepdims=True) + epsilon)


def norm_back(grad, gain, unit, scale):
    scaled = gain * grad
    out = scale * (scaled - unit * jnp.mean(scaled * unit, axis=-1, keepdims=True))
    return (out, jnp.sum(grad * unit, axis=0))


def sequence(ref):
    return ref[:, 0].reshape(-1, ref.shape[-1])


def scaled(value):
    return (value.astype(f32) * HD ** (-0.5)).astype(bf16)


def dot(left, right, left_dim, right_dim):
    return lax.dot_general(
        left, right, (((left_dim,), (right_dim,)), ((), ())), preferred_element_type=f32
    )


def attend_kernel(depth, query_ref, bias_ref, *refs):
    mixed_ref, log_ref = refs[depth:]
    keyval = jnp.concatenate([sequence(ref) for ref in refs[:depth]], axis=0)
    query = scaled(sequence(query_ref))
    bias = bias_ref[0].astype(f32)
    k_width = keyval.shape[1] // 2
    heads = query.shape[1] // HD
    group = heads // (k_width // HD)
    columns = []
    for head in range(heads):
        at = head // group * HD
        key = keyval[:, at : at + HD]
        value = keyval[:, k_width + at : k_width + at + HD]
        scores = dot(key, query[:, head * HD : (head + 1) * HD], 1, 1) + bias
        row_max = jnp.max(scores, axis=0, keepdims=True)
        weights = jnp.exp(scores - row_max)
        total = jnp.sum(weights, axis=0, keepdims=True)
        probs = (weights * (1.0 / total)).astype(bf16)
        columns.append(dot(value, probs, 0, 0))
        log_ref[0, head : head + 1, :] = row_max + jnp.log(total)
    mixed = jnp.concatenate(columns, axis=0).T.astype(bf16)
    mixed_ref[:, 0] = mixed.reshape(2, -1, mixed.shape[1])


def attend_back_kernel(depth, query_ref, grad_ref, log_ref, bias_ref, *refs):
    grad_query_ref, grad_refs = refs[depth], refs[depth + 1 :]
    keyval = jnp.concatenate([sequence(ref) for ref in refs[:depth]], axis=0)
    query = scaled(sequence(query_ref))
    grad = sequence(grad_ref)
    bias = bias_ref[0].astype(f32)
    k_width = keyval.shape[1] // 2
    heads = query.shape[1] // HD
    group = heads // (k_width // HD)
    columns, grad_keys, grad_values = [], [], []
    for head in range(heads):
        at = head // group * HD
        key = keyval[:, at : at + HD]
        value = keyval[:, k_width + at : k_width + at + HD]
        own_query = query[:, head * HD : (head + 1) * HD]
        own_grad = grad[:, head * HD : (head + 1) * HD]
        scores = dot(key, own_query, 1, 1) + bias
        probs = jnp.exp(scores - log_ref[0, head : head + 1, :])
        grad_probs = dot(value, own_grad, 1, 1)
        inner = jnp.sum(probs * grad_probs, axis=0, keepdims=True)
        grad_scores = (probs * (grad_probs - inner)).astype(bf16)
        columns.append(dot(key, grad_scores, 0, 0))
        grad_key = dot(grad_scores, own_query, 1, 0)
        grad_value = dot(probs.astype(bf16), own_grad, 1, 0)
        if head % group == 0:
            grad_keys.append(grad_key)
            grad_values.append(grad_value)
        else:
            grad_keys[-1] = grad_keys[-1] + grad_key
            grad_values[-1] = grad_values[-1] + grad_value
    grad_query = jnp.concatenate(columns, axis=0).T * HD ** (-0.5)
    grad_query_ref[:, 0] = grad_query.reshape(2, -1, grad_query.shape[1])
    both = jnp.concatenate(grad_keys + grad_values, axis=1).astype(bf16)
    rows = both.shape[0] // depth
    for step, ref in enumerate(grad_refs):
        part = both[step * rows : (step + 1) * rows]
        ref[:, 0] = part.reshape(2, rows // 2, part.shape[1])


def sequence_spec(array):
    two, _, half, columns = array.shape
    return pl.BlockSpec((two, 1, half, columns), lambda j: (0, j, 0, 0))


def row_spec(array):
    return pl.BlockSpec((1,) + array.shape[1:], lambda j: (j, 0, 0))


def attend(query, keyvals, bias):
    two, reps, half, width = query.shape
    logs = jax.ShapeDtypeStruct((reps, width // HD, two * half), f32)
    cells = reps * width * two * half * bias.shape[1]
    return pl.pallas_call(
        functools.partial(attend_kernel, len(keyvals)),
        grid=(reps,),
        in_specs=[sequence_spec(query), row_spec(bias)] + [sequence_spec(v) for v in keyvals],
        out_specs=[sequence_spec(query), row_spec(logs)],
        out_shape=[jax.ShapeDtypeStruct(query.shape, bf16), logs],
        compiler_params=pltpu.CompilerParams(vmem_limit_bytes=48 << 20),
        cost_estimate=pl.CostEstimate(
            flops=16 * cells, bytes_accessed=8 << 20, transcendentals=cells // HD
        ),
        name="attend",
    )(query, bias, *keyvals)


def attend_back(query, keyvals, grad_mixed, log_total, bias):
    two, reps, half, width = query.shape
    cells = reps * width * two * half * bias.shape[1]
    outs = pl.pallas_call(
        functools.partial(attend_back_kernel, len(keyvals)),
        grid=(reps,),
        in_specs=[sequence_spec(query), sequence_spec(grad_mixed), row_spec(log_total)]
        + [row_spec(bias)]
        + [sequence_spec(v) for v in keyvals],
        out_specs=[sequence_spec(query)] + [sequence_spec(v) for v in keyvals],
        out_shape=[jax.ShapeDtypeStruct(query.shape, f32)]
        + [jax.ShapeDtypeStruct(v.shape, bf16) for v in keyvals],
        compiler_params=pltpu.CompilerParams(vmem_limit_bytes=48 << 20),
        cost_estimate=pl.CostEstimate(
            flops=40 * cells, bytes_accessed=12 << 20, transcendentals=cells // HD
        ),
        name="attend_back",
    )(query, grad_mixed, log_total, bias, *keyvals)
    return outs[0], outs[1:]


def turned_pair(value):
    lane = lax.broadcasted_iota(jnp.int32, value.shape, 1)
    half = HD // 2
    ahead = pltpu.roll(value, value.shape[1] - half, 1)
    behind = pltpu.roll(value, half, 1)
    return jnp.where(lane % HD < half, ahead, behind)


def widened(table, width):
    return jnp.concatenate([table] * (width // table.shape[1]), axis=1)


def rows_of(ref):
    return ref[0].reshape(-1, ref.shape[-1])


def project_kernel(k_width, a_ref, weight_ref, cosine_ref, sine_ref, query_ref, keyval_ref):
    mixed = dot(rows_of(a_ref), weight_ref[...], 1, 0)
    width = mixed.shape[1]
    cosine = widened(rows_of(cosine_ref), width)
    sine = widened(rows_of(sine_ref), width)
    rotated = mixed * cosine + turned_pair(mixed) * sine
    lane = lax.broadcasted_iota(jnp.int32, mixed.shape, 1)
    rotated = jnp.where(lane < width - k_width, rotated, mixed).astype(bf16)
    q_width = query_ref.shape[-1]
    query_ref[0] = rotated[:, :q_width].reshape(query_ref.shape[1:])
    keyval_ref[0] = rotated[:, q_width:].reshape(keyval_ref.shape[1:])


def project_back_kernel(k_width, grad_ref, weight_ref, cosine_ref, sine_ref, *refs):
    parts, (joined_ref, out_ref) = refs[:-2], refs[-2:]
    keyval = rows_of(parts[0]).astype(f32)
    for part in parts[1:]:
        keyval = keyval + rows_of(part).astype(f32)
    joined = jnp.concatenate([rows_of(grad_ref), keyval], axis=1)
    width = joined.shape[1]
    cosine = widened(rows_of(cosine_ref), width)
    sine = widened(rows_of(sine_ref), width)
    rotated = joined * cosine - turned_pair(joined) * sine
    lane = lax.broadcasted_iota(jnp.int32, joined.shape, 1)
    rotated = jnp.where(lane < width - k_width, rotated, joined).astype(bf16)
    joined_ref[0] = rotated.reshape(joined_ref.shape[1:])
    out = dot(rotated, weight_ref[...], 1, 1).astype(bf16)
    out_ref[0] = out.reshape(out_ref.shape[1:])


def half_spec(array):
    return pl.BlockSpec((1,) + array.shape[1:], lambda i: (i, 0, 0, 0))


def all_spec(array):
    return pl.BlockSpec(array.shape, lambda i: (0, 0))


def project(a_all, weight, cosine, sine, q_width, k_width):
    shape = a_all.shape[:3]
    outs = [
        jax.ShapeDtypeStruct(shape + (q_width,), bf16),
        jax.ShapeDtypeStruct(shape + (2 * k_width,), bf16),
    ]
    cells = a_all.size * weight.shape[1]
    return pl.pallas_call(
        functools.partial(project_kernel, k_width),
        grid=(2,),
        in_specs=[half_spec(a_all), all_spec(weight), half_spec(cosine), half_spec(sine)],
        out_specs=[half_spec(v) for v in outs],
        out_shape=outs,
        compiler_params=pltpu.CompilerParams(vmem_limit_bytes=40 << 20),
        cost_estimate=pl.CostEstimate(
            flops=2 * cells, bytes_accessed=10 << 20, transcendentals=0
        ),
        name="project",
    )(a_all, weight, cosine, sine)


def project_back(grad_query, parts, weight, cosine, sine, k_width):
    shape = grad_query.shape[:3]
    outs = [
        jax.ShapeDtypeStruct(shape + (weight.shape[1],), bf16),
        jax.ShapeDtypeStruct(shape + (weight.shape[0],), bf16),
    ]
    cells = outs[0].size * weight.shape[0]
    return pl.pallas_call(
        functools.partial(project_back_kernel, k_width),
        grid=(2,),
        in_specs=[half_spec(grad_query), all_spec(weight), half_spec(cosine), half_spec(sine)]
        + [half_spec(v) for v in parts],
        out_specs=[half_spec(v) for v in outs],
        out_shape=outs,
        compiler_params=pltpu.CompilerParams(vmem_limit_bytes=48 << 20),
        cost_estimate=pl.CostEstimate(
            flops=2 * cells, bytes_accessed=14 << 20, transcendentals=0
        ),
        name="project_back",
    )(grad_query, weight, cosine, sine, *parts)


def by_place(info, refs, write):
    which = info[0] + 2 * pl.program_id(0) + 4 * pl.program_id(1)
    for at, ref in enumerate(refs):
        pl.when(which == at)(functools.partial(write, ref))


def columns_kernel(piece, info, *refs):
    out_ref = refs[8]
    reps, _, taken = refs[0].shape

    def write(ref):
        for at in range(taken // piece):
            for rep in range(reps):
                start = (at * reps + rep) * piece
                found = ref[rep ^ info[1], :, at * piece : (at + 1) * piece]
                out_ref[:, start : start + piece] = found.astype(f32)

    by_place(info, refs[:8], write)


def rows_kernel(info, *refs):
    out_ref = refs[8]

    def write(ref):
        for rep in range(out_ref.shape[0]):
            out_ref[rep, 0] = ref[rep ^ info[1]].astype(f32)

    by_place(info, refs[:8], write)


def rest_kernel(proj_width, info, *refs):
    outs, output_ref = refs[8:11], refs[11]
    reps, rows, width = refs[0].shape
    height, piece = output_ref.shape[2], width - proj_width

    def write(ref):
        for rep in range(reps):
            block = ref[rep ^ info[1]].astype(f32)
            start = 0
            for out_ref in outs:
                size = out_ref.shape[1] // reps
                out_ref[:, rep * size : (rep + 1) * size] = block[:, start : start + size]
                start += size
            for at in range(rows // height):
                part = block[at * height : (at + 1) * height, proj_width:]
                output_ref[rep, 0, :, at * piece : (at + 1) * piece] = part

    by_place(info, refs[:8], write)


def assembled(kernel, grid, block, index, out_blocks, out_index, out_shapes, info, eight):
    def chosen(at):
        def where_from(*steps):
            taken = steps[-1][0] + 2 * steps[0] + 4 * steps[1] == at
            return tuple(jnp.where(taken, v, 0) for v in index(at % 2, *steps))

        return where_from

    return pl.pallas_call(
        kernel,
        grid_spec=pltpu.PrefetchScalarGridSpec(
            num_scalar_prefetch=1,
            grid=grid,
            in_specs=[pl.BlockSpec(block, chosen(at)) for at in range(8)],
            out_specs=[pl.BlockSpec(b, f) for b, f in zip(out_blocks, out_index)],
        ),
        out_shape=[jax.ShapeDtypeStruct(v, f32) for v in out_shapes],
        compiler_params=pltpu.CompilerParams(vmem_limit_bytes=56 << 20),
        name="assemble",
    )(info, *eight)


def assemble_columns(info, eight, offsets, piece, pieces):
    reps, rows, _ = eight[0].shape
    step = 2 if pieces % 2 == 0 else 1
    return assembled(
        functools.partial(columns_kernel, piece),
        (2, 2, pieces // step),
        (reps, rows, step * piece),
        lambda layer, k, sub, at, info: (0, 0, offsets[layer] // step + at),
        [(rows, step * reps * piece)],
        [lambda k, sub, at, info: (2 * k + sub, at)],
        [(4 * rows, reps * piece * pieces)],
        info,
        eight,
    )[0]


def assemble_rows(info, eight):
    reps, rows, columns = eight[0].shape
    return assembled(
        rows_kernel,
        (2, 2),
        (reps, rows, columns),
        lambda layer, k, sub, info: (0, 0, 0),
        [(reps, 1, rows, columns)],
        [lambda k, sub, info: (0, 2 * k + sub, 0, 0)],
        [(reps, 4, rows, columns)],
        info,
        eight,
    )[0].reshape(-1, columns)


def assemble_rest(info, eight, sizes, proj_width, height, width):
    reps, rows, columns = eight[0].shape
    outs = assembled(
        functools.partial(rest_kernel, proj_width),
        (2, 2),
        (reps, rows, columns),
        lambda layer, k, sub, info: (0, 0, 0),
        [(rows, reps * size) for size in sizes] + [(reps, 1, height, width // 2)],
        [lambda k, sub, info: (2 * k + sub, 0)] * len(sizes)
        + [lambda k, sub, info: (0, k, 0, sub)],
        [(4 * rows, reps * size) for size in sizes] + [(reps, 2, height, width)],
        info,
        eight,
    )
    return (*outs[:-1], outs[-1].reshape(-1, width))


def together(*values):
    return lax.optimization_barrier(values)


def shards(
    tokens,
    segment_ids,
    cotangent,
    norm_attn,
    w_query,
    w_key,
    w_value,
    w_output,
    norm_ffn,
    w_gate,
    w_up,
    w_down,
):
    core = lax.axis_index("section")
    layer_z = lax.axis_index("fsdp")
    rep = lax.axis_index("rep")
    depth = lax.axis_size("fsdp")
    reps = lax.axis_size("rep")
    rows, width = tokens.shape[2:]
    half = rows // 2
    count = reps * rows
    q_width = HQ * HD // reps
    k_width = KVH * HD // reps
    ff_width = FF // reps
    ff_piece = FF // (reps * depth)

    def back(value, step):
        return lax.ppermute(value, "fsdp", [(i, i + step) for i in range(depth - step)])

    def by_layer(own, got):
        return (jnp.where(core == 0, own, got), jnp.where(core == 0, got, own))

    own_gain = jnp.concatenate([norm_attn, norm_ffn], axis=0)
    turned = jnp.stack(
        [own_gain]
        + [
            lax.ppermute(own_gain, "fsdp", [(i, (i + s) % depth) for i in range(depth)])
            for s in range(1, depth)
        ]
    )
    own_gain = jnp.concatenate(
        [
            lax.dynamic_index_in_dim(turned, (layer_z - k + depth) % depth, 0, keepdims=False)
            for k in range(depth)
        ],
        axis=1,
    ).astype(f32)
    gains = by_layer(own_gain, lax.ppermute(own_gain, "section", SWAP))

    plane_ids = lax.dynamic_index_in_dim(segment_ids[0], core, 0, keepdims=True)
    for bit in bit_list(reps):
        plane_ids = jnp.concatenate([plane_ids, partner(plane_ids, bit)], axis=0)
    ids = [plane_ids] + [back(plane_ids, step) for step in range(1, depth)]

    def split(cut, total):
        size = total // 2
        got = lax.ppermute(cut((1 - core) * size, size), "section", SWAP)
        return by_layer(cut(core * size, size), got)

    def spread(pieces):
        return [lax.all_gather(v, ("fsdp", "section"), axis=0, tiled=True) for v in pieces]

    def qkv_cut(row, size):
        parts = ((w_query, q_width), (w_key, k_width), (w_value, k_width))
        return jnp.concatenate(
            [lax.dynamic_slice(w[0], (row, rep * n), (size, n)) for w, n in parts], axis=1
        )

    def ffn_cut(row, size):
        return jnp.concatenate(
            [
                lax.dynamic_slice(
                    w[0], (row, k * reps * ff_piece + rep * ff_piece), (size, ff_piece)
                )
                for w in (w_gate, w_up)
                for k in range(depth)
            ],
            axis=1,
        )

    out_rows = w_output.shape[1] // reps

    def attn_cut(row, size):
        height = out_rows * size // w_query.shape[1]
        first = rep * out_rows + row * out_rows // w_query.shape[1]
        out = lax.dynamic_slice_in_dim(w_output[0], first, height)
        return jnp.concatenate([qkv_cut(row, size), out.reshape(size, -1)], axis=1)

    def all_ffn_cut(row, size):
        height = ff_piece * size // w_gate.shape[1]
        first = rep * ff_piece + row * ff_piece // w_gate.shape[1]
        down = lax.dynamic_slice_in_dim(w_down[0], first, height)
        return jnp.concatenate([ffn_cut(row, size), down.reshape(size, -1)], axis=1)

    attn_all = spread(split(attn_cut, w_query.shape[1]))
    qkv_width = q_width + 2 * k_width
    qkv_all = [v[:, :qkv_width] for v in attn_all]
    out_all = [
        lax.all_to_all(v[:, qkv_width:].reshape(-1, width), "rep", 0, 0, tiled=True)
        for v in attn_all
    ]
    both_all = spread(split(all_ffn_cut, w_gate.shape[1]))
    ffn_all = [v[:, : 2 * ff_width] for v in both_all]
    down_all = [v[:, 2 * ff_width :].reshape(ff_width, width) for v in both_all]

    starts = jnp.zeros((reps, rows), jnp.int32)
    biases = []
    within = jnp.arange(rows)
    for step in range(depth):
        key_ids, here = ids[step][:, :, None], plane_ids[:, None, :]
        exists = layer_z >= step
        starts = starts + jnp.sum((exists & (key_ids < here)).astype(jnp.int32), axis=1)
        allowed = exists & (key_ids == here)
        if step == 0:
            allowed = allowed & (within[:, None] <= within[None, :])
        biases.append(jnp.where(allowed, 0.0, masked_score).astype(bf16))
    bias = jnp.concatenate(biases, axis=1)
    cosine, sine = rope_tables((layer_z * rows + within - starts).astype(f32))

    def by_half(table):
        return table.reshape(reps, 2, half, 2 * HD).transpose(1, 0, 2, 3)

    cosine, sine = by_half(cosine), by_half(sine)

    def flat(value):
        return value.reshape(count, -1)

    def blocks(value):
        return value.reshape(2, reps, half, -1)

    def forward(layer, layer_in):
        gain_attn, gain_ffn = gains[layer][0], gains[layer][1]
        scale_in = scale_of(layer_in)
        a_all = plane_gather((layer_in * scale_in * gain_attn).astype(bf16))
        query, keyval = project(a_all, qkv_all[layer], cosine, sine, q_width, k_width)
        keyvals = [keyval] + [
            back(keyval, step) for step in range(1, depth)
        ]
        mixed, log_total = attend(query, keyvals, bias)
        residual = layer_in + plane_reduce(blocks(times(flat(mixed), out_all[layer]).astype(bf16)))
        scale_mid = scale_of(residual)
        b_all = plane_gather((residual * scale_mid * gain_ffn).astype(bf16))
        pre = times(flat(b_all), ffn_all[layer]).astype(bf16)
        gate, up = pre[:, :ff_width], pre[:, ff_width:]
        hidden = (jax.nn.silu(gate.astype(f32)) * up.astype(f32)).astype(bf16)
        out = residual + plane_reduce(blocks(times(hidden, down_all[layer]).astype(bf16)))
        kept = (layer_in, scale_in, a_all, query, keyvals, mixed, log_total)
        return out.astype(bf16), kept + (residual, scale_mid, b_all, gate, up, hidden)

    def core_product(left, right, extra=None):
        size = left.shape[1] // (2 * depth)

        def half_of(value, which):
            return jnp.concatenate(
                [
                    lax.dynamic_slice_in_dim(value, (2 * k + which) * size, size, axis=1)
                    for k in range(depth)
                ],
                axis=1,
            )

        def product(which, right):
            found = dot(half_of(left, which), right, 0, 0)
            if extra is None:
                return found
            more = half_of(extra, which).T
            more = jnp.pad(more, ((0, 0), (0, 128 - more.shape[1])))
            return jnp.concatenate([found, more], axis=1)

        def finish(right, sent):
            got = lax.ppermute(sent, "section", SWAP)
            return (product(core, right) + got.astype(f32)).astype(bf16)

        return product(1 - core, right).astype(bf16), finish

    info = jnp.stack([core, rep]).astype(jnp.int32)

    def collect(total):
        return lax.psum_scatter(total, "fsdp", scatter_dimension=0, tiled=True)

    def backward(layer, grad_out, kept, earlier, ready):
        (layer_in, scale_in, a_all, query, keyvals, mixed, log_total) = kept[:7]
        (residual, scale_mid, b_all, gate, up, hidden) = kept[7:]
        gain_attn, gain_ffn = gains[layer][0], gains[layer][1]
        last = earlier is not None
        if last:
            old_rest, old_gate, old_up, old_down = earlier
            tall = old_up.shape[0]

            state = gather_step(gather_start(grad_out), 0)
            *state, old_gate, old_up = together(*state, old_gate, old_up)
            old_ffn = jnp.concatenate([old_gate, old_up], axis=1)
            gm_all = flat(gather_rest(state, 1))
            sent_down, finish = core_product(hidden, gm_all)
            gm_all, sent_down, old_ffn = together(gm_all, sent_down, old_ffn)
            ffn_state = gather_step(gather_start(old_ffn), 0)
        else:
            gm_all = flat(plane_gather(grad_out))
            sent_down, finish = core_product(hidden, gm_all)
            gm_all, sent_down, *ready = together(gm_all, sent_down, *ready)
        grad_hidden = times_back(gm_all, down_all[layer])
        gate, up = gate.astype(f32), up.astype(f32)
        sig = jax.nn.sigmoid(gate)
        grad_gate = (grad_hidden * up * (sig * (1.0 + gate * (1.0 - sig)))).astype(bf16)
        grad_up = (grad_hidden * (gate * sig)).astype(bf16)
        part_down = finish(gm_all, sent_down)
        if last:
            grad_gate, grad_up, *ffn_state = together(grad_gate, grad_up, *ffn_state)
        own_down = collect(part_down)
        weight_gate, weight_up = ffn_all[layer][:, :ff_width], ffn_all[layer][:, ff_width:]
        db = times_back(grad_gate, weight_gate) + times_back(grad_up, weight_up)
        db = blocks(db.astype(bf16))
        db, grad_gate, grad_up = together(db, grad_gate, grad_up)
        db = plane_reduce(db)
        sent_gate, finish_gate = core_product(flat(b_all), grad_gate)
        sent_up, finish_up = core_product(flat(b_all), grad_up)
        unit = residual * scale_mid
        grad_mid, gain_grad_ffn = norm_back(db, gain_ffn, unit, scale_mid)
        grad_mid = grad_mid + grad_out.astype(f32)
        go = grad_mid.astype(bf16)
        if last:
            go, old_rest = together(go, old_rest)
        go_all = flat(plane_gather(go))
        go_all, part_gate, part_up = together(
            go_all, finish_gate(grad_gate, sent_gate), finish_up(grad_up, sent_up)
        )
        own_gate, own_up = collect(part_gate), collect(part_up)
        grad_mixed = blocks(times_back(go_all, out_all[layer]).astype(bf16))
        def output_part(go_all):
            sent_o, finish_o = core_product(flat(mixed), go_all)
            return lax.all_to_all(finish_o(go_all, sent_o), "rep", 0, 0, tiled=True)

        if last:
            grad_mixed, old_rest, *ffn_state = together(grad_mixed, old_rest, *ffn_state)
            ffn_state = gather_step(ffn_state, 1)
            rest_state = gather_step(gather_start(old_rest), 0)
            part_o = output_part(go_all)
        else:
            grad_mixed, own_down = together(grad_mixed, own_down)
            own_down = gather_pair(gather_start(own_down), 0)
        grad_query, grad_kv = attend_back(query, keyvals, grad_mixed, log_total, bias)
        if last:
            grad_query, part_o, own_down, *grad_kv = together(
                grad_query, part_o, own_down, *grad_kv
            )
            own_down = gather_pair(gather_start(own_down), 0)
        else:
            grad_query, go_all, *grad_kv = together(grad_query, go_all, *grad_kv)
        grad_kv = [grad_kv[0]] + [
            lax.ppermute(grad_kv[step], "fsdp", [(i, i - step) for i in range(step, depth)])
            for step in range(1, depth)
        ]
        if not last:
            part_o = output_part(go_all)
        grad_qkv, da = project_back(grad_query, grad_kv, qkv_all[layer], cosine, sine, k_width)
        grad_qkv = flat(grad_qkv)

        def input_side(da):
            unit = layer_in * scale_in
            grad_in, gain_grad_attn = norm_back(da, gain_attn, unit, scale_in)
            grad_in = (grad_in + grad_mid).astype(bf16)
            gain_grads = jnp.stack([gain_grad_attn, gain_grad_ffn])
            sent_proj, finish = core_product(flat(a_all), grad_qkv, gain_grads)
            part_proj = finish(grad_qkv, sent_proj)
            pieces = part_proj.shape[0] // part_o.shape[0]
            aside = part_o.reshape(depth, -1, pieces, width // pieces).transpose(0, 2, 1, 3)
            aside = aside.reshape(part_proj.shape[0], -1)
            return grad_in, jnp.concatenate([part_proj, aside], axis=1)

        if not last:
            da, grad_qkv, part_o, own_gate, *own_down = together(
                da, grad_qkv, part_o, own_gate, *own_down
            )
            grad_in, part_rest = input_side(plane_reduce(da))
            return grad_in, (collect(part_rest), own_gate, own_up, own_down), ready

        def send(pair):
            return [lax.ppermute(v, "section", [(0, 1)]) for v in pair]

        def eight(zero, one, one_sent):
            found = []
            for sub in range(2):
                got = lax.ppermute(zero[sub], "section", [(1, 0)])
                found += [zero[sub], one_sent[sub], got, one[sub]]
            return found

        da, *states = together(da, *own_down, *ffn_state, *rest_state)
        zero_down = states[:2]
        old_ffn, old_rest = gather_pair(states[2:4], 2), gather_pair(states[4:], 1)
        olds_sent = send(old_ffn) + send(old_down)
        da, own_gate = together(plane_reduce(da), own_gate)
        grad_in, part_rest = input_side(da)
        gate_state = gather_step(gather_start(own_gate), 0)
        own_rest = collect(part_rest)
        own_up, *tied = together(own_up, *gate_state, *olds_sent, *old_rest)
        gate_state, olds_sent, old_rest = tied[:2], tied[2:6], tied[6:]
        ffn_sent, down_sent = olds_sent[:2], olds_sent[2:]
        rest_sent = send(old_rest)
        zero_gate = gather_pair(gate_state, 1)
        up_state = gather_step(gather_start(own_up), 0)
        tied = together(*zero_gate, *up_state, *rest_sent)
        zero_gate, up_state, rest_sent = tied[:2], tied[2:4], tied[4:]
        zero_up = gather_pair(up_state, 1)
        places = eight(zero_gate, old_ffn, ffn_sent)
        grad_gate = assemble_columns(info, places, (0, 0), ff_piece, depth)
        grad_down = assemble_rows(info, eight(zero_down, old_down, down_sent))
        grad_gate, grad_down, own_rest, *zero_up = together(
            grad_gate, grad_down, own_rest, *zero_up
        )
        rest_state = gather_step(gather_start(own_rest), 0)
        places = eight(zero_up, old_ffn, ffn_sent)
        grad_up = assemble_columns(info, places, (0, depth), ff_piece, depth)
        grad_up, *rest_state = together(grad_up, *rest_state)
        zero_rest = gather_pair(rest_state, 1)
        height = out_rows // 2
        proj_width = own_rest.shape[1] - height * width // tall
        places = eight(zero_rest, old_rest, rest_sent)
        sizes = (q_width, k_width, k_width)
        rest = assemble_rest(info, places, sizes, proj_width, height, width)
        gain_parts = [
            jnp.sum(v[..., qkv_width : qkv_width + 2].astype(f32), axis=0) for v in places
        ]
        gain_sums = jnp.concatenate(
            [
                jnp.where(core == 0, gain_parts[at], gain_parts[at + 1])
                for at in (0, 4, 2, 6)
            ],
            axis=0,
        )
        return grad_in, gain_sums, (*rest, grad_gate, grad_up, grad_down)

    own_tokens = lax.dynamic_index_in_dim(tokens[0], core, 0, keepdims=False)
    own_cotangent = lax.dynamic_index_in_dim(cotangent[0], core, 0, keepdims=False)
    out0, kept0 = forward(0, own_tokens.astype(f32))
    out1, kept1 = forward(1, out0.astype(f32))

    def swapped(zero, one):
        got = lax.ppermute(jnp.where(core == 0, one, zero), "section", SWAP)
        return jnp.where(core == 0, zero, got), jnp.where(core == 0, got, one)

    grad1, sums1, outputs = backward(1, own_cotangent, kept1, None, swapped(out0, out1))
    grad0, gain_sums, weight_grads = backward(0, grad1, kept0, sums1, None)
    outputs = jnp.stack(outputs)[None, None]
    input_grads = jnp.stack(swapped(grad0, grad1))[None, None]
    grad_query, grad_key, grad_value, grad_output, grad_gate, grad_up, grad_down = weight_grads
    return (
        outputs,
        input_grads,
        gain_sums[:, 0][None],
        grad_query[None],
        grad_key[None],
        grad_value[None],
        grad_output[None],
        gain_sums[:, 1][None],
        grad_gate[None],
        grad_up[None],
        grad_down[None],
    )


def solution(mesh):
    in_specs = (
        P("rep", None, "fsdp", None),
        P("rep", None, "fsdp"),
        P("rep", None, "fsdp", None),
        P("section", "fsdp"),
        P("section", "fsdp", None),
        P("section", "fsdp", None),
        P("section", "fsdp", None),
        P("section", "fsdp", None),
        P("section", "fsdp"),
        P("section", "fsdp", None),
        P("section", "fsdp", None),
        P("section", "fsdp", None),
    )
    out_specs = (
        P("section", "rep", None, "fsdp", None),
        P("section", "rep", None, "fsdp", None),
        P("section", "fsdp"),
        P("section", "fsdp", None),
        P("section", "fsdp", None),
        P("section", "fsdp", None),
        P("section", "fsdp", None),
        P("section", "fsdp"),
        P("section", "fsdp", None),
        P("section", "fsdp", None),
        P("section", "fsdp", None),
    )
    return jax.shard_map(shards, mesh=mesh, in_specs=in_specs, out_specs=out_specs, check_vma=False)
```

```python
import functools

import jax
import jax.numpy as jnp
from jax import lax
from jax.experimental import pallas as pl
from jax.experimental.pallas import tpu as pltpu
from jax.sharding import PartitionSpec as P

HQ = 32
KVH = 8
HD = 64
FF = 8192

epsilon = 1e-05
rope_base = 500000.0
masked_score = -1e30
bf16 = jnp.bfloat16
f32 = jnp.float32
SWAP = [(0, 1), (1, 0)]


def partner(value, bit):
    count = lax.axis_size("rep")
    return lax.ppermute(value, "rep", [(i, i ^ bit) for i in range(count)])


def bit_list(count):
    found = []
    bit = 1
    while bit < count:
        found.append(bit)
        bit *= 2
    return found


def gather_start(own):
    half = own.shape[0] // 2
    return own[None, :half], own[None, half:]


def gather_step(state, at):
    bits = bit_list(lax.axis_size("rep"))
    first, second = state
    first = jnp.concatenate([first, partner(first, bits[at])], axis=0)
    other = partner(second, bits[-1 - at])
    second = jnp.stack([second, other], axis=1).reshape((-1,) + second.shape[1:])
    return first, second


def gather_pair(state, at):
    for step in range(at, len(bit_list(lax.axis_size("rep")))):
        state = gather_step(state, step)
    return list(state)


def gather_rest(state, at):
    return jnp.stack(gather_pair(state, at))


def plane_gather(own):
    return gather_rest(gather_start(own), 0)


def plane_reduce(parts):
    bits = bit_list(lax.axis_size("rep"))
    first, second = parts[0], parts[1]
    for bit in bits[::-1]:
        keep, away = first[:bit], first[bit:]
        first = keep.astype(f32) + partner(away.astype(bf16), bit).astype(f32)
    for bit in bits:
        pair = second.reshape((-1, 2) + second.shape[1:])
        keep, away = pair[:, 0], pair[:, 1]
        second = keep.astype(f32) + partner(away.astype(bf16), bit).astype(f32)
    return jnp.concatenate([first[0], second[0]], axis=0)


def rope_tables(positions):
    half_size = HD // 2
    frequency = rope_base ** (-(jnp.arange(half_size).astype(f32) * 2.0) / HD)
    angles = positions[..., None] * frequency
    cosine, sine = jnp.cos(angles), jnp.sin(angles)
    return (
        jnp.concatenate([cosine] * 4, axis=-1),
        jnp.concatenate([-sine, sine] * 2, axis=-1),
    )


def times(left, weight):
    return jnp.dot(left, weight, preferred_element_type=f32)


def times_back(left, weight):
    return lax.dot_general(
        left, weight, (((1,), (1,)), ((), ())), preferred_element_type=f32
    )


def scale_of(values):
    return lax.rsqrt(jnp.mean(values * values, axis=-1, keepdims=True) + epsilon)


def norm_back(grad, gain, unit, scale):
    scaled = gain * grad
    out = scale * (scaled - unit * jnp.mean(scaled * unit, axis=-1, keepdims=True))
    return (out, jnp.sum(grad * unit, axis=0))


def sequence(ref):
    return ref[:, 0].reshape(-1, ref.shape[-1])


def scaled(value):
    return (value.astype(f32) * HD ** (-0.5)).astype(bf16)


def dot(left, right, left_dim, right_dim):
    return lax.dot_general(
        left, right, (((left_dim,), (right_dim,)), ((), ())), preferred_element_type=f32
    )


def attend_kernel(depth, query_ref, bias_ref, *refs):
    mixed_ref, log_ref = refs[depth:]
    keyval = jnp.concatenate([sequence(ref) for ref in refs[:depth]], axis=0)
    query = scaled(sequence(query_ref))
    bias = bias_ref[0].astype(f32)
    k_width = keyval.shape[1] // 2
    heads = query.shape[1] // HD
    group = heads // (k_width // HD)
    columns = []
    for head in range(heads):
        at = head // group * HD
        key = keyval[:, at : at + HD]
        value = keyval[:, k_width + at : k_width + at + HD]
        scores = dot(key, query[:, head * HD : (head + 1) * HD], 1, 1) + bias
        row_max = jnp.max(scores, axis=0, keepdims=True)
        weights = jnp.exp(scores - row_max)
        total = jnp.sum(weights, axis=0, keepdims=True)
        probs = (weights * (1.0 / total)).astype(bf16)
        columns.append(dot(value, probs, 0, 0))
        log_ref[0, head : head + 1, :] = row_max + jnp.log(total)
    mixed = jnp.concatenate(columns, axis=0).T.astype(bf16)
    mixed_ref[:, 0] = mixed.reshape(2, -1, mixed.shape[1])


def attend_back_kernel(depth, query_ref, grad_ref, log_ref, bias_ref, *refs):
    grad_query_ref, grad_refs = refs[depth], refs[depth + 1 :]
    keyval = jnp.concatenate([sequence(ref) for ref in refs[:depth]], axis=0)
    query = scaled(sequence(query_ref))
    grad = sequence(grad_ref)
    bias = bias_ref[0].astype(f32)
    k_width = keyval.shape[1] // 2
    heads = query.shape[1] // HD
    group = heads // (k_width // HD)
    columns, grad_keys, grad_values = [], [], []
    for head in range(heads):
        at = head // group * HD
        key = keyval[:, at : at + HD]
        value = keyval[:, k_width + at : k_width + at + HD]
        own_query = query[:, head * HD : (head + 1) * HD]
        own_grad = grad[:, head * HD : (head + 1) * HD]
        scores = dot(key, own_query, 1, 1) + bias
        probs = jnp.exp(scores - log_ref[0, head : head + 1, :])
        grad_probs = dot(value, own_grad, 1, 1)
        inner = jnp.sum(probs * grad_probs, axis=0, keepdims=True)
        grad_scores = (probs * (grad_probs - inner)).astype(bf16)
        columns.append(dot(key, grad_scores, 0, 0))
        grad_key = dot(grad_scores, own_query, 1, 0)
        grad_value = dot(probs.astype(bf16), own_grad, 1, 0)
        if head % group == 0:
            grad_keys.append(grad_key)
            grad_values.append(grad_value)
        else:
            grad_keys[-1] = grad_keys[-1] + grad_key
            grad_values[-1] = grad_values[-1] + grad_value
    grad_query = jnp.concatenate(columns, axis=0).T * HD ** (-0.5)
    grad_query_ref[:, 0] = grad_query.reshape(2, -1, grad_query.shape[1])
    both = jnp.concatenate(grad_keys + grad_values, axis=1).astype(bf16)
    rows = both.shape[0] // depth
    for step, ref in enumerate(grad_refs):
        part = both[step * rows : (step + 1) * rows]
        ref[:, 0] = part.reshape(2, rows // 2, part.shape[1])


def sequence_spec(array):
    two, _, half, columns = array.shape
    return pl.BlockSpec((two, 1, half, columns), lambda j: (0, j, 0, 0))


def row_spec(array):
    return pl.BlockSpec((1,) + array.shape[1:], lambda j: (j, 0, 0))


def attend(query, keyvals, bias):
    two, reps, half, width = query.shape
    logs = jax.ShapeDtypeStruct((reps, width // HD, two * half), f32)
    cells = reps * width * two * half * bias.shape[1]
    return pl.pallas_call(
        functools.partial(attend_kernel, len(keyvals)),
        grid=(reps,),
        in_specs=[sequence_spec(query), row_spec(bias)] + [sequence_spec(v) for v in keyvals],
        out_specs=[sequence_spec(query), row_spec(logs)],
        out_shape=[jax.ShapeDtypeStruct(query.shape, bf16), logs],
        compiler_params=pltpu.CompilerParams(vmem_limit_bytes=48 << 20),
        cost_estimate=pl.CostEstimate(
            flops=16 * cells, bytes_accessed=8 << 20, transcendentals=cells // HD
        ),
        name="attend",
    )(query, bias, *keyvals)


def attend_back(query, keyvals, grad_mixed, log_total, bias):
    two, reps, half, width = query.shape
    cells = reps * width * two * half * bias.shape[1]
    outs = pl.pallas_call(
        functools.partial(attend_back_kernel, len(keyvals)),
        grid=(reps,),
        in_specs=[sequence_spec(query), sequence_spec(grad_mixed), row_spec(log_total)]
        + [row_spec(bias)]
        + [sequence_spec(v) for v in keyvals],
        out_specs=[sequence_spec(query)] + [sequence_spec(v) for v in keyvals],
        out_shape=[jax.ShapeDtypeStruct(query.shape, f32)]
        + [jax.ShapeDtypeStruct(v.shape, bf16) for v in keyvals],
        compiler_params=pltpu.CompilerParams(vmem_limit_bytes=48 << 20),
        cost_estimate=pl.CostEstimate(
            flops=40 * cells, bytes_accessed=12 << 20, transcendentals=cells // HD
        ),
        name="attend_back",
    )(query, grad_mixed, log_total, bias, *keyvals)
    return outs[0], outs[1:]


def turned_pair(value):
    lane = lax.broadcasted_iota(jnp.int32, value.shape, 1)
    half = HD // 2
    ahead = pltpu.roll(value, value.shape[1] - half, 1)
    behind = pltpu.roll(value, half, 1)
    return jnp.where(lane % HD < half, ahead, behind)


def widened(table, width):
    return jnp.concatenate([table] * (width // table.shape[1]), axis=1)


def rows_of(ref):
    return ref[0].reshape(-1, ref.shape[-1])


def project_kernel(k_width, a_ref, weight_ref, cosine_ref, sine_ref, query_ref, keyval_ref):
    mixed = dot(rows_of(a_ref), weight_ref[...], 1, 0)
    width = mixed.shape[1]
    cosine = widened(rows_of(cosine_ref), width)
    sine = widened(rows_of(sine_ref), width)
    rotated = mixed * cosine + turned_pair(mixed) * sine
    lane = lax.broadcasted_iota(jnp.int32, mixed.shape, 1)
    rotated = jnp.where(lane < width - k_width, rotated, mixed).astype(bf16)
    q_width = query_ref.shape[-1]
    query_ref[0] = rotated[:, :q_width].reshape(query_ref.shape[1:])
    keyval_ref[0] = rotated[:, q_width:].reshape(keyval_ref.shape[1:])


def project_back_kernel(k_width, grad_ref, weight_ref, cosine_ref, sine_ref, *refs):
    parts, (joined_ref, out_ref) = refs[:-2], refs[-2:]
    keyval = rows_of(parts[0]).astype(f32)
    for part in parts[1:]:
        keyval = keyval + rows_of(part).astype(f32)
    joined = jnp.concatenate([rows_of(grad_ref), keyval], axis=1)
    width = joined.shape[1]
    cosine = widened(rows_of(cosine_ref), width)
    sine = widened(rows_of(sine_ref), width)
    rotated = joined * cosine - turned_pair(joined) * sine
    lane = lax.broadcasted_iota(jnp.int32, joined.shape, 1)
    rotated = jnp.where(lane < width - k_width, rotated, joined).astype(bf16)
    joined_ref[0] = rotated.reshape(joined_ref.shape[1:])
    out = dot(rotated, weight_ref[...], 1, 1).astype(bf16)
    out_ref[0] = out.reshape(out_ref.shape[1:])


def half_spec(array):
    return pl.BlockSpec((1,) + array.shape[1:], lambda i: (i, 0, 0, 0))


def all_spec(array):
    return pl.BlockSpec(array.shape, lambda i: (0, 0))


def project(a_all, weight, cosine, sine, q_width, k_width):
    shape = a_all.shape[:3]
    outs = [
        jax.ShapeDtypeStruct(shape + (q_width,), bf16),
        jax.ShapeDtypeStruct(shape + (2 * k_width,), bf16),
    ]
    cells = a_all.size * weight.shape[1]
    return pl.pallas_call(
        functools.partial(project_kernel, k_width),
        grid=(2,),
        in_specs=[half_spec(a_all), all_spec(weight), half_spec(cosine), half_spec(sine)],
        out_specs=[half_spec(v) for v in outs],
        out_shape=outs,
        compiler_params=pltpu.CompilerParams(vmem_limit_bytes=40 << 20),
        cost_estimate=pl.CostEstimate(
            flops=2 * cells, bytes_accessed=10 << 20, transcendentals=0
        ),
        name="project",
    )(a_all, weight, cosine, sine)


def project_back(grad_query, parts, weight, cosine, sine, k_width):
    shape = grad_query.shape[:3]
    outs = [
        jax.ShapeDtypeStruct(shape + (weight.shape[1],), bf16),
        jax.ShapeDtypeStruct(shape + (weight.shape[0],), bf16),
    ]
    cells = outs[0].size * weight.shape[0]
    return pl.pallas_call(
        functools.partial(project_back_kernel, k_width),
        grid=(2,),
        in_specs=[half_spec(grad_query), all_spec(weight), half_spec(cosine), half_spec(sine)]
        + [half_spec(v) for v in parts],
        out_specs=[half_spec(v) for v in outs],
        out_shape=outs,
        compiler_params=pltpu.CompilerParams(vmem_limit_bytes=48 << 20),
        cost_estimate=pl.CostEstimate(
            flops=2 * cells, bytes_accessed=14 << 20, transcendentals=0
        ),
        name="project_back",
    )(grad_query, weight, cosine, sine, *parts)


def by_place(info, refs, write):
    which = info[0] + 2 * pl.program_id(0) + 4 * pl.program_id(1)
    for at, ref in enumerate(refs):
        pl.when(which == at)(functools.partial(write, ref))


def columns_kernel(piece, info, *refs):
    out_ref = refs[8]
    reps, _, taken = refs[0].shape

    def write(ref):
        for at in range(taken // piece):
            for rep in range(reps):
                start = (at * reps + rep) * piece
                found = ref[rep ^ info[1], :, at * piece : (at + 1) * piece]
                out_ref[:, start : start + piece] = found.astype(f32)

    by_place(info, refs[:8], write)


def rows_kernel(info, *refs):
    out_ref = refs[8]

    def write(ref):
        for rep in range(out_ref.shape[0]):
            out_ref[rep, 0] = ref[rep ^ info[1]].astype(f32)

    by_place(info, refs[:8], write)


def rest_kernel(proj_width, info, *refs):
    outs, output_ref = refs[8:11], refs[11]
    reps, rows, width = refs[0].shape
    height, piece = output_ref.shape[2], width - proj_width

    def write(ref):
        for rep in range(reps):
            block = ref[rep ^ info[1]].astype(f32)
            start = 0
            for out_ref in outs:
                size = out_ref.shape[1] // reps
                out_ref[:, rep * size : (rep + 1) * size] = block[:, start : start + size]
                start += size
            for at in range(rows // height):
                part = block[at * height : (at + 1) * height, proj_width:]
                output_ref[rep, 0, :, at * piece : (at + 1) * piece] = part

    by_place(info, refs[:8], write)


def assembled(kernel, grid, block, index, out_blocks, out_index, out_shapes, info, eight):
    def chosen(at):
        def where_from(*steps):
            taken = steps[-1][0] + 2 * steps[0] + 4 * steps[1] == at
            return tuple(jnp.where(taken, v, 0) for v in index(at % 2, *steps))

        return where_from

    return pl.pallas_call(
        kernel,
        grid_spec=pltpu.PrefetchScalarGridSpec(
            num_scalar_prefetch=1,
            grid=grid,
            in_specs=[pl.BlockSpec(block, chosen(at)) for at in range(8)],
            out_specs=[pl.BlockSpec(b, f) for b, f in zip(out_blocks, out_index)],
        ),
        out_shape=[jax.ShapeDtypeStruct(v, f32) for v in out_shapes],
        compiler_params=pltpu.CompilerParams(vmem_limit_bytes=56 << 20),
        name="assemble",
    )(info, *eight)


def assemble_columns(info, eight, offsets, piece, pieces):
    reps, rows, _ = eight[0].shape
    step = 2 if pieces % 2 == 0 else 1
    return assembled(
        functools.partial(columns_kernel, piece),
        (2, 2, pieces // step),
        (reps, rows, step * piece),
        lambda layer, k, sub, at, info: (0, 0, offsets[layer] // step + at),
        [(rows, step * reps * piece)],
        [lambda k, sub, at, info: (2 * k + sub, at)],
        [(4 * rows, reps * piece * pieces)],
        info,
        eight,
    )[0]


def assemble_rows(info, eight):
    reps, rows, columns = eight[0].shape
    return assembled(
        rows_kernel,
        (2, 2),
        (reps, rows, columns),
        lambda layer, k, sub, info: (0, 0, 0),
        [(reps, 1, rows, columns)],
        [lambda k, sub, info: (0, 2 * k + sub, 0, 0)],
        [(reps, 4, rows, columns)],
        info,
        eight,
    )[0].reshape(-1, columns)


def assemble_rest(info, eight, sizes, proj_width, height, width):
    reps, rows, columns = eight[0].shape
    outs = assembled(
        functools.partial(rest_kernel, proj_width),
        (2, 2),
        (reps, rows, columns),
        lambda layer, k, sub, info: (0, 0, 0),
        [(rows, reps * size) for size in sizes] + [(reps, 1, height, width // 2)],
        [lambda k, sub, info: (2 * k + sub, 0)] * len(sizes)
        + [lambda k, sub, info: (0, k, 0, sub)],
        [(4 * rows, reps * size) for size in sizes] + [(reps, 2, height, width)],
        info,
        eight,
    )
    return (*outs[:-1], outs[-1].reshape(-1, width))


def together(*values):
    return lax.optimization_barrier(values)


def shards(
    tokens,
    segment_ids,
    cotangent,
    norm_attn,
    w_query,
    w_key,
    w_value,
    w_output,
    norm_ffn,
    w_gate,
    w_up,
    w_down,
):
    core = lax.axis_index("section")
    layer_z = lax.axis_index("fsdp")
    rep = lax.axis_index("rep")
    depth = lax.axis_size("fsdp")
    reps = lax.axis_size("rep")
    rows, width = tokens.shape[2:]
    half = rows // 2
    count = reps * rows
    q_width = HQ * HD // reps
    k_width = KVH * HD // reps
    ff_width = FF // reps
    ff_piece = FF // (reps * depth)

    def back(value, step):
        return lax.ppermute(value, "fsdp", [(i, i + step) for i in range(depth - step)])

    def by_layer(own, got):
        return (jnp.where(core == 0, own, got), jnp.where(core == 0, got, own))

    own_gain = jnp.concatenate([norm_attn, norm_ffn], axis=0)
    turned = jnp.stack(
        [own_gain]
        + [
            lax.ppermute(own_gain, "fsdp", [(i, (i + s) % depth) for i in range(depth)])
            for s in range(1, depth)
        ]
    )
    own_gain = jnp.concatenate(
        [
            lax.dynamic_index_in_dim(turned, (layer_z - k + depth) % depth, 0, keepdims=False)
            for k in range(depth)
        ],
        axis=1,
    ).astype(f32)
    gains = by_layer(own_gain, lax.ppermute(own_gain, "section", SWAP))

    plane_ids = lax.dynamic_index_in_dim(segment_ids[0], core, 0, keepdims=True)
    for bit in bit_list(reps):
        plane_ids = jnp.concatenate([plane_ids, partner(plane_ids, bit)], axis=0)
    ids = [plane_ids] + [back(plane_ids, step) for step in range(1, depth)]

    def split(cut, total):
        size = total // 2
        got = lax.ppermute(cut((1 - core) * size, size), "section", SWAP)
        return by_layer(cut(core * size, size), got)

    def spread(pieces):
        return [lax.all_gather(v, ("fsdp", "section"), axis=0, tiled=True) for v in pieces]

    def qkv_cut(row, size):
        parts = ((w_query, q_width), (w_key, k_width), (w_value, k_width))
        return jnp.concatenate(
            [lax.dynamic_slice(w[0], (row, rep * n), (size, n)) for w, n in parts], axis=1
        )

    def ffn_cut(row, size):
        return jnp.concatenate(
            [
                lax.dynamic_slice(
                    w[0], (row, k * reps * ff_piece + rep * ff_piece), (size, ff_piece)
                )
                for w in (w_gate, w_up)
                for k in range(depth)
            ],
            axis=1,
        )

    out_rows = w_output.shape[1] // reps

    def attn_cut(row, size):
        height = out_rows * size // w_query.shape[1]
        first = rep * out_rows + row * out_rows // w_query.shape[1]
        out = lax.dynamic_slice_in_dim(w_output[0], first, height)
        return jnp.concatenate([qkv_cut(row, size), out.reshape(size, -1)], axis=1)

    def all_ffn_cut(row, size):
        height = ff_piece * size // w_gate.shape[1]
        first = rep * ff_piece + row * ff_piece // w_gate.shape[1]
        down = lax.dynamic_slice_in_dim(w_down[0], first, height)
        return jnp.concatenate([ffn_cut(row, size), down.reshape(size, -1)], axis=1)

    attn_all = spread(split(attn_cut, w_query.shape[1]))
    qkv_width = q_width + 2 * k_width
    qkv_all = [v[:, :qkv_width] for v in attn_all]
    out_all = [
        lax.all_to_all(v[:, qkv_width:].reshape(-1, width), "rep", 0, 0, tiled=True)
        for v in attn_all
    ]
    both_all = spread(split(all_ffn_cut, w_gate.shape[1]))
    ffn_all = [v[:, : 2 * ff_width] for v in both_all]
    down_all = [v[:, 2 * ff_width :].reshape(ff_width, width) for v in both_all]

    starts = jnp.zeros((reps, rows), jnp.int32)
    biases = []
    within = jnp.arange(rows)
    for step in range(depth):
        key_ids, here = ids[step][:, :, None], plane_ids[:, None, :]
        exists = layer_z >= step
        starts = starts + jnp.sum((exists & (key_ids < here)).astype(jnp.int32), axis=1)
        allowed = exists & (key_ids == here)
        if step == 0:
            allowed = allowed & (within[:, None] <= within[None, :])
        biases.append(jnp.where(allowed, 0.0, masked_score).astype(bf16))
    bias = jnp.concatenate(biases, axis=1)
    cosine, sine = rope_tables((layer_z * rows + within - starts).astype(f32))

    def by_half(table):
        return table.reshape(reps, 2, half, 2 * HD).transpose(1, 0, 2, 3)

    cosine, sine = by_half(cosine), by_half(sine)

    def flat(value):
        return value.reshape(count, -1)

    def blocks(value):
        return value.reshape(2, reps, half, -1)

    def forward(layer, layer_in):
        gain_attn, gain_ffn = gains[layer][0], gains[layer][1]
        scale_in = scale_of(layer_in)
        a_all = plane_gather((layer_in * scale_in * gain_attn).astype(bf16))
        query, keyval = project(a_all, qkv_all[layer], cosine, sine, q_width, k_width)
        keyvals = [keyval]
        for step in range(1, depth):
            pairs = [(i, i + 1) for i in range(step - 1, depth - 1)]
            keyvals.append(lax.ppermute(keyvals[-1], "fsdp", pairs))
        mixed, log_total = attend(query, keyvals, bias)
        residual = layer_in + plane_reduce(blocks(times(flat(mixed), out_all[layer]).astype(bf16)))
        scale_mid = scale_of(residual)
        b_all = plane_gather((residual * scale_mid * gain_ffn).astype(bf16))
        pre = times(flat(b_all), ffn_all[layer]).astype(bf16)
        gate, up = pre[:, :ff_width], pre[:, ff_width:]
        hidden = (jax.nn.silu(gate.astype(f32)) * up.astype(f32)).astype(bf16)
        out = residual + plane_reduce(blocks(times(hidden, down_all[layer]).astype(bf16)))
        kept = (layer_in, scale_in, a_all, query, keyvals, mixed, log_total)
        return out.astype(bf16), kept + (residual, scale_mid, b_all, gate, up, hidden)

    def core_product(left, right, extra=None):
        size = left.shape[1] // (2 * depth)

        def half_of(value, which):
            return jnp.concatenate(
                [
                    lax.dynamic_slice_in_dim(value, (2 * k + which) * size, size, axis=1)
                    for k in range(depth)
                ],
                axis=1,
            )

        def product(which, right):
            found = dot(half_of(left, which), right, 0, 0)
            if extra is None:
                return found
            more = half_of(extra, which).T
            more = jnp.pad(more, ((0, 0), (0, 128 - more.shape[1])))
            return jnp.concatenate([found, more], axis=1)

        def finish(right, sent):
            got = lax.ppermute(sent, "section", SWAP)
            return (product(core, right) + got.astype(f32)).astype(bf16)

        return product(1 - core, right).astype(bf16), finish

    info = jnp.stack([core, rep]).astype(jnp.int32)

    def collect(total):
        return lax.psum_scatter(total, "fsdp", scatter_dimension=0, tiled=True)

    def backward(layer, grad_out, kept, earlier, ready):
        (layer_in, scale_in, a_all, query, keyvals, mixed, log_total) = kept[:7]
        (residual, scale_mid, b_all, gate, up, hidden) = kept[7:]
        gain_attn, gain_ffn = gains[layer][0], gains[layer][1]
        last = earlier is not None
        if last:
            old_rest, old_gate, old_up, old_down = earlier
            tall = old_up.shape[0]

            state = gather_step(gather_start(grad_out), 0)
            *state, old_gate, old_up = together(*state, old_gate, old_up)
            old_ffn = jnp.concatenate([old_gate, old_up], axis=1)
            gm_all = flat(gather_rest(state, 1))
            sent_down, finish = core_product(hidden, gm_all)
            gm_all, sent_down, old_ffn = together(gm_all, sent_down, old_ffn)
            ffn_state = gather_step(gather_start(old_ffn), 0)
        else:
            gm_all = flat(plane_gather(grad_out))
            sent_down, finish = core_product(hidden, gm_all)
            gm_all, sent_down, *ready = together(gm_all, sent_down, *ready)
        grad_hidden = times_back(gm_all, down_all[layer])
        gate, up = gate.astype(f32), up.astype(f32)
        sig = jax.nn.sigmoid(gate)
        grad_gate = (grad_hidden * up * (sig * (1.0 + gate * (1.0 - sig)))).astype(bf16)
        grad_up = (grad_hidden * (gate * sig)).astype(bf16)
        grad_pre = jnp.concatenate([grad_gate, grad_up], axis=1)
        part_down = finish(gm_all, sent_down)
        if last:
            grad_pre, *ffn_state = together(grad_pre, *ffn_state)
        own_down = collect(part_down)
        db = blocks(times_back(grad_pre, ffn_all[layer]).astype(bf16))
        db, grad_gate, grad_up = together(db, grad_gate, grad_up)
        db = plane_reduce(db)
        sent_gate, finish_gate = core_product(flat(b_all), grad_gate)
        sent_up, finish_up = core_product(flat(b_all), grad_up)
        unit = residual * scale_mid
        grad_mid, gain_grad_ffn = norm_back(db, gain_ffn, unit, scale_mid)
        grad_mid = grad_mid + grad_out.astype(f32)
        go = grad_mid.astype(bf16)
        if last:
            go, old_rest = together(go, old_rest)
        go_all = flat(plane_gather(go))
        go_all, part_gate, part_up = together(
            go_all, finish_gate(grad_gate, sent_gate), finish_up(grad_up, sent_up)
        )
        own_gate, own_up = collect(part_gate), collect(part_up)
        grad_mixed = blocks(times_back(go_all, out_all[layer]).astype(bf16))
        def output_part(go_all):
            sent_o, finish_o = core_product(flat(mixed), go_all)
            return lax.all_to_all(finish_o(go_all, sent_o), "rep", 0, 0, tiled=True)

        if last:
            grad_mixed, old_rest, *ffn_state = together(grad_mixed, old_rest, *ffn_state)
            ffn_state = gather_step(ffn_state, 1)
            rest_state = gather_step(gather_start(old_rest), 0)
            part_o = output_part(go_all)
        else:
            grad_mixed, own_down = together(grad_mixed, own_down)
            own_down = gather_pair(gather_start(own_down), 0)
        grad_query, grad_kv = attend_back(query, keyvals, grad_mixed, log_total, bias)
        if last:
            grad_query, part_o, own_down, *grad_kv = together(
                grad_query, part_o, own_down, *grad_kv
            )
            own_down = gather_pair(gather_start(own_down), 0)
        else:
            grad_query, go_all, *grad_kv = together(grad_query, go_all, *grad_kv)
        grad_kv = [grad_kv[0]] + [
            lax.ppermute(grad_kv[step], "fsdp", [(i, i - step) for i in range(step, depth)])
            for step in range(1, depth)
        ]
        if not last:
            part_o = output_part(go_all)
        grad_qkv, da = project_back(grad_query, grad_kv, qkv_all[layer], cosine, sine, k_width)
        grad_qkv = flat(grad_qkv)

        def input_side(da):
            unit = layer_in * scale_in
            grad_in, gain_grad_attn = norm_back(da, gain_attn, unit, scale_in)
            grad_in = (grad_in + grad_mid).astype(bf16)
            gain_grads = jnp.stack([gain_grad_attn, gain_grad_ffn])
            sent_proj, finish = core_product(flat(a_all), grad_qkv, gain_grads)
            part_proj = finish(grad_qkv, sent_proj)
            pieces = part_proj.shape[0] // part_o.shape[0]
            aside = part_o.reshape(depth, -1, pieces, width // pieces).transpose(0, 2, 1, 3)
            aside = aside.reshape(part_proj.shape[0], -1)
            return grad_in, jnp.concatenate([part_proj, aside], axis=1)

        if not last:
            da, grad_qkv, part_o, own_gate, *own_down = together(
                da, grad_qkv, part_o, own_gate, *own_down
            )
            grad_in, part_rest = input_side(plane_reduce(da))
            return grad_in, (collect(part_rest), own_gate, own_up, own_down), ready

        def send(pair):
            return [lax.ppermute(v, "section", [(0, 1)]) for v in pair]

        def eight(zero, one, one_sent):
            found = []
            for sub in range(2):
                got = lax.ppermute(zero[sub], "section", [(1, 0)])
                found += [zero[sub], one_sent[sub], got, one[sub]]
            return found

        da, *states = together(da, *own_down, *ffn_state, *rest_state)
        zero_down = states[:2]
        old_ffn, old_rest = gather_pair(states[2:4], 2), gather_pair(states[4:], 1)
        olds_sent = send(old_ffn) + send(old_down)
        da, own_gate = together(plane_reduce(da), own_gate)
        grad_in, part_rest = input_side(da)
        gate_state = gather_step(gather_start(own_gate), 0)
        own_rest = collect(part_rest)
        own_up, *tied = together(own_up, *gate_state, *olds_sent, *old_rest)
        gate_state, olds_sent, old_rest = tied[:2], tied[2:6], tied[6:]
        ffn_sent, down_sent = olds_sent[:2], olds_sent[2:]
        rest_sent = send(old_rest)
        zero_gate = gather_pair(gate_state, 1)
        up_state = gather_step(gather_start(own_up), 0)
        tied = together(*zero_gate, *up_state, *rest_sent)
        zero_gate, up_state, rest_sent = tied[:2], tied[2:4], tied[4:]
        zero_up = gather_pair(up_state, 1)
        places = eight(zero_gate, old_ffn, ffn_sent)
        grad_gate = assemble_columns(info, places, (0, 0), ff_piece, depth)
        grad_down = assemble_rows(info, eight(zero_down, old_down, down_sent))
        grad_gate, grad_down, own_rest, *zero_up = together(
            grad_gate, grad_down, own_rest, *zero_up
        )
        rest_state = gather_step(gather_start(own_rest), 0)
        places = eight(zero_up, old_ffn, ffn_sent)
        grad_up = assemble_columns(info, places, (0, depth), ff_piece, depth)
        grad_up, *rest_state = together(grad_up, *rest_state)
        zero_rest = gather_pair(rest_state, 1)
        height = out_rows // 2
        proj_width = own_rest.shape[1] - height * width // tall
        places = eight(zero_rest, old_rest, rest_sent)
        sizes = (q_width, k_width, k_width)
        rest = assemble_rest(info, places, sizes, proj_width, height, width)
        gain_parts = [
            jnp.sum(v[..., qkv_width : qkv_width + 2].astype(f32), axis=0) for v in places
        ]
        gain_sums = jnp.concatenate(
            [
                jnp.where(core == 0, gain_parts[at], gain_parts[at + 1])
                for at in (0, 4, 2, 6)
            ],
            axis=0,
        )
        return grad_in, gain_sums, (*rest, grad_gate, grad_up, grad_down)

    own_tokens = lax.dynamic_index_in_dim(tokens[0], core, 0, keepdims=False)
    own_cotangent = lax.dynamic_index_in_dim(cotangent[0], core, 0, keepdims=False)
    out0, kept0 = forward(0, own_tokens.astype(f32))
    out1, kept1 = forward(1, out0.astype(f32))

    def swapped(zero, one):
        got = lax.ppermute(jnp.where(core == 0, one, zero), "section", SWAP)
        return jnp.where(core == 0, zero, got), jnp.where(core == 0, got, one)

    grad1, sums1, outputs = backward(1, own_cotangent, kept1, None, swapped(out0, out1))
    grad0, gain_sums, weight_grads = backward(0, grad1, kept0, sums1, None)
    outputs = jnp.stack(outputs)[None, None]
    input_grads = jnp.stack(swapped(grad0, grad1))[None, None]
    grad_query, grad_key, grad_value, grad_output, grad_gate, grad_up, grad_down = weight_grads
    return (
        outputs,
        input_grads,
        gain_sums[:, 0][None],
        grad_query[None],
        grad_key[None],
        grad_value[None],
        grad_output[None],
        gain_sums[:, 1][None],
        grad_gate[None],
        grad_up[None],
        grad_down[None],
    )


def solution(mesh):
    in_specs = (
        P("rep", None, "fsdp", None),
        P("rep", None, "fsdp"),
        P("rep", None, "fsdp", None),
        P("section", "fsdp"),
        P("section", "fsdp", None),
        P("section", "fsdp", None),
        P("section", "fsdp", None),
        P("section", "fsdp", None),
        P("section", "fsdp"),
        P("section", "fsdp", None),
        P("section", "fsdp", None),
        P("section", "fsdp", None),
    )
    out_specs = (
        P("section", "rep", None, "fsdp", None),
        P("section", "rep", None, "fsdp", None),
        P("section", "fsdp"),
        P("section", "fsdp", None),
        P("section", "fsdp", None),
        P("section", "fsdp", None),
        P("section", "fsdp", None),
        P("section", "fsdp"),
        P("section", "fsdp", None),
        P("section", "fsdp", None),
        P("section", "fsdp", None),
    )
    return jax.shard_map(shards, mesh=mesh, in_specs=in_specs, out_specs=out_specs, check_vma=False)
```
